32 devices in a mesh: dp: 4 (over z), fsdp: 8 (over y, x, core).
Axes of the slice: x: 2, y: 2, z: 4, core: 2. Of those that a mesh axis runs over, the one named last changes fastest.
Arguments:
- tokens: bfloat16 [32, 1024, 1024], P(('dp', 'fsdp')), may hold values from -6 to 6
- prompt: bfloat16 [32, 128, 1024], P(('dp', 'fsdp')), may hold values from -6 to 6
- prompt_len: int32 [32], P(('dp', 'fsdp')), may hold values from 8 to 128, as said below
- cotangent: bfloat16 [32, 1024, 1024], P(('dp', 'fsdp')), may hold values from -6 to 6
- attn_master: float32 [8, 1024, 1024], P(None, ('dp', 'fsdp')), may hold values from -2 to 2
- attn_first: float32 [8, 1024, 1024], P(None, ('dp', 'fsdp')), may hold values from -0.0034179688 to 0.0034179688
- attn_second: float32 [8, 1024, 1024], P(None, ('dp', 'fsdp')), may hold values from 2.9791412e-08 to 4.766626e-07
- mlp_master: float32 [2, 1024, 4096], P(None, ('dp', 'fsdp')), may hold values from -0.1875 to 0.1875
- mlp_first: float32 [2, 1024, 4096], P(None, ('dp', 'fsdp')), may hold values from -0.0034179688 to 0.0034179688
- mlp_second: float32 [2, 1024, 4096], P(None, ('dp', 'fsdp')), may hold values from 2.9791412e-08 to 4.766626e-07
- norm_master: float32 [6, 1024], P(None, ('dp', 'fsdp')), may hold values from -1.5 to 2.6
- norm_first: float32 [6, 1024], P(None, ('dp', 'fsdp')), may hold values from -0.0068359375 to 0.0068359375
- norm_second: float32 [6, 1024], P(None, ('dp', 'fsdp')), may hold values from 1.1916565e-07 to 1.9066504e-06
Outputs:
- output: bfloat16 [32, 1024, 1024], P(('dp', 'fsdp'))
- token_grad: float32 [32, 1024, 1024], P(('dp', 'fsdp'))
- prompt_grad: float32 [32, 128, 1024], P(('dp', 'fsdp'))
- grad_norm: float32 [], replicated
- attn_first_new: float32 [8, 1024, 1024], P(None, ('dp', 'fsdp'))
- attn_second_new: float32 [8, 1024, 1024], P(None, ('dp', 'fsdp'))
- attn_new: float32 [8, 1024, 1024], P(None, ('dp', 'fsdp'))
- attn_copy: bfloat16 [8, 1024, 1024], P(None, ('dp', 'fsdp'))
- mlp_first_new: float32 [2, 1024, 4096], P(None, ('dp', 'fsdp'))
- mlp_second_new: float32 [2, 1024, 4096], P(None, ('dp', 'fsdp'))
- mlp_new: float32 [2, 1024, 4096], P(None, ('dp', 'fsdp'))
- mlp_copy: bfloat16 [2, 1024, 4096], P(None, ('dp', 'fsdp'))
- norm_first_new: float32 [6, 1024], P(None, ('dp', 'fsdp'))
- norm_second_new: float32 [6, 1024], P(None, ('dp', 'fsdp'))
- norm_new: float32 [6, 1024], P(None, ('dp', 'fsdp'))
- norm_copy: bfloat16 [6, 1024], P(None, ('dp', 'fsdp'))
The draws below stay inside these ranges and needn't reach their ends.
Inputs may be any that keep to these rules, and one draw needn't show every extreme that they name: `prompt_len`: some item has a prompt of exactly 128 states and some of exactly 8.
All inputs are finite; a program needn't handle non-finite values.
Results may differ from the reference program's by a relative error of at most 0.022.
The reference program's roundings to bfloat16 on the way count: a program that leaves them out, or rounds other values in their place, can miss the bound.
Values may be sent and summed in bfloat16 or wider, within the bound.
No kernel may reach another device: no remote copies, remote signals or barrier semaphores. Data moves between devices by JAX's collectives and lax.ppermute only.
A program may use at most 448 MiB of HBM per device.

```python
import math
import jax
import jax.numpy as jnp
from jax import lax

D = 1024
HEADS = 16
HD = 64
FF = 4096
SEQ = 1024
PROMPT = 128
STEP = 10
ITEMS = 32
N_DP = 4
N_FSDP = 8


def draw_attn_master(key, part):
    key = jax.random.fold_in(key, 1)
    factors = jnp.array([1.3, 1.3, 1.0, 5.0, 1.3, 1.3, 1.0, 3.0], jnp.float32) * D ** (-0.5)
    base = jnp.clip(jax.random.normal(key, (8, D, D), jnp.float32), -4.0, 4.0)
    return base * factors[:, None, None]


def draw_norm_master(key, part):
    key = jax.random.fold_in(key, 2)
    first_key, second_key = jax.random.split(key)
    places = jnp.arange(D, dtype=jnp.int32)
    outer = (places // (D // N_DP)).astype(jnp.float32) / max(N_DP - 1, 1)
    inner = (places // (D // (N_DP * N_FSDP)) % N_FSDP).astype(jnp.float32) / max(N_FSDP - 1, 1)
    gains = 0.5 * 3.0 ** (0.5 * (outer + inner)) * jax.random.uniform(first_key, (3, D), jnp.float32, 0.8, 1.2)
    biases = jnp.clip(0.3 * jax.random.normal(second_key, (3, D), jnp.float32), -1.2, 1.2)
    return jnp.stack([gains, biases], axis=1).reshape(6, D)


def draw_prompt_len(key, part):
    key = jax.random.fold_in(key, 3)
    first_key, second_key = jax.random.split(key)
    lengths = jax.random.randint(first_key, (ITEMS,), 8, PROMPT + 1, jnp.int32)
    spots = jax.random.permutation(second_key, ITEMS)
    lengths = lengths.at[spots[0]].set(PROMPT)
    return lengths.at[spots[1]].set(8)


def block_scale(key, shape, shards, low, top_value):
    loudness, own = 1.0, jax.random.fold_in(key, 6)
    for position, blocks in shards:
        heights = jnp.exp(jax.random.uniform(jax.random.fold_in(own, position), (blocks,), jnp.float32, low / len(shards), top_value / len(shards)))
        loudness = loudness * jnp.repeat(heights, shape[position] // blocks).reshape([-1 if axis == position else 1 for axis in range(len(shape))])
    return loudness


def bell_draw(rng, extent, width, most, pieces=(), held_as=jnp.bfloat16):
    loudness = block_scale(rng, extent, pieces, -0.22, 0.18) if pieces else 1.0
    values = jax.random.normal(rng, extent, jnp.float32) * width * loudness
    return jnp.minimum(jnp.maximum(values, -most), most).astype(held_as)


def setup_inputs(seed: int = 0) -> dict:
    keys = jax.random.split(jax.random.key(seed), 14)
    tokens = bell_draw(keys[0], (ITEMS, SEQ, D), 1.0, 6.0, ((0, 32),))
    prompt = bell_draw(keys[1], (ITEMS, PROMPT, D), 1.0, 6.0, ((0, 32),))
    prompt_len = draw_prompt_len(jax.random.fold_in(keys[13], 71), 0)
    cotangent = bell_draw(keys[3], (ITEMS, SEQ, D), 1.0, 6.0, ((0, 32),))
    attn_master = draw_attn_master(jax.random.fold_in(keys[13], 71), 0)
    attn_first = bell_draw(keys[5], (8, D, D), ((8 * D * D + 2 * D * FF + 6 * D) ** -0.5), 0.0034179688, ((1, 32),), jnp.float32)
    attn_second = jnp.clip(jnp.exp(math.log(4.7666259206380346e-07) - 2.7725887 * jax.random.uniform(keys[6], (8, D, D), jnp.float32) ** block_scale(keys[6], (8, D, D), ((1, 32),), -0.2, 0.2)), 2.9791412003987716e-08, 4.7666259206380346e-07)
    mlp_master = bell_draw(keys[7], (2, D, FF), D ** -0.5, 0.1875, ((1, 32),), jnp.float32)
    mlp_first = bell_draw(keys[8], (2, D, FF), ((8 * D * D + 2 * D * FF + 6 * D) ** -0.5), 0.0034179688, ((1, 32),), jnp.float32)
    mlp_second = jnp.clip(jnp.exp(math.log(4.7666259206380346e-07) - 2.7725887 * jax.random.uniform(keys[9], (2, D, FF), jnp.float32) ** block_scale(keys[9], (2, D, FF), ((1, 32),), -0.2, 0.2)), 2.9791412003987716e-08, 4.7666259206380346e-07)
    norm_master = draw_norm_master(jax.random.fold_in(keys[13], 71), 0)
    norm_first = bell_draw(keys[11], (6, D), (2 * (8 * D * D + 2 * D * FF + 6 * D) ** -0.5), 0.0068359375, ((1, 32),), jnp.float32)
    norm_second = jnp.clip(jnp.exp(math.log(1.9066503682552138e-06) - 2.7725887 * jax.random.uniform(keys[12], (6, D), jnp.float32) ** block_scale(keys[12], (6, D), ((1, 32),), -0.2, 0.2)), 1.1916564801595086e-07, 1.9066503682552138e-06)
    return dict(tokens=tokens, prompt=prompt, prompt_len=prompt_len, cotangent=cotangent, attn_master=attn_master, attn_first=attn_first, attn_second=attn_second, mlp_master=mlp_master, mlp_first=mlp_first, mlp_second=mlp_second, norm_master=norm_master, norm_first=norm_first, norm_second=norm_second)


EPSILON = 1e-05
CLIP_NORM = 1.0
BETA_ONE = 0.5
BETA_TWO = 0.5
MATRIX_RATE = 0.04
VECTOR_RATE = 0.3
WEIGHT_DECAY = 0.1
ADAM_EPSILON = 1e-08
SCORE_SCALE = 0.125
HIGHEST_PREC = lax.Precision.HIGHEST

@jax.custom_vjp
def low(v):
    return lax.optimization_barrier(v.astype(jnp.bfloat16)).astype(jnp.float32)

@jax.custom_vjp
def low_back(v):
    return v

def low_keep(v):
    return (low(v), None)

def low_pass(kept, grad):
    return (grad,)

def back_keep(v):
    return (v, None)

def back_low(kept, grad):
    return (low(grad),)
low.defvjp(low_keep, low_pass)
low_back.defvjp(back_keep, back_low)

def layer_norm(vector, norm_gain, norm_bias):
    centre = lax.optimization_barrier(jnp.mean(vector, axis=-1, keepdims=True))
    centred = vector - centre
    spread = lax.optimization_barrier(jnp.mean(centred * centred, axis=-1, keepdims=True))
    return centred * lax.rsqrt(spread + EPSILON) * norm_gain + norm_bias

def rounded(value):
    return low_back(low(value))

def product(left, right):
    return jnp.dot(left, right, precision=HIGHEST_PREC)

def attention(queries, keys_all, values_all, allowed):
    block_rows = min(512, SEQ)
    blocks = queries.reshape(SEQ // block_rows, block_rows, HEADS, HD)
    offsets = jnp.arange(SEQ // block_rows, dtype=jnp.int32) * block_rows

    def one_block(pair):
        query_block, offset = pair
        scores = low_back(SCORE_SCALE * jnp.einsum('qhe,khe->hqk', query_block, keys_all, precision=HIGHEST_PREC))
        positions = offset + jnp.arange(block_rows, dtype=jnp.int32)
        scores = jnp.where(allowed(positions)[None], scores, -1000000000.0)
        attn_probs = low(jax.nn.softmax(scores, axis=-1))
        return jnp.einsum('hqk,khe->qhe', attn_probs, values_all, precision=HIGHEST_PREC)
    mixed = lax.map(jax.checkpoint(one_block), (blocks, offsets))
    return mixed.reshape(SEQ, HEADS * HD)

def forward(inputs, states, prompt_size, attn_weights, mlp_weights, norm_weights):
    key_places = jnp.arange(SEQ, dtype=jnp.int32)
    prompt_places = jnp.arange(PROMPT, dtype=jnp.int32)

    def causal(positions):
        return positions[:, None] >= key_places[None, :]

    def padded(positions):
        return jnp.broadcast_to(prompt_places[None, :] < prompt_size, (positions.shape[0], PROMPT))
    normed_one = low(layer_norm(inputs, norm_weights[0], norm_weights[1]))
    queries = rounded(product(normed_one, attn_weights[0])).reshape(SEQ, HEADS, HD)
    keys_self = rounded(product(normed_one, attn_weights[1])).reshape(SEQ, HEADS, HD)
    values_self = rounded(product(normed_one, attn_weights[2])).reshape(SEQ, HEADS, HD)
    mixed = rounded(attention(queries, keys_self, values_self, causal))
    after_self = inputs + low_back(product(mixed, attn_weights[3]))
    normed_two = low(layer_norm(after_self, norm_weights[2], norm_weights[3]))
    cross_queries = rounded(product(normed_two, attn_weights[4])).reshape(SEQ, HEADS, HD)
    cross_keys = rounded(product(states, attn_weights[5])).reshape(PROMPT, HEADS, HD)
    cross_values = rounded(product(states, attn_weights[6])).reshape(PROMPT, HEADS, HD)
    crossed = rounded(attention(cross_queries, cross_keys, cross_values, padded))
    after_cross = after_self + low_back(product(crossed, attn_weights[7]))
    normed_three = low(layer_norm(after_cross, norm_weights[4], norm_weights[5]))
    hidden = low_back(product(normed_three, mlp_weights[0]))
    activated = low(jax.nn.gelu(hidden, approximate=False))
    return after_cross + low_back(product(activated, mlp_weights[1].T))

def adam_update(master, first, second, gradient, factor, rate, decay):
    gradient = gradient * factor
    first_new = BETA_ONE * first + (1.0 - BETA_ONE) * gradient
    second_new = BETA_TWO * second + (1.0 - BETA_TWO) * gradient * gradient
    first_fix = 1.0 - BETA_ONE ** STEP
    second_fix = 1.0 - BETA_TWO ** STEP
    update = first_new / first_fix / (jnp.sqrt(second_new / second_fix) + ADAM_EPSILON)
    master_new = master - rate * (update + decay * master)
    return (first_new, second_new, master_new, master_new.astype(jnp.bfloat16))

def reference(tokens, prompt, prompt_len, cotangent, attn_master, attn_first, attn_second, mlp_master, mlp_first, mlp_second, norm_master, norm_first, norm_second):
    attn_weights = low(attn_master)
    mlp_weights = low(mlp_master)
    norm_weights = low(norm_master)

    def item_step(carry, item_data):
        inputs, states, prompt_size, upstream = item_data

        def local_pass(inputs_in, states_in, attn_in, mlp_in, norm_in):
            return forward(inputs_in, states_in, prompt_size, attn_in, mlp_in, norm_in)
        result, pullback = jax.vjp(local_pass, inputs, states, attn_weights, mlp_weights, norm_weights)
        grad_inputs, grad_states, grad_attn, grad_mlp, grad_norms = pullback(upstream)
        carry = (carry[0] + grad_attn, carry[1] + grad_mlp, carry[2] + grad_norms)
        return (carry, (result.astype(jnp.bfloat16), grad_inputs, grad_states))
    initial = (jnp.zeros((8, D, D), jnp.float32), jnp.zeros((2, D, FF), jnp.float32), jnp.zeros((6, D), jnp.float32))
    totals, per_item = lax.scan(item_step, initial, (tokens.astype(jnp.float32), prompt.astype(jnp.float32), prompt_len, cotangent.astype(jnp.float32)))
    grad_attn, grad_mlp, grad_norms = totals
    output, token_grad, prompt_grad = per_item
    squares = jnp.sum(grad_attn * grad_attn) + jnp.sum(grad_mlp * grad_mlp) + jnp.sum(grad_norms * grad_norms)
    grad_norm = jnp.sqrt(squares)
    factor = CLIP_NORM / jnp.maximum(grad_norm, CLIP_NORM)
    attn_out = adam_update(attn_master, attn_first, attn_second, grad_attn, factor, MATRIX_RATE, WEIGHT_DECAY)
    mlp_out = adam_update(mlp_master, mlp_first, mlp_second, grad_mlp, factor, MATRIX_RATE, WEIGHT_DECAY)
    norm_out = adam_update(norm_master, norm_first, norm_second, grad_norms, factor, VECTOR_RATE, 0.0)
    return (output, token_grad, prompt_grad, grad_norm, attn_out[0], attn_out[1], attn_out[2], attn_out[3], mlp_out[0], mlp_out[1], mlp_out[2], mlp_out[3], norm_out[0], norm_out[1], norm_out[2], norm_out[3])
```

```python
import functools

import jax
import jax.numpy as jnp
from jax import lax
from jax.experimental import pallas as pl
from jax.experimental.pallas import tpu as pltpu
from jax.sharding import PartitionSpec as P

HD = 64
PAIR = 2 * HD
STEP = 10
TILE = 256

EPSILON = 1e-05
CLIP_NORM = 1.0
BETA_ONE = 0.5
BETA_TWO = 0.5
MATRIX_RATE = 0.04
VECTOR_RATE = 0.3
WEIGHT_DECAY = 0.1
ADAM_EPSILON = 1e-08
SCORE_SCALE = 0.125
MASKED = -1000000000.0
AXES = ("dp", "chip", "core")
LOW = jnp.bfloat16
FULL = jnp.float32


def dot_nn(left, right):
    return lax.dot_general(left, right, (((1,), (0,)), ((), ())), preferred_element_type=FULL)


def dot_nt(left, right):
    return lax.dot_general(left, right, (((1,), (1,)), ((), ())), preferred_element_type=FULL)


def dot_tn(left, right):
    return lax.dot_general(left, right, (((0,), (0,)), ((), ())), preferred_element_type=FULL)


def lane_masks(rows):
    lane = lax.broadcasted_iota(jnp.int32, (rows, PAIR), 1)
    return (lane < HD, lane >= HD)


def forward_pair(queries, keys, values, causal, limit):
    seq = queries.shape[0]
    span = keys.shape[0]
    block = min(TILE, seq)
    masks = lane_masks(block)
    key_masks = lane_masks(span)
    counted = [jnp.where(mask, values, jnp.ones_like(values)) for mask in key_masks]

    def score(start):
        found = []
        for head in range(2):
            query = queries[start : start + block]
            query = jnp.where(masks[head], query, jnp.zeros_like(query)) * SCORE_SCALE
            if causal:
                row = lax.broadcasted_iota(jnp.int32, (block, block), 0)
                col = lax.broadcasted_iota(jnp.int32, (block, block), 1)
                parts = [(start, start + block, col <= row)]
                if start:
                    parts.append((0, start, None))
            else:
                col = lax.broadcasted_iota(jnp.int32, (block, span), 1)
                parts = [(0, span, col < limit)]
            scores = []
            for low, high, allowed in parts:
                value = dot_nt(query, keys[low:high])
                if allowed is not None:
                    value = jnp.where(allowed, value, MASKED)
                scores.append((low, high, value))
            found.append(scores)
        return found

    results = []
    ahead = score(0)
    for start in range(0, seq, block):
        found = ahead
        if start + block < seq:
            ahead = score(start + block)
        peaks, sums = [], []
        for head in range(2):
            peak = None
            for _, _, value in found[head]:
                most = jnp.max(value, axis=1, keepdims=True)
                peak = most if peak is None else jnp.maximum(peak, most)
            peaks.append(peak)
        for head in range(2):
            mixed = None
            for low, high, value in found[head]:
                weight = jnp.exp(value - peaks[head]).astype(LOW)
                part = dot_nn(weight, counted[head][low:high])
                mixed = part if mixed is None else mixed + part
            sums.append(mixed)
        mixed = jnp.where(masks[0], sums[0], sums[1])
        total = pltpu.roll(jnp.where(masks[0], sums[1], sums[0]), HD, 1)
        level = jnp.where(masks[0], peaks[0], peaks[1]) + jnp.log(total)
        results.append((start, start + block, (mixed / total).astype(LOW), level.T))
    return results


def backward_pair(queries, keys, values, mixed, upstream, levels, causal, limit):
    seq = queries.shape[0]
    span = keys.shape[0]
    block = min(TILE, span)
    masks = lane_masks(block)
    scaled = queries * SCORE_SCALE
    inner = (upstream.astype(FULL) * mixed.astype(FULL)).T
    products = [
        jnp.sum(inner[HD * head : HD * (head + 1)], axis=0, keepdims=True) for head in range(2)
    ]
    units = []
    for low in range(0, span, block):
        for head in range(2):
            if not causal:
                units.append((low, head, 0, seq, True))
                continue
            units.append((low, head, low, low + block, True))
            if low + block < seq:
                units.append((low, head, low + block, seq, False))

    def scores(unit):
        low, head, begin, end, checked = unit
        key, value = keys[low : low + block], values[low : low + block]
        key = jnp.where(masks[head], key, jnp.zeros_like(key))
        value = jnp.where(masks[head], value, jnp.zeros_like(value))
        return dot_nt(key, scaled[begin:end]), dot_nt(value, upstream[begin:end])

    def exponents(unit, score, grad_weight):
        low, head, begin, end, checked = unit
        if checked:
            row = lax.broadcasted_iota(jnp.int32, (block, end - begin), 0) + low
            if causal:
                col = lax.broadcasted_iota(jnp.int32, (block, end - begin), 1) + begin
                allowed = row <= col
            else:
                allowed = row < limit
            score = jnp.where(allowed, score, MASKED)
        weight = jnp.exp(score - levels[8 * head : 8 * head + 1, begin:end])
        grad_score = (weight * (grad_weight - products[head][:, begin:end])).astype(LOW)
        return weight.astype(LOW), grad_score

    grad_q = [[None] * (seq // block) for _ in range(2)]
    sums_k, sums_v = {}, {}

    def gather(unit, weight, grad_score):
        low, head, begin, end, _ = unit
        part_v = dot_nn(weight, upstream[begin:end])
        part_k = dot_nn(grad_score, scaled[begin:end])
        part_q = dot_tn(grad_score, keys[low : low + block])
        for sums, part in ((sums_k, part_k), (sums_v, part_v)):
            old = sums.get((low, head))
            sums[low, head] = part if old is None else old + part
        for at in range(begin, end, block):
            piece = part_q[at - begin : at - begin + block]
            old = grad_q[head][at // block]
            grad_q[head][at // block] = piece if old is None else old + piece

    ahead = scores(units[0])
    for number, unit in enumerate(units):
        found = ahead
        if number + 1 < len(units):
            ahead = scores(units[number + 1])
        gather(unit, *exponents(unit, *found))

    grad_k, grad_v, done_q = [], [], []
    for low in range(0, span, block):
        for sums, out in ((sums_k, grad_k), (sums_v, grad_v)):
            value = jnp.where(masks[0], sums[low, 0], sums[low, 1])
            out.append((low, low + block, value.astype(LOW)))
    for number, (one, two) in enumerate(zip(grad_q[0], grad_q[1])):
        value = (jnp.where(masks[0], one, two) * SCORE_SCALE).astype(LOW)
        done_q.append((number * block, (number + 1) * block, value))
    return done_q, grad_k, grad_v


def self_forward_kernel(qkv_ref, out_ref, level_ref):
    queries = qkv_ref[:, :PAIR]
    keys = qkv_ref[:, PAIR : 2 * PAIR]
    values = qkv_ref[:, 2 * PAIR :]
    for start, stop, out, level in forward_pair(queries, keys, values, True, None):
        out_ref[start:stop, :] = out
        level_ref[0, 0:8, start:stop] = level[0:8]
        level_ref[0, 8:16, start:stop] = level[HD : HD + 8]


def self_backward_kernel(qkv_ref, mixed_ref, upstream_ref, level_ref, *rest):
    grad_ref = rest[-1]
    queries = qkv_ref[:, :PAIR]
    keys = qkv_ref[:, PAIR : 2 * PAIR]
    values = qkv_ref[:, 2 * PAIR :]
    found = backward_pair(
        queries, keys, values, mixed_ref[...], upstream_ref[...], level_ref[0], True, None
    )
    for place, rows in enumerate(found):
        for start, stop, value in rows:
            grad_ref[start:stop, place * PAIR : (place + 1) * PAIR] = value


def cross_forward_kernel(limit_ref, query_ref, kv_ref, out_ref, level_ref):
    found = forward_pair(query_ref[...], kv_ref[:, :PAIR], kv_ref[:, PAIR:], False, limit_ref[0])
    for start, stop, out, level in found:
        out_ref[start:stop, :] = out
        level_ref[0, 0:8, start:stop] = level[0:8]
        level_ref[0, 8:16, start:stop] = level[HD : HD + 8]


def cross_backward_kernel(
    limit_ref, query_ref, kv_ref, mixed_ref, upstream_ref, level_ref, grad_q_ref, grad_kv_ref
):
    found = backward_pair(
        query_ref[...],
        kv_ref[:, :PAIR],
        kv_ref[:, PAIR:],
        mixed_ref[...],
        upstream_ref[...],
        level_ref[0],
        False,
        limit_ref[0],
    )
    for start, stop, value in found[0]:
        grad_q_ref[start:stop, :] = value
    for place, rows in enumerate(found[1:]):
        for start, stop, value in rows:
            grad_kv_ref[start:stop, place * PAIR : (place + 1) * PAIR] = value


LARGE = pltpu.CompilerParams(vmem_limit_bytes=56 * 1024 * 1024)
MIDDLE = pltpu.CompilerParams(vmem_limit_bytes=42 * 1024 * 1024)
PARAMS = pltpu.CompilerParams(vmem_limit_bytes=28 * 1024 * 1024)
SCALAR = pl.BlockSpec(memory_space=pltpu.SMEM)


def columns(rows, width, offset=0):
    return pl.BlockSpec((rows, width), lambda pair: (0, pair + offset))


def planes(seq):
    return pl.BlockSpec((1, 16, seq), lambda pair: (pair, 0, 0))


SHORT = pl.CostEstimate(flops=1, bytes_accessed=1, transcendentals=0)


def self_forward(qkv):
    seq, width = qkv.shape[0], qkv.shape[1] // 3
    pairs = width // PAIR
    return pl.pallas_call(
        self_forward_kernel,
        grid=(pairs,),
        in_specs=[columns(seq, 3 * PAIR)],
        out_specs=[columns(seq, PAIR), planes(seq)],
        out_shape=[
            jax.ShapeDtypeStruct((seq, width), LOW),
            jax.ShapeDtypeStruct((pairs, 16, seq), FULL),
        ],
        compiler_params=LARGE,
        cost_estimate=SHORT,
        name="self_forward",
    )(qkv)


def self_backward(qkv, mixed, upstream, levels, start, count, total=None, at=0, old=None):
    seq = qkv.shape[0]
    total = count if total is None else total
    old = [] if old is None else [old]
    return pl.pallas_call(
        self_backward_kernel,
        grid=(count,),
        in_specs=[
            columns(seq, 3 * PAIR, start),
            columns(seq, PAIR, start),
            columns(seq, PAIR, start),
            pl.BlockSpec((1, 16, seq), lambda pair: (pair + start, 0, 0)),
        ]
        + [pl.BlockSpec(memory_space=pl.ANY)] * len(old),
        out_specs=columns(seq, 3 * PAIR, at),
        out_shape=jax.ShapeDtypeStruct((seq, 3 * PAIR * total), LOW),
        input_output_aliases={4: 0} if old else {},
        compiler_params=PARAMS,
        cost_estimate=SHORT,
        name="self_backward",
    )(qkv, mixed, upstream, levels, *old)


def cross_forward(limit, queries, pair_states):
    seq, width = queries.shape
    span = pair_states.shape[0]
    pairs = width // PAIR
    return pl.pallas_call(
        cross_forward_kernel,
        grid=(pairs,),
        in_specs=[SCALAR, columns(seq, PAIR), columns(span, 2 * PAIR)],
        out_specs=[columns(seq, PAIR), planes(seq)],
        out_shape=[
            jax.ShapeDtypeStruct((seq, width), LOW),
            jax.ShapeDtypeStruct((pairs, 16, seq), FULL),
        ],
        compiler_params=PARAMS,
        cost_estimate=SHORT,
        name="cross_forward",
    )(limit, queries, pair_states)


def cross_backward(limit, queries, pair_states, mixed, upstream, levels):
    seq, width = queries.shape
    span = pair_states.shape[0]
    pairs = width // PAIR
    return pl.pallas_call(
        cross_backward_kernel,
        grid=(pairs,),
        in_specs=[
            SCALAR,
            columns(seq, PAIR),
            columns(span, 2 * PAIR),
            columns(seq, PAIR),
            columns(seq, PAIR),
            planes(seq),
        ],
        out_specs=[columns(seq, PAIR), columns(span, 2 * PAIR)],
        out_shape=[
            jax.ShapeDtypeStruct((seq, width), LOW),
            jax.ShapeDtypeStruct((span, 2 * width), LOW),
        ],
        compiler_params=PARAMS,
        cost_estimate=SHORT,
        name="cross_backward",
    )(limit, queries, pair_states, mixed, upstream, levels)


def mlp_kernel(order, core_ref, rows_ref, grad_ref, up_ref, down_ref, *rest):
    del core_ref
    count = 2 + max(piece for _, _, piece, _ in order) * 2
    halves_refs, rest = rest[-4 - count : -4], rest[-4:]
    out_ref, back_ref, rows_turned_ref, grad_turned_ref = rest
    step = pl.program_id(0)

    @pl.when(step == 0)
    def _():
        rows_turned_ref[...] = rows_ref[...].T
        grad_turned_ref[...] = grad_ref[...].T
        back_ref[...] = jnp.zeros_like(back_ref)

    seq = rows_ref.shape[0]
    size = min(512, seq)
    width = up_ref.shape[1]

    def ahead(start):
        rows = slice(start, start + size)
        return dot_nn(rows_ref[rows, :], up_ref[...]), dot_nn(grad_ref[rows, :], down_ref[...])

    down_grad, up_grad = None, None
    found = ahead(0)
    for start in range(0, seq, size):
        hidden, grad = found
        if start + size < seq:
            found = ahead(start + size)
        rows = slice(start, start + size)
        share = 0.5 + 0.5 * lax.erf(hidden * 0.7071067811865476)
        bell = jnp.exp(hidden * hidden * -0.5)
        active = (hidden * share).astype(LOW)
        grad_hidden = (grad * (share + hidden * (bell * 0.3989422804014327))).astype(LOW)
        out_ref[rows, :] = active
        down_part = dot_nn(grad_turned_ref[:, rows], active)
        up_part = dot_nn(rows_turned_ref[:, rows], grad_hidden)
        back_ref[rows, :] += dot_nt(grad_hidden, up_ref[...])
        down_grad = down_part if start == 0 else down_grad + down_part
        up_grad = up_part if start == 0 else up_grad + up_part

    for number, half_ref in enumerate(halves_refs):
        steps = [
            at for at, (_, side, piece, _) in enumerate(order) if 2 * piece + 1 - side == number
        ]

        @pl.when((step >= steps[0]) & (step <= steps[-1]))
        def _(half_ref=half_ref):
            half_ref[:, :width] = down_grad.astype(LOW)
            half_ref[:, width:] = up_grad.astype(LOW)


def mlp(core, rows, grad, weights, up_at, down_at, order, old=None):
    seq, width = rows.shape
    block = width // 2
    pieces = 1 + max(piece for _, _, piece, _ in order)

    def chosen(j, values):
        found = values[0]
        for number, value in enumerate(values[1:], 1):
            found = jnp.where(j == number, value, found)
        return found

    def place(j, core):
        quarter = chosen(j, [quarter for quarter, _, _, _ in order])
        return 2 * quarter + (core[0] ^ chosen(j, [side for _, side, _, _ in order]))

    def strip(start):
        return pl.BlockSpec((width, block), lambda j, core: (0, start // block + place(j, core)))

    once = pl.Buffered(1)

    def strips(number):
        mine = [at for at, (_, side, piece, _) in enumerate(order) if 2 * piece + 1 - side == number]
        places = [order[min(max(at, mine[0]), mine[-1])][3] for at in range(len(order))]
        return pl.BlockSpec(
            (width, width), lambda j, core: (0, chosen(j, places)), pipeline_mode=once
        )

    old = [] if old is None else list(old)
    whole = pl.BlockSpec((seq, width), lambda j, core: (0, 0), pipeline_mode=once)
    return pl.pallas_call(
        functools.partial(mlp_kernel, order),
        grid_spec=pltpu.PrefetchScalarGridSpec(
            num_scalar_prefetch=1,
            grid=(len(order),),
            in_specs=[whole, whole, strip(up_at), strip(down_at)]
            + [pl.BlockSpec(memory_space=pl.ANY)] * len(old),
            out_specs=[strips(number) for number in range(2 * pieces)]
            + [pl.BlockSpec((seq, block), lambda j, core: (0, place(j, core))), whole],
            scratch_shapes=[pltpu.VMEM((width, seq), LOW)] * 2,
        ),
        out_shape=[jax.ShapeDtypeStruct((width, 2 * width), LOW)] * (2 * pieces)
        + [
            jax.ShapeDtypeStruct((seq, len(order) * block), LOW),
            jax.ShapeDtypeStruct((seq, width), FULL),
        ],
        input_output_aliases={5: 0, 6: 1} if old else {},
        compiler_params=MIDDLE,
        cost_estimate=SHORT,
        name="mlp",
    )(core, rows, grad, weights, weights, *old)


def matmul_kernel(left_ref, right_ref, out_ref):
    out_ref[...] = dot_nn(left_ref[...], right_ref[...]).astype(LOW)


def matmul(left, right, at, count):
    seq, depth = left.shape
    block = min(512, count)
    return pl.pallas_call(
        matmul_kernel,
        grid=(count // block,),
        in_specs=[
            pl.BlockSpec((seq, depth), lambda step: (0, 0)),
            pl.BlockSpec((depth, block), lambda step: (0, at // block + step)),
        ],
        out_specs=pl.BlockSpec((seq, block), lambda step: (0, step)),
        out_shape=jax.ShapeDtypeStruct((seq, count), LOW),
        compiler_params=PARAMS,
        cost_estimate=SHORT,
        name="matmul",
    )(left, right)


def turned_kernel(left_ref, right_ref, out_ref):
    out_ref[...] = dot_nt(left_ref[...], right_ref[...])


def matmul_turned(left, right, at):
    seq, depth = left.shape
    width = right.shape[0]
    block = min(512, width)
    return pl.pallas_call(
        turned_kernel,
        grid=(width // block,),
        in_specs=[
            pl.BlockSpec((seq, depth), lambda step: (0, 0)),
            pl.BlockSpec((block, depth), lambda step: (step, at // depth)),
        ],
        out_specs=pl.BlockSpec((seq, block), lambda step: (0, step)),
        out_shape=jax.ShapeDtypeStruct((seq, width), FULL),
        compiler_params=PARAMS,
        cost_estimate=SHORT,
        name="matmul_turned",
    )(left, right)


def product_kernel(core_ref, left_ref, sent_ref, kept_ref, *rest):
    del core_ref
    send_ref, keep_ref, turned_ref = rest[-3:]

    @pl.when(pl.program_id(0) == 0)
    def _():
        turned_ref[...] = left_ref[...].T

    send_ref[...] = dot_nn(turned_ref[...], sent_ref[...]).astype(LOW)
    keep_ref[...] = dot_nn(turned_ref[...], kept_ref[...]).astype(LOW)


def product(core, left, right, total=None, at=0, old=None):
    rows, width = left.shape
    half = right.shape[1] // 2
    block = max(b for b in (128, 256, 384, 512) if half % b == 0 and at % b == 0)
    steps, offset = half // block, at // block
    total = half if total is None else total
    old = [] if old is None else list(old)
    return pl.pallas_call(
        product_kernel,
        grid_spec=pltpu.PrefetchScalarGridSpec(
            num_scalar_prefetch=1,
            grid=(steps,),
            in_specs=[
                pl.BlockSpec((rows, width), lambda j, core: (0, 0)),
                pl.BlockSpec((rows, block), lambda j, core: (0, (1 - core[0]) * steps + j)),
                pl.BlockSpec((rows, block), lambda j, core: (0, core[0] * steps + j)),
            ]
            + [pl.BlockSpec(memory_space=pl.ANY)] * len(old),
            out_specs=[pl.BlockSpec((width, block), lambda j, core: (0, offset + j))] * 2,
            scratch_shapes=[pltpu.VMEM((width, rows), LOW)],
        ),
        out_shape=[jax.ShapeDtypeStruct((width, total), LOW)] * 2,
        input_output_aliases={4: 0, 5: 1} if old else {},
        compiler_params=PARAMS,
        cost_estimate=SHORT,
        name="product",
    )(core, left, right, right, *old)


def pack_kernel(attn_ref, mlp_ref, norm_ref, out_ref, rest_ref):
    width = attn_ref.shape[2]
    hidden = mlp_ref.shape[2]
    quarter = hidden // 4
    for pair in range(width // PAIR):
        source = slice(pair * PAIR, (pair + 1) * PAIR)
        for kind in range(3):
            place = (3 * pair + kind) * PAIR
            out_ref[:, place : place + PAIR] = attn_ref[kind, :, source].astype(LOW)
        for kind in range(2):
            place = 5 * width + (2 * pair + kind) * PAIR
            out_ref[:, place : place + PAIR] = attn_ref[5 + kind, :, source].astype(LOW)
    out_ref[:, 3 * width : 4 * width] = attn_ref[3].astype(LOW)
    out_ref[:, 4 * width : 5 * width] = attn_ref[4].astype(LOW)
    out_ref[:, 7 * width : 8 * width] = attn_ref[7].astype(LOW)
    for kind in range(2):
        place = 8 * width + kind * quarter
        out_ref[:, place : place + quarter] = mlp_ref[kind, :, :quarter].astype(LOW)
        place = kind * 3 * quarter
        rest_ref[:, place : place + 3 * quarter] = mlp_ref[kind, :, quarter:].astype(LOW)
    out_ref[:, 8 * width + 2 * quarter :] = norm_ref[...].astype(LOW)


def pack(attn_master, mlp_master, norm_columns):
    _, rows, width = attn_master.shape
    hidden = mlp_master.shape[2]
    return pl.pallas_call(
        pack_kernel,
        out_shape=[
            jax.ShapeDtypeStruct((rows, 8 * width + hidden // 2 + norm_columns.shape[1]), LOW),
            jax.ShapeDtypeStruct((rows, 3 * hidden // 2), LOW),
        ],
        compiler_params=PARAMS,
        cost_estimate=SHORT,
        name="pack",
    )(attn_master, mlp_master, norm_columns)


class Grid:
    def __init__(self, sizes):
        self.outer, self.chips = sizes
        self.inner = 2 * self.chips
        self.count = self.outer * self.inner
        self.bits = (self.count - 1).bit_length()
        self.core = lax.axis_index("core")
        self.me = lax.axis_index(AXES)
        self.plane = lax.axis_index("dp")
        near = ((self.chips - 1).bit_length() + 1) // 2
        self.x = list(range(near, 0, -1))
        self.y = list(range((self.chips - 1).bit_length(), near, -1))

    def own(self, bit):
        return lax.shift_right_logical(self.me, jnp.int32(bit)) & 1

    def turn(self, value, mask):
        return lax.ppermute(value, AXES, [(i, i ^ mask) for i in range(self.count)])

    def add_all(self, value):
        for bit in range(self.bits):
            value = value + self.turn(value, 1 << bit)
        return value

    def unpair(self, total):
        total = total.reshape(2, total.shape[0] // 2, total.shape[1])
        mine = lax.dynamic_index_in_dim(total, self.core, 0, keepdims=False)
        other = lax.dynamic_index_in_dim(total, 1 - self.core, 0, keepdims=False)
        return mine, self.turn(other, 1)


def add_kernel(counts, side_ref, *refs):
    del side_ref
    outs = refs[sum(counts) :]
    at = 0
    for count, out_ref in zip(counts, outs):
        total = refs[at][...].reshape(out_ref.shape).astype(FULL)
        for ref in refs[at + 1 : at + count]:
            total = total + ref[...].reshape(out_ref.shape).astype(FULL)
        out_ref[...] = total.astype(LOW)
        at += count


def layer_kernel(outer, steps, first, one, two, side_ref, *refs):
    ins, outs = refs[: first + one + two], refs[first + one + two :]

    def fill(parts):
        for step in range(outer):
            plane = side_ref[0] ^ step
            out_ref = outs[step]
            total = parts[0][plane].reshape(out_ref.shape).astype(FULL)
            for part in parts[1:]:
                total = total + part[plane].reshape(out_ref.shape).astype(FULL)
            out_ref[...] = total.astype(out_ref.dtype)

    @pl.when(pl.program_id(0) < steps)
    def _():
        fill(ins[:first] + ins[first : first + one])

    @pl.when(pl.program_id(0) >= steps)
    def _():
        fill(ins[:first] + ins[first + one :])


def plane_kernel(steps, first, one, two, side_ref, *refs):
    del side_ref
    ins, out_ref = refs[:-1], refs[-1]

    def fill(parts):
        total = parts[0][...].reshape(out_ref.shape).astype(FULL)
        for part in parts[1:]:
            total = total + part[...].reshape(out_ref.shape).astype(FULL)
        out_ref[...] = total.astype(LOW)

    @pl.when(pl.program_id(0) < steps)
    def _():
        fill(ins[:first] + ins[first : first + one])

    @pl.when(pl.program_id(0) >= steps)
    def _():
        fill(ins[:first] + ins[first + one :])


class Sum:
    def __init__(self, grid, keep, got):
        self.grid = grid
        self.bits = sorted(grid.x + grid.y, reverse=True)
        self.cut = keep.shape[1] // 2
        self.block = max(b for b in (128, 256, 384, 512, 640) if self.cut % b == 0)
        self.steps = self.cut // self.block
        self.base = [(keep, []), (got, [])]
        self.orders = [grid.x + grid.y, grid.y + grid.x]
        self.extra = [[], []]
        self.stages = len(self.bits)
        sides = [grid.plane] + [grid.own(bit) for bit in self.bits]
        self.sides = jnp.stack(sides).astype(jnp.int32)

    def view(self, term):
        value, done = term
        left = [bit for bit in self.bits if bit not in done]
        outer = self.grid.outer
        share = value.shape[0] // (outer << len(left))
        return value.reshape([outer] + [2] * len(left) + [share, value.shape[1]]), left

    def spec(self, view, left, flips, column):
        places = {bit: 1 + self.bits.index(bit) for bit in flips}

        def index(j, side):
            picks = [
                (side[places[bit]] ^ flips[bit]) if bit in flips else 0 for bit in left
            ]
            return (0, *picks, 0, column(j))

        shape = [view.shape[0]] + [1 if bit in flips else 2 for bit in left]
        return pl.BlockSpec((*shape, view.shape[-2], self.block), index)

    def call(self, kernel, grid, views, specs, out_specs, out_shape, name):
        return pl.pallas_call(
            kernel,
            grid_spec=pltpu.PrefetchScalarGridSpec(
                num_scalar_prefetch=1, grid=grid, in_specs=specs, out_specs=out_specs
            ),
            out_shape=out_shape,
            compiler_params=PARAMS,
            cost_estimate=SHORT,
            name=name,
        )(self.sides, *views)

    def send(self, stage):
        views, specs, counts = [], [], []
        for half, order in enumerate(self.orders):
            flips = {bit: 0 for bit in order[:stage]}
            flips[order[stage]] = 1
            terms = self.base + self.extra[half]
            counts.append(len(terms))
            for number, term in enumerate(terms):
                view, left = self.view(term)
                shift = half * self.steps if number < len(self.base) else 0
                views.append(view)
                picked = {bit: flip for bit, flip in flips.items() if bit in left}
                specs.append(self.spec(view, left, picked, lambda j, shift=shift: shift + j))
        rows = self.base[0][0].shape[0] >> (stage + 1)
        return self.call(
            functools.partial(add_kernel, counts),
            (self.steps,),
            views,
            specs,
            [pl.BlockSpec((rows, self.block), lambda j, side: (0, j))] * 2,
            [jax.ShapeDtypeStruct((rows, self.cut), LOW)] * 2,
            "add",
        )

    def swap(self, stage, out):
        return [self.grid.turn(v, 1 << order[stage]) for order, v in zip(self.orders, out)]

    def receive(self, stage, got):
        for half, value in enumerate(got):
            self.extra[half].append((value, self.orders[half][: stage + 1]))

    def between(self, main):
        for stage in range(1, self.stages - 1):
            main, sent = tie((main, self.send(stage)))
            main, got = tie((main, self.swap(stage, sent)))
            self.receive(stage, got)
        return main

    def layers(self):
        views, specs, counts = self.columns()
        outer = self.grid.outer
        share = views[0].shape[-2]
        shape = (share, 2 * self.cut)
        return self.call(
            functools.partial(layer_kernel, outer, self.steps, *counts),
            (2 * self.steps,),
            views,
            specs,
            [pl.BlockSpec((share, self.block), lambda j, side: (0, j))] * outer,
            [jax.ShapeDtypeStruct(shape, FULL)] + [jax.ShapeDtypeStruct(shape, LOW)] * (outer - 1),
            "layers",
        )

    def planes(self):
        views, specs, counts = self.columns()
        rows = views[0].shape[0] * views[0].shape[-2]
        value = self.call(
            functools.partial(plane_kernel, self.steps, *counts),
            (2 * self.steps,),
            views,
            specs,
            pl.BlockSpec((rows, self.block), lambda j, side: (0, j)),
            jax.ShapeDtypeStruct((rows, 2 * self.cut), LOW),
            "planes",
        )
        return value

    def columns(self):
        views, specs = [], []
        steps = self.steps
        groups = (
            (self.base, lambda j: j),
            (self.extra[0], lambda j: jnp.minimum(j, steps - 1)),
            (self.extra[1], lambda j: jnp.maximum(j - steps, 0)),
        )
        for terms, column in groups:
            for term in terms:
                view, left = self.view(term)
                views.append(view)
                specs.append(self.spec(view, left, {bit: 0 for bit in left}, column))
        return views, specs, [len(terms) for terms, _ in groups]

    def turn_layers(self, layers, steps=None):
        grid = self.grid
        found = [
            grid.turn(layers[step], step * grid.inner) for step in steps or range(1, grid.outer)
        ]
        return found if steps else [layers[0]] + found

    def finish(self, got):
        return sum((value.astype(FULL) for value in got[1:]), got[0])


def norm_forward(rows, gain, bias):
    centre = jnp.mean(rows, axis=-1, keepdims=True)
    centred = rows - centre
    spread = jnp.mean(centred * centred, axis=-1, keepdims=True)
    scale = lax.rsqrt(spread + EPSILON)
    return (centred * scale * gain + bias).astype(LOW)


def norm_backward_kernel(count, rows_ref, gain_ref, base_ref, *rest):
    grad_refs, out_ref, rest = rest[:count], rest[count], rest[count + 1 :]
    sums_ref = rest[-1]
    rows = rows_ref[...].astype(FULL)
    centred = rows - jnp.mean(rows, axis=1, keepdims=True)
    spread = jnp.mean(centred * centred, axis=1, keepdims=True)
    scale = lax.rsqrt(spread + EPSILON)
    plain = centred * scale
    grad = grad_refs[0][...]
    for ref in grad_refs[1:]:
        grad = grad + ref[...]
    weighted = grad * gain_ref[...]
    mean_one = jnp.mean(weighted, axis=1, keepdims=True)
    mean_two = jnp.mean(weighted * plain, axis=1, keepdims=True)
    total = base_ref[...].astype(FULL) + scale * (weighted - mean_one - plain * mean_two)
    out_ref[...] = total
    if len(rest) > 1:
        rest[0][...] = total.astype(LOW)

    @pl.when(pl.program_id(0) == 0)
    def _():
        sums_ref[...] = jnp.zeros_like(sums_ref)

    sums_ref[0:1, :] += jnp.sum(grad * plain, axis=0, keepdims=True)
    sums_ref[1:2, :] += jnp.sum(grad, axis=0, keepdims=True)


def norm_backward(rows, gain, grads, base, rounded=True):
    seq, width = rows.shape
    block = pl.BlockSpec((min(TILE, seq), width), lambda step: (step, 0))
    more = [jax.ShapeDtypeStruct((seq, width), LOW)] if rounded else []
    out = pl.pallas_call(
        functools.partial(norm_backward_kernel, len(grads)),
        grid=(max(1, seq // TILE),),
        in_specs=[block, pl.BlockSpec((1, width), lambda step: (0, 0)), block]
        + [block] * len(grads),
        out_specs=[block] * (1 + len(more)) + [pl.BlockSpec((8, width), lambda step: (0, 0))],
        out_shape=[jax.ShapeDtypeStruct((seq, width), FULL)]
        + more
        + [jax.ShapeDtypeStruct((8, width), FULL)],
        compiler_params=PARAMS,
        cost_estimate=SHORT,
        name="norm_backward",
    )(rows, gain.reshape(1, width), base, *grads)
    return *out[:-1], out[-1][:2]


def adam_update(master, first, second, gradient, factor, rate, decay):
    gradient = gradient * factor
    first_new = BETA_ONE * first + (1.0 - BETA_ONE) * gradient
    second_new = BETA_TWO * second + (1.0 - BETA_TWO) * gradient * gradient
    first_fix = 1.0 - BETA_ONE**STEP
    second_fix = 1.0 - BETA_TWO**STEP
    update = first_new / first_fix / (jnp.sqrt(second_new / second_fix) + ADAM_EPSILON)
    master_new = master - rate * (update + decay * master)
    return (first_new, second_new, master_new, master_new.astype(LOW))


def adam_places(width, hidden):
    pairs = width // PAIR
    cut, half = pairs // 2, width // 2
    places = []
    for side in range(2):
        block = hidden // 8
        for piece, part in ((0, 0), (0, 1), (1, 0), (1, 1)):
            number = 4 * piece + 2 * part + side
            for kind in range(2):
                start = (2 * part + kind) * block
                places.append((1, 1 - kind, number * block, piece, start, side, block))
        for piece, first, count in ((3, 0, cut), (4, cut, pairs - cut)):
            for pair in range(count // 2):
                column = (first + side * (count // 2) + pair) * PAIR
                for kind in range(3):
                    places.append((0, kind, column, piece, (3 * pair + kind) * PAIR, side, PAIR))
        places.append((0, 3, side * half, 3, 3 * PAIR * cut // 2, side, half))
        places.append((0, 4, side * half, 2, half, side, half))
        for pair in range(pairs // 2):
            column = (side * (pairs // 2) + pair) * PAIR
            for kind in range(2):
                start = width + (2 * pair + kind) * PAIR
                places.append((0, 5 + kind, column, 2, start, side, PAIR))
        places.append((0, 7, side * half, 2, 0, side, half))
    return places


def adam_kernel(places, factor_ref, core_ref, *refs):
    grads, olds, news = refs[:10], refs[10:16], refs[16:]
    factor = factor_ref[0]
    core = core_ref[0]
    for into, matrix, column, piece, start, side, size in places:
        mine, other = (ref[:, start : start + size] for ref in grads[2 * piece : 2 * piece + 2])
        gradient = jnp.where(core == side, mine, other)
        old = [ref[matrix, :, column : column + size] for ref in olds[3 * into : 3 * into + 3]]
        new = adam_update(*old, gradient, factor, MATRIX_RATE, WEIGHT_DECAY)
        for ref, value in zip(news[4 * into : 4 * into + 4], new):
            ref[matrix, :, column : column + size] = value


def adam(factor, core, pieces, attn, mlp):
    width, hidden = attn[0].shape[2], mlp[0].shape[2]
    shapes = []
    for group in (attn, mlp):
        shape = group[0].shape
        shapes += [jax.ShapeDtypeStruct(shape, FULL)] * 3 + [jax.ShapeDtypeStruct(shape, LOW)]
    operands = [value for pair in pieces for value in pair] + list(attn) + list(mlp)
    def whole(value):
        return pl.BlockSpec(value.shape, lambda step: (0,) * len(value.shape))

    out = pl.pallas_call(
        functools.partial(adam_kernel, adam_places(width, hidden)),
        grid=(1,),
        in_specs=[SCALAR, SCALAR] + [whole(value) for value in operands],
        out_specs=[whole(value) for value in shapes],
        out_shape=shapes,
        compiler_params=LARGE,
        cost_estimate=SHORT,
        name="adam",
    )(factor.reshape(1), core, *operands)
    return out[:4], out[4:]


def tie(values):
    return lax.optimization_barrier(values)


def local(
    sizes,
    tokens,
    prompt,
    prompt_len,
    cotangent,
    attn_master,
    attn_first,
    attn_second,
    mlp_master,
    mlp_first,
    mlp_second,
    norm_master,
    norm_first,
    norm_second,
):
    grid = Grid(sizes)
    _, seq, width = tokens.shape
    own_rows = attn_master.shape[1]
    hidden = mlp_master.shape[2]
    norm_columns = jnp.pad(norm_master.T, ((0, 0), (0, PAIR - norm_master.shape[0])))
    shard, rest_shard = pack(attn_master, mlp_master, norm_columns)
    weights = lax.all_gather(shard, AXES, axis=0, tiled=True)
    rest_w = lax.all_gather(rest_shard, AXES, axis=0, tiled=True)
    grad_out = cotangent[0]
    up_at, quarter = 8 * width, hidden // 4
    gains = weights[:, up_at + 2 * quarter :].T[: norm_master.shape[0]].astype(FULL)
    out_w, cq_w, ckv_w, cout_w = (
        weights[:, low * width : high * width] for low, high in ((3, 4), (4, 5), (5, 7), (7, 8))
    )

    inputs = tokens[0].astype(FULL)
    normed_one = norm_forward(inputs, gains[0], gains[1])
    qkv = matmul(normed_one, weights, 0, 3 * width)
    mixed, levels = self_forward(qkv)
    after_self = inputs + dot_nn(mixed, out_w)
    normed_two = norm_forward(after_self, gains[2], gains[3])
    cross_q = dot_nn(normed_two, cq_w).astype(LOW)
    states = prompt[0]
    cross_kv = dot_nn(states, ckv_w).astype(LOW)
    crossed, cross_levels = cross_forward(prompt_len, cross_q, cross_kv)
    after_cross = after_self + dot_nn(crossed, cout_w)
    normed_three = norm_forward(after_cross, gains[4], gains[5])

    core = grid.core.astype(jnp.int32).reshape(1)
    half = width // 2
    pairs = width // PAIR
    def across(value):
        return lax.psum_scatter(value, "dp", scatter_dimension=0, tiled=True)

    *one_halves, active_one, back_one = mlp(
        core,
        normed_three,
        grad_out,
        weights,
        up_at,
        up_at + quarter,
        ((0, 0, 0, 0), (0, 1, 0, 0)),
    )
    normed_three, one_halves, rest_w = tie((normed_three, one_halves, rest_w))
    *halves, active_two, back_two = mlp(
        core,
        normed_three,
        grad_out,
        rest_w,
        0,
        3 * quarter,
        ((0, 0, 0, 1), (0, 1, 0, 1), (1, 0, 1, 0), (2, 0, 1, 1), (1, 1, 1, 0), (2, 1, 1, 1)),
        one_halves,
    )
    one_halves, two_halves = halves[:2], halves[2:]
    grads, one_halves, two_halves = tie(((back_one, back_two), one_halves, two_halves))

    one_got = grid.turn(one_halves[0], 1)
    grad_after_cross, branch, norm_three = norm_backward(after_cross, gains[4], grads, grad_out)
    cross_halves = product(core, crossed, branch, 2 * width, 0)
    grad_crossed = dot_nt(branch, cout_w).astype(LOW)
    grad_crossed, one_got, cross_halves = tie((grad_crossed, one_got, cross_halves))
    one_sum = Sum(grid, one_halves[1], one_got)
    last = one_sum.stages - 1
    sent = one_sum.send(0)
    grad_crossed, sent, two_halves = tie((grad_crossed, sent, two_halves))

    one_got, two_got = one_sum.swap(0, sent), grid.turn(two_halves[0], 1)
    grad_cq, grad_ckv = cross_backward(
        prompt_len, cross_q, cross_kv, crossed, grad_crossed, cross_levels
    )
    cross_halves = product(core, normed_two, grad_cq, 2 * width, half, cross_halves)
    cross_halves = product(core, states, grad_ckv, 2 * width, width, cross_halves)
    grad_cq, cross_halves, two_got = tie((grad_cq, cross_halves, two_got))

    grad_normed = matmul_turned(grad_cq, weights, 4 * width)
    grad_after_self, branch, norm_two = norm_backward(
        after_self, gains[2], [grad_normed], grad_after_cross
    )
    branch, one_got, cross_halves = tie((branch, one_got, cross_halves))
    one_sum.receive(0, one_got)
    branch = one_sum.between(branch)
    two_sum = Sum(grid, two_halves[1], two_got)
    sent, begun = one_sum.send(last), two_sum.send(0)
    branch, sent, begun = tie((branch, sent, begun))

    cross_got = grid.turn(cross_halves[0], 1)
    one_got, two_got = one_sum.swap(last, sent), two_sum.swap(0, begun)
    cut = pairs // 2
    part_width = 3 * PAIR * cut // 2
    front_width = half + part_width
    front_halves = product(core, mixed, branch, front_width, part_width)
    grad_mixed = dot_nt(branch, out_w).astype(LOW)
    grad_front = self_backward(qkv, mixed, grad_mixed, levels, 0, cut)
    front_halves = product(core, normed_one, grad_front, front_width, 0, front_halves)
    grad_mixed, grad_front, one_got, two_got, front_halves, cross_got = tie(
        (grad_mixed, grad_front, one_got, two_got, front_halves, cross_got)
    )
    one_sum.receive(last, one_got)
    two_sum.receive(0, two_got)
    grad_mixed = two_sum.between(grad_mixed)
    cross_sum = Sum(grid, cross_halves[1], cross_got)
    sent, begun, one_total = two_sum.send(last), cross_sum.send(0), one_sum.planes()
    grad_mixed, grad_front, sent, begun, one_total = tie(
        (grad_mixed, grad_front, sent, begun, one_total)
    )

    one_total = across(one_total)
    two_got, cross_got = two_sum.swap(last, sent), cross_sum.swap(0, begun)
    front_got = grid.turn(front_halves[0], 1)
    some = (pairs - cut) // 2
    split = 3 * PAIR * cut
    grad_normed = dot_nt(grad_front, weights[:, :split])
    grad_mixed, grad_normed = tie((grad_mixed, grad_normed))
    grad_back = self_backward(qkv, mixed, grad_mixed, levels, cut, some, pairs - cut)
    grad_mixed, grad_back, two_got, front_got = tie((grad_mixed, grad_back, two_got, front_got))
    two_sum.receive(last, two_got)
    two_total = two_sum.planes()
    grad_mixed, two_total = tie((grad_mixed, two_total))

    grad_back = self_backward(
        qkv, mixed, grad_mixed, levels, cut + some, pairs - cut - some, pairs - cut, some, grad_back
    )
    back_halves = product(core, normed_one, grad_back)
    grad_back, back_halves, cross_got, one_total, two_total = tie(
        (grad_back, back_halves, cross_got, one_total, two_total)
    )
    two_total = across(two_total)
    cross_sum.receive(0, cross_got)
    grad_back = cross_sum.between(grad_back)
    front_sum = Sum(grid, front_halves[1], front_got)
    sent, begun = cross_sum.send(last), front_sum.send(0)
    grad_back, sent, begun = tie((grad_back, sent, begun))

    cross_got, front_got = cross_sum.swap(last, sent), front_sum.swap(0, begun)
    back_got = grid.turn(back_halves[0], 1)
    grad_normed = grad_normed + dot_nt(grad_back, weights[:, split : 3 * width])
    token_grad, norm_one = norm_backward(
        tokens[0], gains[0], [grad_normed], grad_after_self, False
    )
    token_grad = token_grad[None]
    token_grad, cross_got, front_got, back_got, two_total = tie(
        (token_grad, cross_got, front_got, back_got, two_total)
    )
    cross_sum.receive(last, cross_got)
    front_sum.receive(0, front_got)
    token_grad = front_sum.between(token_grad)
    back_sum = Sum(grid, back_halves[1], back_got)
    sent, begun, cross_total = front_sum.send(last), back_sum.send(0), cross_sum.planes()
    grad_ckv, sent, begun, cross_total, active = tie(
        (grad_ckv, sent, begun, cross_total, (active_one, active_two))
    )

    cross_total = across(cross_total)
    front_got, back_got = front_sum.swap(last, sent), back_sum.swap(0, begun)
    prompt_grad = dot_nt(grad_ckv, ckv_w)[None]
    down_at = up_at + quarter
    output = after_cross + dot_nt(active[0], weights[:, down_at : down_at + quarter])
    output = output + dot_nt(active[1][:, :quarter], rest_w[:, 3 * quarter : 4 * quarter])
    prompt_grad, output, front_got, back_got = tie((prompt_grad, output, front_got, back_got))
    front_sum.receive(last, front_got)
    back_sum.receive(0, back_got)
    output = back_sum.between(output)
    layers, sent = front_sum.layers(), back_sum.send(last)
    output, active, layers, sent = tie((output, active, layers, sent))

    front_layers, got = front_sum.turn_layers(layers), back_sum.swap(last, sent)
    output = output + dot_nt(active[1][:, quarter:], rest_w[:, 4 * quarter :])
    output = output.astype(LOW)[None]
    output, got = tie((output, got))
    back_sum.receive(last, got)
    layers = back_sum.layers()
    one_total, two_total, layers = tie((one_total, two_total, layers))

    back_layers = back_sum.turn_layers(layers)
    totals = [total.astype(FULL) for total in (one_total, two_total, cross_total)]
    totals.append(front_sum.finish(front_layers))
    squares = sum(jnp.sum(total * total) for total in totals)
    squares, back_layers = tie((squares, back_layers))
    totals.append(back_sum.finish(back_layers))
    squares = squares + jnp.sum(totals[-1] * totals[-1])

    norm_stack = jnp.concatenate([norm_one, norm_two, norm_three])
    payload = jnp.concatenate([norm_stack, jnp.full((2, width), squares, FULL)])
    payload = grid.add_all(payload)
    norm_grads = payload[:-2]
    grad_norm = jnp.sqrt(payload[-1, 0] + jnp.sum(norm_grads * norm_grads))
    norm_grads = lax.dynamic_slice_in_dim(norm_grads, grid.me * own_rows, own_rows, 1)
    factor = CLIP_NORM / jnp.maximum(grad_norm, CLIP_NORM)
    attn_out, mlp_out = adam(
        factor,
        core,
        [grid.unpair(total) for total in totals],
        (attn_master, attn_first, attn_second),
        (mlp_master, mlp_first, mlp_second),
    )
    norm_out = adam_update(
        norm_master, norm_first, norm_second, norm_grads, factor, VECTOR_RATE, 0.0
    )
    return (output, token_grad, prompt_grad, grad_norm, *attn_out, *mlp_out, *norm_out)


def solution(mesh):
    outer, inner = mesh.shape["dp"], mesh.shape["fsdp"]
    fine = jax.sharding.Mesh(mesh.devices.reshape(outer, inner // 2, 2), AXES)
    items = P(AXES, None, None)
    weights = P(None, AXES, None)
    vectors = P(None, AXES)
    return jax.shard_map(
        functools.partial(local, (outer, inner // 2)),
        mesh=fine,
        in_specs=(items, items, P(AXES), items) + (weights,) * 6 + (vectors,) * 3,
        out_specs=(items,) * 3 + (P(),) + (weights,) * 8 + (vectors,) * 4,
        check_vma=False,
    )
```

```python
import functools

import jax
import jax.numpy as jnp
from jax import lax
from jax.experimental import pallas as pl
from jax.experimental.pallas import tpu as pltpu
from jax.sharding import PartitionSpec as P

HD = 64
PAIR = 2 * HD
STEP = 10
TILE = 256

EPSILON = 1e-05
CLIP_NORM = 1.0
BETA_ONE = 0.5
BETA_TWO = 0.5
MATRIX_RATE = 0.04
VECTOR_RATE = 0.3
WEIGHT_DECAY = 0.1
ADAM_EPSILON = 1e-08
SCORE_SCALE = 0.125
MASKED = -1000000000.0
AXES = ("dp", "chip", "core")
LOW = jnp.bfloat16
FULL = jnp.float32


def dot_nn(left, right):
    return lax.dot_general(left, right, (((1,), (0,)), ((), ())), preferred_element_type=FULL)


def dot_nt(left, right):
    return lax.dot_general(left, right, (((1,), (1,)), ((), ())), preferred_element_type=FULL)


def dot_tn(left, right):
    return lax.dot_general(left, right, (((0,), (0,)), ((), ())), preferred_element_type=FULL)


def lane_masks(rows):
    lane = lax.broadcasted_iota(jnp.int32, (rows, PAIR), 1)
    return (lane < HD, lane >= HD)


def forward_pair(queries, keys, values, causal, limit):
    seq = queries.shape[0]
    span = keys.shape[0]
    block = min(TILE, seq)
    masks = lane_masks(block)
    key_masks = lane_masks(span)
    counted = [jnp.where(mask, values, jnp.ones_like(values)) for mask in key_masks]

    def score(start):
        found = []
        for head in range(2):
            query = queries[start : start + block]
            query = jnp.where(masks[head], query, jnp.zeros_like(query)) * SCORE_SCALE
            if causal:
                row = lax.broadcasted_iota(jnp.int32, (block, block), 0)
                col = lax.broadcasted_iota(jnp.int32, (block, block), 1)
                parts = [(start, start + block, col <= row)]
                if start:
                    parts.append((0, start, None))
            else:
                col = lax.broadcasted_iota(jnp.int32, (block, span), 1)
                parts = [(0, span, col < limit)]
            scores = []
            for low, high, allowed in parts:
                value = dot_nt(query, keys[low:high])
                if allowed is not None:
                    value = jnp.where(allowed, value, MASKED)
                scores.append((low, high, value))
            found.append(scores)
        return found

    results = []
    ahead = score(0)
    for start in range(0, seq, block):
        found = ahead
        if start + block < seq:
            ahead = score(start + block)
        peaks, sums = [], []
        for head in range(2):
            peak = None
            for _, _, value in found[head]:
                most = jnp.max(value, axis=1, keepdims=True)
                peak = most if peak is None else jnp.maximum(peak, most)
            peaks.append(peak)
        for head in range(2):
            mixed = None
            for low, high, value in found[head]:
                weight = jnp.exp(value - peaks[head]).astype(LOW)
                part = dot_nn(weight, counted[head][low:high])
                mixed = part if mixed is None else mixed + part
            sums.append(mixed)
        mixed = jnp.where(masks[0], sums[0], sums[1])
        total = pltpu.roll(jnp.where(masks[0], sums[1], sums[0]), HD, 1)
        level = jnp.where(masks[0], peaks[0], peaks[1]) + jnp.log(total)
        results.append((start, start + block, (mixed / total).astype(LOW), level.T))
    return results


def backward_pair(queries, keys, values, mixed, upstream, levels, causal, limit):
    seq = queries.shape[0]
    span = keys.shape[0]
    block = min(TILE, span)
    masks = lane_masks(block)
    scaled = queries * SCORE_SCALE
    inner = (upstream.astype(FULL) * mixed.astype(FULL)).T
    products = [
        jnp.sum(inner[HD * head : HD * (head + 1)], axis=0, keepdims=True) for head in range(2)
    ]
    units = []
    for low in range(0, span, block):
        for head in range(2):
            if not causal:
                units.append((low, head, 0, seq, True))
                continue
            units.append((low, head, low, low + block, True))
            if low + block < seq:
                units.append((low, head, low + block, seq, False))

    def scores(unit):
        low, head, begin, end, checked = unit
        key, value = keys[low : low + block], values[low : low + block]
        key = jnp.where(masks[head], key, jnp.zeros_like(key))
        value = jnp.where(masks[head], value, jnp.zeros_like(value))
        return dot_nt(key, scaled[begin:end]), dot_nt(value, upstream[begin:end])

    def exponents(unit, score, grad_weight):
        low, head, begin, end, checked = unit
        if checked:
            row = lax.broadcasted_iota(jnp.int32, (block, end - begin), 0) + low
            if causal:
                col = lax.broadcasted_iota(jnp.int32, (block, end - begin), 1) + begin
                allowed = row <= col
            else:
                allowed = row < limit
            score = jnp.where(allowed, score, MASKED)
        weight = jnp.exp(score - levels[8 * head : 8 * head + 1, begin:end])
        grad_score = (weight * (grad_weight - products[head][:, begin:end])).astype(LOW)
        return weight.astype(LOW), grad_score

    grad_q = [[None] * (seq // block) for _ in range(2)]
    sums_k, sums_v = {}, {}

    def gather(unit, weight, grad_score):
        low, head, begin, end, _ = unit
        part_v = dot_nn(weight, upstream[begin:end])
        part_k = dot_nn(grad_score, scaled[begin:end])
        part_q = dot_tn(grad_score, keys[low : low + block])
        for sums, part in ((sums_k, part_k), (sums_v, part_v)):
            old = sums.get((low, head))
            sums[low, head] = part if old is None else old + part
        for at in range(begin, end, block):
            piece = part_q[at - begin : at - begin + block]
            old = grad_q[head][at // block]
            grad_q[head][at // block] = piece if old is None else old + piece

    ahead = scores(units[0])
    for number, unit in enumerate(units):
        found = ahead
        if number + 1 < len(units):
            ahead = scores(units[number + 1])
        gather(unit, *exponents(unit, *found))

    grad_k, grad_v, done_q = [], [], []
    for low in range(0, span, block):
        for sums, out in ((sums_k, grad_k), (sums_v, grad_v)):
            value = jnp.where(masks[0], sums[low, 0], sums[low, 1])
            out.append((low, low + block, value.astype(LOW)))
    for number, (one, two) in enumerate(zip(grad_q[0], grad_q[1])):
        value = (jnp.where(masks[0], one, two) * SCORE_SCALE).astype(LOW)
        done_q.append((number * block, (number + 1) * block, value))
    return done_q, grad_k, grad_v


def self_forward_kernel(qkv_ref, out_ref, level_ref):
    queries = qkv_ref[:, :PAIR]
    keys = qkv_ref[:, PAIR : 2 * PAIR]
    values = qkv_ref[:, 2 * PAIR :]
    for start, stop, out, level in forward_pair(queries, keys, values, True, None):
        out_ref[start:stop, :] = out
        level_ref[0, 0:8, start:stop] = level[0:8]
        level_ref[0, 8:16, start:stop] = level[HD : HD + 8]


def self_backward_kernel(qkv_ref, mixed_ref, upstream_ref, level_ref, *rest):
    grad_ref = rest[-1]
    queries = qkv_ref[:, :PAIR]
    keys = qkv_ref[:, PAIR : 2 * PAIR]
    values = qkv_ref[:, 2 * PAIR :]
    found = backward_pair(
        queries, keys, values, mixed_ref[...], upstream_ref[...], level_ref[0], True, None
    )
    for place, rows in enumerate(found):
        for start, stop, value in rows:
            grad_ref[start:stop, place * PAIR : (place + 1) * PAIR] = value


def cross_forward_kernel(limit_ref, query_ref, kv_ref, out_ref, level_ref):
    found = forward_pair(query_ref[...], kv_ref[:, :PAIR], kv_ref[:, PAIR:], False, limit_ref[0])
    for start, stop, out, level in found:
        out_ref[start:stop, :] = out
        level_ref[0, 0:8, start:stop] = level[0:8]
        level_ref[0, 8:16, start:stop] = level[HD : HD + 8]


def cross_backward_kernel(
    limit_ref, query_ref, kv_ref, mixed_ref, upstream_ref, level_ref, grad_q_ref, grad_kv_ref
):
    found = backward_pair(
        query_ref[...],
        kv_ref[:, :PAIR],
        kv_ref[:, PAIR:],
        mixed_ref[...],
        upstream_ref[...],
        level_ref[0],
        False,
        limit_ref[0],
    )
    for start, stop, value in found[0]:
        grad_q_ref[start:stop, :] = value
    for place, rows in enumerate(found[1:]):
        for start, stop, value in rows:
            grad_kv_ref[start:stop, place * PAIR : (place + 1) * PAIR] = value


LARGE = pltpu.CompilerParams(vmem_limit_bytes=56 * 1024 * 1024)
MIDDLE = pltpu.CompilerParams(vmem_limit_bytes=42 * 1024 * 1024)
PARAMS = pltpu.CompilerParams(vmem_limit_bytes=28 * 1024 * 1024)
SCALAR = pl.BlockSpec(memory_space=pltpu.SMEM)


def streamed(value):
    return pltpu.with_memory_space_constraint(value, pltpu.HBM)


def columns(rows, width, offset=0):
    return pl.BlockSpec((rows, width), lambda pair: (0, pair + offset))


def planes(seq):
    return pl.BlockSpec((1, 16, seq), lambda pair: (pair, 0, 0))


SHORT = pl.CostEstimate(flops=1, bytes_accessed=1, transcendentals=0)


def self_forward(qkv):
    seq, width = qkv.shape[0], qkv.shape[1] // 3
    pairs = width // PAIR
    return pl.pallas_call(
        self_forward_kernel,
        grid=(pairs,),
        in_specs=[columns(seq, 3 * PAIR)],
        out_specs=[columns(seq, PAIR), planes(seq)],
        out_shape=[
            jax.ShapeDtypeStruct((seq, width), LOW),
            jax.ShapeDtypeStruct((pairs, 16, seq), FULL),
        ],
        compiler_params=LARGE,
        cost_estimate=SHORT,
        name="self_forward",
    )(streamed(qkv))


def self_backward(qkv, mixed, upstream, levels, start, count, total=None, at=0, old=None):
    seq = qkv.shape[0]
    total = count if total is None else total
    old = [] if old is None else [old]
    return pl.pallas_call(
        self_backward_kernel,
        grid=(count,),
        in_specs=[
            columns(seq, 3 * PAIR, start),
            columns(seq, PAIR, start),
            columns(seq, PAIR, start),
            pl.BlockSpec((1, 16, seq), lambda pair: (pair + start, 0, 0)),
        ]
        + [pl.BlockSpec(memory_space=pl.ANY)] * len(old),
        out_specs=columns(seq, 3 * PAIR, at),
        out_shape=jax.ShapeDtypeStruct((seq, 3 * PAIR * total), LOW),
        input_output_aliases={4: 0} if old else {},
        compiler_params=PARAMS,
        cost_estimate=SHORT,
        name="self_backward",
    )(streamed(qkv), streamed(mixed), upstream, levels, *old)


def cross_forward(limit, queries, pair_states):
    seq, width = queries.shape
    span = pair_states.shape[0]
    pairs = width // PAIR
    return pl.pallas_call(
        cross_forward_kernel,
        grid=(pairs,),
        in_specs=[SCALAR, columns(seq, PAIR), columns(span, 2 * PAIR)],
        out_specs=[columns(seq, PAIR), planes(seq)],
        out_shape=[
            jax.ShapeDtypeStruct((seq, width), LOW),
            jax.ShapeDtypeStruct((pairs, 16, seq), FULL),
        ],
        compiler_params=PARAMS,
        cost_estimate=SHORT,
        name="cross_forward",
    )(limit, queries, pair_states)


def cross_backward(limit, queries, pair_states, mixed, upstream, levels):
    seq, width = queries.shape
    span = pair_states.shape[0]
    pairs = width // PAIR
    return pl.pallas_call(
        cross_backward_kernel,
        grid=(pairs,),
        in_specs=[
            SCALAR,
            columns(seq, PAIR),
            columns(span, 2 * PAIR),
            columns(seq, PAIR),
            columns(seq, PAIR),
            planes(seq),
        ],
        out_specs=[columns(seq, PAIR), columns(span, 2 * PAIR)],
        out_shape=[
            jax.ShapeDtypeStruct((seq, width), LOW),
            jax.ShapeDtypeStruct((span, 2 * width), LOW),
        ],
        compiler_params=PARAMS,
        cost_estimate=SHORT,
        name="cross_backward",
    )(limit, queries, pair_states, mixed, upstream, levels)


def mlp_kernel(order, core_ref, rows_ref, grad_ref, up_ref, down_ref, *rest):
    del core_ref
    count = 2 + max(piece for _, _, piece, _ in order) * 2
    halves_refs, rest = rest[-4 - count : -4], rest[-4:]
    out_ref, back_ref, rows_turned_ref, grad_turned_ref = rest
    step = pl.program_id(0)

    @pl.when(step == 0)
    def _():
        rows_turned_ref[...] = rows_ref[...].T
        grad_turned_ref[...] = grad_ref[...].T
        back_ref[...] = jnp.zeros_like(back_ref)

    seq = rows_ref.shape[0]
    size = min(512, seq)
    width = up_ref.shape[1]

    def ahead(start):
        rows = slice(start, start + size)
        return dot_nn(rows_ref[rows, :], up_ref[...]), dot_nn(grad_ref[rows, :], down_ref[...])

    down_grad, up_grad = None, None
    found = ahead(0)
    for start in range(0, seq, size):
        hidden, grad = found
        if start + size < seq:
            found = ahead(start + size)
        rows = slice(start, start + size)
        share = 0.5 + 0.5 * lax.erf(hidden * 0.7071067811865476)
        bell = jnp.exp(hidden * hidden * -0.5)
        active = (hidden * share).astype(LOW)
        grad_hidden = (grad * (share + hidden * (bell * 0.3989422804014327))).astype(LOW)
        out_ref[rows, :] = active
        down_part = dot_nn(grad_turned_ref[:, rows], active)
        up_part = dot_nn(rows_turned_ref[:, rows], grad_hidden)
        back_ref[rows, :] += dot_nt(grad_hidden, up_ref[...])
        down_grad = down_part if start == 0 else down_grad + down_part
        up_grad = up_part if start == 0 else up_grad + up_part

    for number, half_ref in enumerate(halves_refs):
        steps = [
            at for at, (_, side, piece, _) in enumerate(order) if 2 * piece + 1 - side == number
        ]

        @pl.when((step >= steps[0]) & (step <= steps[-1]))
        def _(half_ref=half_ref):
            half_ref[:, :width] = down_grad.astype(LOW)
            half_ref[:, width:] = up_grad.astype(LOW)


def mlp(core, rows, grad, weights, up_at, down_at, order, old=None):
    seq, width = rows.shape
    block = width // 2
    pieces = 1 + max(piece for _, _, piece, _ in order)

    def chosen(j, values):
        found = values[0]
        for number, value in enumerate(values[1:], 1):
            found = jnp.where(j == number, value, found)
        return found

    def place(j, core):
        quarter = chosen(j, [quarter for quarter, _, _, _ in order])
        return 2 * quarter + (core[0] ^ chosen(j, [side for _, side, _, _ in order]))

    def strip(start):
        return pl.BlockSpec((width, block), lambda j, core: (0, start // block + place(j, core)))

    once = pl.Buffered(1)

    def strips(number):
        mine = [at for at, (_, side, piece, _) in enumerate(order) if 2 * piece + 1 - side == number]
        places = [order[min(max(at, mine[0]), mine[-1])][3] for at in range(len(order))]
        return pl.BlockSpec(
            (width, width), lambda j, core: (0, chosen(j, places)), pipeline_mode=once
        )

    old = [] if old is None else list(old)
    whole = pl.BlockSpec((seq, width), lambda j, core: (0, 0), pipeline_mode=once)
    return pl.pallas_call(
        functools.partial(mlp_kernel, order),
        grid_spec=pltpu.PrefetchScalarGridSpec(
            num_scalar_prefetch=1,
            grid=(len(order),),
            in_specs=[whole, whole, strip(up_at), strip(down_at)]
            + [pl.BlockSpec(memory_space=pl.ANY)] * len(old),
            out_specs=[strips(number) for number in range(2 * pieces)]
            + [pl.BlockSpec((seq, block), lambda j, core: (0, place(j, core))), whole],
            scratch_shapes=[pltpu.VMEM((width, seq), LOW)] * 2,
        ),
        out_shape=[jax.ShapeDtypeStruct((width, 2 * width), LOW)] * (2 * pieces)
        + [
            jax.ShapeDtypeStruct((seq, len(order) * block), LOW),
            jax.ShapeDtypeStruct((seq, width), FULL),
        ],
        input_output_aliases={5: 0, 6: 1} if old else {},
        compiler_params=MIDDLE,
        cost_estimate=SHORT,
        name="mlp",
    )(core, rows, grad, weights, weights, *old)


def matmul_kernel(left_ref, right_ref, out_ref):
    out_ref[...] = dot_nn(left_ref[...], right_ref[...]).astype(LOW)


def matmul(left, right, at, count):
    seq, depth = left.shape
    block = min(512, count)
    return pl.pallas_call(
        matmul_kernel,
        grid=(count // block,),
        in_specs=[
            pl.BlockSpec((seq, depth), lambda step: (0, 0)),
            pl.BlockSpec((depth, block), lambda step: (0, at // block + step)),
        ],
        out_specs=pl.BlockSpec((seq, block), lambda step: (0, step)),
        out_shape=jax.ShapeDtypeStruct((seq, count), LOW),
        compiler_params=PARAMS,
        cost_estimate=SHORT,
        name="matmul",
    )(left, right)


def turned_kernel(left_ref, right_ref, out_ref):
    out_ref[...] = dot_nt(left_ref[...], right_ref[...])


def matmul_turned(left, right, at):
    seq, depth = left.shape
    width = right.shape[0]
    block = min(512, width)
    return pl.pallas_call(
        turned_kernel,
        grid=(width // block,),
        in_specs=[
            pl.BlockSpec((seq, depth), lambda step: (0, 0)),
            pl.BlockSpec((block, depth), lambda step: (step, at // depth)),
        ],
        out_specs=pl.BlockSpec((seq, block), lambda step: (0, step)),
        out_shape=jax.ShapeDtypeStruct((seq, width), FULL),
        compiler_params=PARAMS,
        cost_estimate=SHORT,
        name="matmul_turned",
    )(left, right)


def product_kernel(core_ref, left_ref, sent_ref, kept_ref, *rest):
    del core_ref
    send_ref, keep_ref, turned_ref = rest[-3:]

    @pl.when(pl.program_id(0) == 0)
    def _():
        turned_ref[...] = left_ref[...].T

    send_ref[...] = dot_nn(turned_ref[...], sent_ref[...]).astype(LOW)
    keep_ref[...] = dot_nn(turned_ref[...], kept_ref[...]).astype(LOW)


def product(core, left, right, total=None, at=0, old=None):
    rows, width = left.shape
    half = right.shape[1] // 2
    block = max(b for b in (128, 256, 384, 512) if half % b == 0 and at % b == 0)
    steps, offset = half // block, at // block
    total = half if total is None else total
    old = [] if old is None else list(old)
    return pl.pallas_call(
        product_kernel,
        grid_spec=pltpu.PrefetchScalarGridSpec(
            num_scalar_prefetch=1,
            grid=(steps,),
            in_specs=[
                pl.BlockSpec((rows, width), lambda j, core: (0, 0)),
                pl.BlockSpec((rows, block), lambda j, core: (0, (1 - core[0]) * steps + j)),
                pl.BlockSpec((rows, block), lambda j, core: (0, core[0] * steps + j)),
            ]
            + [pl.BlockSpec(memory_space=pl.ANY)] * len(old),
            out_specs=[pl.BlockSpec((width, block), lambda j, core: (0, offset + j))] * 2,
            scratch_shapes=[pltpu.VMEM((width, rows), LOW)],
        ),
        out_shape=[jax.ShapeDtypeStruct((width, total), LOW)] * 2,
        input_output_aliases={4: 0, 5: 1} if old else {},
        compiler_params=PARAMS,
        cost_estimate=SHORT,
        name="product",
    )(core, streamed(left), right, right, *old)


def pack_kernel(attn_ref, mlp_ref, norm_ref, out_ref, rest_ref):
    width = attn_ref.shape[2]
    hidden = mlp_ref.shape[2]
    quarter = hidden // 4
    for pair in range(width // PAIR):
        source = slice(pair * PAIR, (pair + 1) * PAIR)
        for kind in range(3):
            place = (3 * pair + kind) * PAIR
            out_ref[:, place : place + PAIR] = attn_ref[kind, :, source].astype(LOW)
        for kind in range(2):
            place = 5 * width + (2 * pair + kind) * PAIR
            out_ref[:, place : place + PAIR] = attn_ref[5 + kind, :, source].astype(LOW)
    out_ref[:, 3 * width : 4 * width] = attn_ref[3].astype(LOW)
    out_ref[:, 4 * width : 5 * width] = attn_ref[4].astype(LOW)
    out_ref[:, 7 * width : 8 * width] = attn_ref[7].astype(LOW)
    for kind in range(2):
        place = 8 * width + kind * quarter
        out_ref[:, place : place + quarter] = mlp_ref[kind, :, :quarter].astype(LOW)
        place = kind * 3 * quarter
        rest_ref[:, place : place + 3 * quarter] = mlp_ref[kind, :, quarter:].astype(LOW)
    out_ref[:, 8 * width + 2 * quarter :] = norm_ref[...].astype(LOW)


def pack(attn_master, mlp_master, norm_columns):
    _, rows, width = attn_master.shape
    hidden = mlp_master.shape[2]
    return pl.pallas_call(
        pack_kernel,
        out_shape=[
            jax.ShapeDtypeStruct((rows, 8 * width + hidden // 2 + norm_columns.shape[1]), LOW),
            jax.ShapeDtypeStruct((rows, 3 * hidden // 2), LOW),
        ],
        compiler_params=PARAMS,
        cost_estimate=SHORT,
        name="pack",
    )(attn_master, mlp_master, norm_columns)


class Grid:
    def __init__(self, sizes):
        self.outer, self.chips = sizes
        self.inner = 2 * self.chips
        self.count = self.outer * self.inner
        self.bits = (self.count - 1).bit_length()
        self.core = lax.axis_index("core")
        self.me = lax.axis_index(AXES)
        self.plane = lax.axis_index("dp")
        near = ((self.chips - 1).bit_length() + 1) // 2
        self.x = list(range(near, 0, -1))
        self.y = list(range((self.chips - 1).bit_length(), near, -1))

    def own(self, bit):
        return lax.shift_right_logical(self.me, jnp.int32(bit)) & 1

    def turn(self, value, mask):
        return lax.ppermute(value, AXES, [(i, i ^ mask) for i in range(self.count)])

    def add_all(self, value):
        for bit in range(self.bits):
            value = value + self.turn(value, 1 << bit)
        return value

    def unpair(self, total):
        total = total.reshape(2, total.shape[0] // 2, total.shape[1])
        mine = lax.dynamic_index_in_dim(total, self.core, 0, keepdims=False)
        other = lax.dynamic_index_in_dim(total, 1 - self.core, 0, keepdims=False)
        return mine, self.turn(other, 1)


def add_kernel(counts, side_ref, *refs):
    del side_ref
    outs = refs[sum(counts) :]
    at = 0
    for count, out_ref in zip(counts, outs):
        total = refs[at][...].reshape(out_ref.shape).astype(FULL)
        for ref in refs[at + 1 : at + count]:
            total = total + ref[...].reshape(out_ref.shape).astype(FULL)
        out_ref[...] = total.astype(LOW)
        at += count


def layer_kernel(outer, steps, first, one, two, side_ref, *refs):
    ins, outs = refs[: first + one + two], refs[first + one + two :]

    def fill(parts):
        for step in range(outer):
            plane = side_ref[0] ^ step
            out_ref = outs[step]
            total = parts[0][plane].reshape(out_ref.shape).astype(FULL)
            for part in parts[1:]:
                total = total + part[plane].reshape(out_ref.shape).astype(FULL)
            out_ref[...] = total.astype(out_ref.dtype)

    @pl.when(pl.program_id(0) < steps)
    def _():
        fill(ins[:first] + ins[first : first + one])

    @pl.when(pl.program_id(0) >= steps)
    def _():
        fill(ins[:first] + ins[first + one :])


def plane_kernel(steps, first, one, two, side_ref, *refs):
    del side_ref
    ins, out_ref = refs[:-1], refs[-1]

    def fill(parts):
        total = parts[0][...].reshape(out_ref.shape).astype(FULL)
        for part in parts[1:]:
            total = total + part[...].reshape(out_ref.shape).astype(FULL)
        out_ref[...] = total.astype(LOW)

    @pl.when(pl.program_id(0) < steps)
    def _():
        fill(ins[:first] + ins[first : first + one])

    @pl.when(pl.program_id(0) >= steps)
    def _():
        fill(ins[:first] + ins[first + one :])


class Sum:
    def __init__(self, grid, keep, got):
        self.grid = grid
        self.bits = sorted(grid.x + grid.y, reverse=True)
        self.cut = keep.shape[1] // 2
        self.block = max(b for b in (128, 256, 384, 512, 640) if self.cut % b == 0)
        self.steps = self.cut // self.block
        self.base = [(keep, []), (got, [])]
        self.orders = [grid.x + grid.y, grid.y + grid.x]
        self.extra = [[], []]
        self.stages = len(self.bits)
        sides = [grid.plane] + [grid.own(bit) for bit in self.bits]
        self.sides = jnp.stack(sides).astype(jnp.int32)

    def view(self, term):
        value, done = term
        left = [bit for bit in self.bits if bit not in done]
        outer = self.grid.outer
        share = value.shape[0] // (outer << len(left))
        return value.reshape([outer] + [2] * len(left) + [share, value.shape[1]]), left

    def spec(self, view, left, flips, column):
        places = {bit: 1 + self.bits.index(bit) for bit in flips}

        def index(j, side):
            picks = [
                (side[places[bit]] ^ flips[bit]) if bit in flips else 0 for bit in left
            ]
            return (0, *picks, 0, column(j))

        shape = [view.shape[0]] + [1 if bit in flips else 2 for bit in left]
        return pl.BlockSpec((*shape, view.shape[-2], self.block), index)

    def call(self, kernel, grid, views, specs, out_specs, out_shape, name):
        return pl.pallas_call(
            kernel,
            grid_spec=pltpu.PrefetchScalarGridSpec(
                num_scalar_prefetch=1, grid=grid, in_specs=specs, out_specs=out_specs
            ),
            out_shape=out_shape,
            compiler_params=PARAMS,
            cost_estimate=SHORT,
            name=name,
        )(self.sides, *(streamed(view) for view in views))

    def send(self, stage):
        views, specs, counts = [], [], []
        for half, order in enumerate(self.orders):
            flips = {bit: 0 for bit in order[:stage]}
            flips[order[stage]] = 1
            terms = self.base + self.extra[half]
            counts.append(len(terms))
            for number, term in enumerate(terms):
                view, left = self.view(term)
                shift = half * self.steps if number < len(self.base) else 0
                views.append(view)
                picked = {bit: flip for bit, flip in flips.items() if bit in left}
                specs.append(self.spec(view, left, picked, lambda j, shift=shift: shift + j))
        rows = self.base[0][0].shape[0] >> (stage + 1)
        return self.call(
            functools.partial(add_kernel, counts),
            (self.steps,),
            views,
            specs,
            [pl.BlockSpec((rows, self.block), lambda j, side: (0, j))] * 2,
            [jax.ShapeDtypeStruct((rows, self.cut), LOW)] * 2,
            "add",
        )

    def swap(self, stage, out):
        return [self.grid.turn(v, 1 << order[stage]) for order, v in zip(self.orders, out)]

    def receive(self, stage, got):
        for half, value in enumerate(got):
            self.extra[half].append((value, self.orders[half][: stage + 1]))

    def between(self, main):
        for stage in range(1, self.stages - 1):
            main, sent = tie((main, self.send(stage)))
            main, got = tie((main, self.swap(stage, sent)))
            self.receive(stage, got)
        return main

    def layers(self):
        views, specs, counts = self.columns()
        outer = self.grid.outer
        share = views[0].shape[-2]
        shape = (share, 2 * self.cut)
        return self.call(
            functools.partial(layer_kernel, outer, self.steps, *counts),
            (2 * self.steps,),
            views,
            specs,
            [pl.BlockSpec((share, self.block), lambda j, side: (0, j))] * outer,
            [jax.ShapeDtypeStruct(shape, FULL)] + [jax.ShapeDtypeStruct(shape, LOW)] * (outer - 1),
            "layers",
        )

    def planes(self):
        views, specs, counts = self.columns()
        rows = views[0].shape[0] * views[0].shape[-2]
        value = self.call(
            functools.partial(plane_kernel, self.steps, *counts),
            (2 * self.steps,),
            views,
            specs,
            pl.BlockSpec((rows, self.block), lambda j, side: (0, j)),
            jax.ShapeDtypeStruct((rows, 2 * self.cut), LOW),
            "planes",
        )
        return value

    def columns(self):
        views, specs = [], []
        steps = self.steps
        groups = (
            (self.base, lambda j: j),
            (self.extra[0], lambda j: jnp.minimum(j, steps - 1)),
            (self.extra[1], lambda j: jnp.maximum(j - steps, 0)),
        )
        for terms, column in groups:
            for term in terms:
                view, left = self.view(term)
                views.append(view)
                specs.append(self.spec(view, left, {bit: 0 for bit in left}, column))
        return views, specs, [len(terms) for terms, _ in groups]

    def turn_layers(self, layers, steps=None):
        grid = self.grid
        found = [
            grid.turn(layers[step], step * grid.inner) for step in steps or range(1, grid.outer)
        ]
        return found if steps else [layers[0]] + found

    def finish(self, got):
        return sum((value.astype(FULL) for value in got[1:]), got[0])


def norm_forward(rows, gain, bias):
    centre = jnp.mean(rows, axis=-1, keepdims=True)
    centred = rows - centre
    spread = jnp.mean(centred * centred, axis=-1, keepdims=True)
    scale = lax.rsqrt(spread + EPSILON)
    return (centred * scale * gain + bias).astype(LOW)


def norm_backward_kernel(count, rows_ref, gain_ref, base_ref, *rest):
    grad_refs, out_ref, rest = rest[:count], rest[count], rest[count + 1 :]
    sums_ref = rest[-1]
    rows = rows_ref[...].astype(FULL)
    centred = rows - jnp.mean(rows, axis=1, keepdims=True)
    spread = jnp.mean(centred * centred, axis=1, keepdims=True)
    scale = lax.rsqrt(spread + EPSILON)
    plain = centred * scale
    grad = grad_refs[0][...]
    for ref in grad_refs[1:]:
        grad = grad + ref[...]
    weighted = grad * gain_ref[...]
    mean_one = jnp.mean(weighted, axis=1, keepdims=True)
    mean_two = jnp.mean(weighted * plain, axis=1, keepdims=True)
    total = base_ref[...].astype(FULL) + scale * (weighted - mean_one - plain * mean_two)
    out_ref[...] = total
    if len(rest) > 1:
        rest[0][...] = total.astype(LOW)

    @pl.when(pl.program_id(0) == 0)
    def _():
        sums_ref[...] = jnp.zeros_like(sums_ref)

    sums_ref[0:1, :] += jnp.sum(grad * plain, axis=0, keepdims=True)
    sums_ref[1:2, :] += jnp.sum(grad, axis=0, keepdims=True)


def norm_backward(rows, gain, grads, base, rounded=True):
    seq, width = rows.shape
    block = pl.BlockSpec((min(TILE, seq), width), lambda step: (step, 0))
    more = [jax.ShapeDtypeStruct((seq, width), LOW)] if rounded else []
    out = pl.pallas_call(
        functools.partial(norm_backward_kernel, len(grads)),
        grid=(max(1, seq // TILE),),
        in_specs=[block, pl.BlockSpec((1, width), lambda step: (0, 0)), block]
        + [block] * len(grads),
        out_specs=[block] * (1 + len(more)) + [pl.BlockSpec((8, width), lambda step: (0, 0))],
        out_shape=[jax.ShapeDtypeStruct((seq, width), FULL)]
        + more
        + [jax.ShapeDtypeStruct((8, width), FULL)],
        compiler_params=PARAMS,
        cost_estimate=SHORT,
        name="norm_backward",
    )(streamed(rows), gain.reshape(1, width), streamed(base), *grads)
    return *out[:-1], out[-1][:2]


def adam_update(master, first, second, gradient, factor, rate, decay):
    gradient = gradient * factor
    first_new = BETA_ONE * first + (1.0 - BETA_ONE) * gradient
    second_new = BETA_TWO * second + (1.0 - BETA_TWO) * gradient * gradient
    first_fix = 1.0 - BETA_ONE**STEP
    second_fix = 1.0 - BETA_TWO**STEP
    update = first_new / first_fix / (jnp.sqrt(second_new / second_fix) + ADAM_EPSILON)
    master_new = master - rate * (update + decay * master)
    return (first_new, second_new, master_new, master_new.astype(LOW))


def adam_places(width, hidden):
    pairs = width // PAIR
    cut, half = pairs // 2, width // 2
    places = []
    for side in range(2):
        block = hidden // 8
        for piece, part in ((0, 0), (0, 1), (1, 0), (1, 1)):
            number = 4 * piece + 2 * part + side
            for kind in range(2):
                start = (2 * part + kind) * block
                places.append((1, 1 - kind, number * block, piece, start, side, block))
        for piece, first, count in ((3, 0, cut), (4, cut, pairs - cut)):
            for pair in range(count // 2):
                column = (first + side * (count // 2) + pair) * PAIR
                for kind in range(3):
                    places.append((0, kind, column, piece, (3 * pair + kind) * PAIR, side, PAIR))
        places.append((0, 3, side * half, 3, 3 * PAIR * cut // 2, side, half))
        places.append((0, 4, side * half, 2, half, side, half))
        for pair in range(pairs // 2):
            column = (side * (pairs // 2) + pair) * PAIR
            for kind in range(2):
                start = width + (2 * pair + kind) * PAIR
                places.append((0, 5 + kind, column, 2, start, side, PAIR))
        places.append((0, 7, side * half, 2, 0, side, half))
    return places


def adam_kernel(places, factor_ref, core_ref, *refs):
    grads, olds, news = refs[:10], refs[10:16], refs[16:]
    factor = factor_ref[0]
    core = core_ref[0]
    for into, matrix, column, piece, start, side, size in places:
        mine, other = (ref[:, start : start + size] for ref in grads[2 * piece : 2 * piece + 2])
        gradient = jnp.where(core == side, mine, other)
        old = [ref[matrix, :, column : column + size] for ref in olds[3 * into : 3 * into + 3]]
        new = adam_update(*old, gradient, factor, MATRIX_RATE, WEIGHT_DECAY)
        for ref, value in zip(news[4 * into : 4 * into + 4], new):
            ref[matrix, :, column : column + size] = value


def adam(factor, core, pieces, attn, mlp):
    width, hidden = attn[0].shape[2], mlp[0].shape[2]
    shapes = []
    for group in (attn, mlp):
        shape = group[0].shape
        shapes += [jax.ShapeDtypeStruct(shape, FULL)] * 3 + [jax.ShapeDtypeStruct(shape, LOW)]
    operands = [value for pair in pieces for value in pair] + list(attn) + list(mlp)
    def whole(value):
        return pl.BlockSpec(value.shape, lambda step: (0,) * len(value.shape))

    out = pl.pallas_call(
        functools.partial(adam_kernel, adam_places(width, hidden)),
        grid=(1,),
        in_specs=[SCALAR, SCALAR] + [whole(value) for value in operands],
        out_specs=[whole(value) for value in shapes],
        out_shape=shapes,
        compiler_params=LARGE,
        cost_estimate=SHORT,
        name="adam",
    )(factor.reshape(1), core, *operands)
    return out[:4], out[4:]


def tie(values):
    return lax.optimization_barrier(values)


def local(
    sizes,
    tokens,
    prompt,
    prompt_len,
    cotangent,
    attn_master,
    attn_first,
    attn_second,
    mlp_master,
    mlp_first,
    mlp_second,
    norm_master,
    norm_first,
    norm_second,
):
    grid = Grid(sizes)
    _, seq, width = tokens.shape
    own_rows = attn_master.shape[1]
    hidden = mlp_master.shape[2]
    norm_columns = jnp.pad(norm_master.T, ((0, 0), (0, PAIR - norm_master.shape[0])))
    shard, rest_shard = pack(attn_master, mlp_master, norm_columns)
    weights = lax.all_gather(shard, AXES, axis=0, tiled=True)
    rest_w = lax.all_gather(rest_shard, AXES, axis=0, tiled=True)
    grad_out = cotangent[0]
    up_at, quarter = 8 * width, hidden // 4
    gains = weights[:, up_at + 2 * quarter :].T[: norm_master.shape[0]].astype(FULL)
    out_w, cq_w, ckv_w, cout_w = (
        weights[:, low * width : high * width] for low, high in ((3, 4), (4, 5), (5, 7), (7, 8))
    )

    inputs = tokens[0].astype(FULL)
    normed_one = norm_forward(inputs, gains[0], gains[1])
    qkv = matmul(normed_one, weights, 0, 3 * width)
    mixed, levels = self_forward(qkv)
    after_self = inputs + dot_nn(mixed, out_w)
    normed_two = norm_forward(after_self, gains[2], gains[3])
    cross_q = dot_nn(normed_two, cq_w).astype(LOW)
    states = prompt[0]
    cross_kv = dot_nn(states, ckv_w).astype(LOW)
    crossed, cross_levels = cross_forward(prompt_len, cross_q, cross_kv)
    after_cross = after_self + dot_nn(crossed, cout_w)
    normed_three = norm_forward(after_cross, gains[4], gains[5])

    core = grid.core.astype(jnp.int32).reshape(1)
    half = width // 2
    pairs = width // PAIR
    def across(value):
        return lax.psum_scatter(value, "dp", scatter_dimension=0, tiled=True)

    *one_halves, active_one, back_one = mlp(
        core,
        normed_three,
        grad_out,
        weights,
        up_at,
        up_at + quarter,
        ((0, 0, 0, 0), (0, 1, 0, 0)),
    )
    normed_three, one_halves, rest_w = tie((normed_three, one_halves, rest_w))
    *halves, active_two, back_two = mlp(
        core,
        normed_three,
        grad_out,
        rest_w,
        0,
        3 * quarter,
        ((0, 0, 0, 1), (0, 1, 0, 1), (1, 0, 1, 0), (2, 0, 1, 1), (1, 1, 1, 0), (2, 1, 1, 1)),
        one_halves,
    )
    one_halves, two_halves = halves[:2], halves[2:]
    grads, one_halves, two_halves = tie(((back_one, back_two), one_halves, two_halves))

    one_got = grid.turn(one_halves[0], 1)
    grad_after_cross, branch, norm_three = norm_backward(after_cross, gains[4], grads, grad_out)
    cross_halves = product(core, crossed, branch, 2 * width, 0)
    grad_crossed = dot_nt(branch, cout_w).astype(LOW)
    grad_crossed, one_got, cross_halves = tie((grad_crossed, one_got, cross_halves))
    one_sum = Sum(grid, one_halves[1], one_got)
    last = one_sum.stages - 1
    sent = one_sum.send(0)
    grad_crossed, sent, two_halves = tie((grad_crossed, sent, two_halves))

    one_got, two_got = one_sum.swap(0, sent), grid.turn(two_halves[0], 1)
    grad_cq, grad_ckv = cross_backward(
        prompt_len, cross_q, cross_kv, crossed, grad_crossed, cross_levels
    )
    cross_halves = product(core, normed_two, grad_cq, 2 * width, half, cross_halves)
    cross_halves = product(core, states, grad_ckv, 2 * width, width, cross_halves)
    grad_cq, cross_halves, two_got = tie((grad_cq, cross_halves, two_got))

    grad_normed = matmul_turned(grad_cq, weights, 4 * width)
    grad_after_self, branch, norm_two = norm_backward(
        after_self, gains[2], [grad_normed], grad_after_cross
    )
    branch, one_got, cross_halves = tie((branch, one_got, cross_halves))
    one_sum.receive(0, one_got)
    branch = one_sum.between(branch)
    two_sum = Sum(grid, two_halves[1], two_got)
    sent, begun = one_sum.send(last), two_sum.send(0)
    branch, sent, begun = tie((branch, sent, begun))

    cross_got = grid.turn(cross_halves[0], 1)
    one_got, two_got = one_sum.swap(last, sent), two_sum.swap(0, begun)
    cut = pairs // 2
    part_width = 3 * PAIR * cut // 2
    front_width = half + part_width
    front_halves = product(core, mixed, branch, front_width, part_width)
    grad_mixed = dot_nt(branch, out_w).astype(LOW)
    grad_front = self_backward(qkv, mixed, grad_mixed, levels, 0, cut)
    front_halves = product(core, normed_one, grad_front, front_width, 0, front_halves)
    grad_mixed, grad_front, one_got, two_got, front_halves, cross_got = tie(
        (grad_mixed, grad_front, one_got, two_got, front_halves, cross_got)
    )
    one_sum.receive(last, one_got)
    two_sum.receive(0, two_got)
    grad_mixed = two_sum.between(grad_mixed)
    cross_sum = Sum(grid, cross_halves[1], cross_got)
    sent, begun, one_total = two_sum.send(last), cross_sum.send(0), one_sum.planes()
    grad_mixed, grad_front, sent, begun, one_total = tie(
        (grad_mixed, grad_front, sent, begun, one_total)
    )

    one_total = across(one_total)
    two_got, front_got = two_sum.swap(last, sent), grid.turn(front_halves[0], 1)
    split = 3 * PAIR * cut
    grad_normed = dot_nt(grad_front, weights[:, :split])
    grad_mixed, grad_normed, two_got, front_got, begun = tie(
        (grad_mixed, grad_normed, two_got, front_got, begun)
    )

    cross_got = cross_sum.swap(0, begun)
    two_sum.receive(last, two_got)
    two_total = two_sum.planes()
    some = (pairs - cut) // 2
    grad_back = self_backward(qkv, mixed, grad_mixed, levels, cut, some, pairs - cut)
    grad_mixed, grad_back, two_total = tie((grad_mixed, grad_back, two_total))
    grad_back = self_backward(
        qkv, mixed, grad_mixed, levels, cut + some, pairs - cut - some, pairs - cut, some, grad_back
    )
    back_halves = product(core, normed_one, grad_back)
    grad_back, back_halves, cross_got, one_total, two_total = tie(
        (grad_back, back_halves, cross_got, one_total, two_total)
    )
    two_total = across(two_total)
    cross_sum.receive(0, cross_got)
    grad_back = cross_sum.between(grad_back)
    front_sum = Sum(grid, front_halves[1], front_got)
    sent, begun = cross_sum.send(last), front_sum.send(0)
    grad_back, sent, begun = tie((grad_back, sent, begun))

    cross_got, front_got = cross_sum.swap(last, sent), front_sum.swap(0, begun)
    back_got = grid.turn(back_halves[0], 1)
    grad_normed = grad_normed + dot_nt(grad_back, weights[:, split : 3 * width])
    token_grad, norm_one = norm_backward(
        tokens[0], gains[0], [grad_normed], grad_after_self, False
    )
    token_grad = token_grad[None]
    prompt_grad = dot_nt(grad_ckv, ckv_w)[None]
    down_at = up_at + quarter
    output = after_cross + dot_nt(active_one, weights[:, down_at : down_at + quarter])
    token_grad, prompt_grad, output, cross_got, front_got, back_got, two_total = tie(
        (token_grad, prompt_grad, output, cross_got, front_got, back_got, two_total)
    )
    cross_sum.receive(last, cross_got)
    front_sum.receive(0, front_got)
    token_grad = front_sum.between(token_grad)
    back_sum = Sum(grid, back_halves[1], back_got)
    sent, begun, cross_total = front_sum.send(last), back_sum.send(0), cross_sum.planes()
    output, sent, begun, cross_total, active_two = tie(
        (output, sent, begun, cross_total, active_two)
    )

    cross_total = across(cross_total)
    front_got, back_got = front_sum.swap(last, sent), back_sum.swap(0, begun)
    output = output + dot_nt(active_two[:, : 2 * quarter], rest_w[:, 3 * quarter : 5 * quarter])
    output, front_got, back_got = tie((output, front_got, back_got))
    front_sum.receive(last, front_got)
    back_sum.receive(0, back_got)
    output = back_sum.between(output)
    layers, sent = front_sum.layers(), back_sum.send(last)
    output, active_two, layers, sent = tie((output, active_two, layers, sent))

    front_layers, got = front_sum.turn_layers(layers), back_sum.swap(last, sent)
    output = output + dot_nt(active_two[:, 2 * quarter :], rest_w[:, 5 * quarter :])
    output = output.astype(LOW)[None]
    output, got = tie((output, got))
    back_sum.receive(last, got)
    layers = back_sum.layers()
    one_total, two_total, layers = tie((one_total, two_total, layers))

    back_layers = back_sum.turn_layers(layers)
    totals = [total.astype(FULL) for total in (one_total, two_total, cross_total)]
    totals.append(front_sum.finish(front_layers))
    squares = sum(jnp.sum(total * total) for total in totals)
    squares, back_layers = tie((squares, back_layers))
    totals.append(back_sum.finish(back_layers))
    squares = squares + jnp.sum(totals[-1] * totals[-1])

    norm_stack = jnp.concatenate([norm_one, norm_two, norm_three])
    payload = jnp.concatenate([norm_stack, jnp.full((2, width), squares, FULL)])
    payload = grid.add_all(payload)
    norm_grads = payload[:-2]
    grad_norm = jnp.sqrt(payload[-1, 0] + jnp.sum(norm_grads * norm_grads))
    norm_grads = lax.dynamic_slice_in_dim(norm_grads, grid.me * own_rows, own_rows, 1)
    factor = CLIP_NORM / jnp.maximum(grad_norm, CLIP_NORM)
    attn_out, mlp_out = adam(
        factor,
        core,
        [grid.unpair(total) for total in totals],
        (attn_master, attn_first, attn_second),
        (mlp_master, mlp_first, mlp_second),
    )
    norm_out = adam_update(
        norm_master, norm_first, norm_second, norm_grads, factor, VECTOR_RATE, 0.0
    )
    return (output, token_grad, prompt_grad, grad_norm, *attn_out, *mlp_out, *norm_out)


def solution(mesh):
    outer, inner = mesh.shape["dp"], mesh.shape["fsdp"]
    fine = jax.sharding.Mesh(mesh.devices.reshape(outer, inner // 2, 2), AXES)
    items = P(AXES, None, None)
    weights = P(None, AXES, None)
    vectors = P(None, AXES)
    return jax.shard_map(
        functools.partial(local, (outer, inner // 2)),
        mesh=fine,
        in_specs=(items, items, P(AXES), items) + (weights,) * 6 + (vectors,) * 3,
        out_specs=(items,) * 3 + (P(),) + (weights,) * 8 + (vectors,) * 4,
        check_vma=False,
    )
```

```python
import functools

import jax
import jax.numpy as jnp
from jax import lax
from jax.experimental import pallas as pl
from jax.experimental.pallas import tpu as pltpu
from jax.sharding import PartitionSpec as P

HD = 64
PAIR = 2 * HD
STEP = 10
TILE = 256

EPSILON = 1e-05
CLIP_NORM = 1.0
BETA_ONE = 0.5
BETA_TWO = 0.5
MATRIX_RATE = 0.04
VECTOR_RATE = 0.3
WEIGHT_DECAY = 0.1
ADAM_EPSILON = 1e-08
SCORE_SCALE = 0.125
MASKED = -1000000000.0
AXES = ("dp", "chip", "core")
LOW = jnp.bfloat16
FULL = jnp.float32


def dot_nn(left, right):
    return lax.dot_general(left, right, (((1,), (0,)), ((), ())), preferred_element_type=FULL)


def dot_nt(left, right):
    return lax.dot_general(left, right, (((1,), (1,)), ((), ())), preferred_element_type=FULL)


def dot_tn(left, right):
    return lax.dot_general(left, right, (((0,), (0,)), ((), ())), preferred_element_type=FULL)


def lane_masks(rows):
    lane = lax.broadcasted_iota(jnp.int32, (rows, PAIR), 1)
    return (lane < HD, lane >= HD)


def forward_pair(queries, keys, values, causal, limit):
    seq = queries.shape[0]
    span = keys.shape[0]
    block = min(TILE, seq)
    masks = lane_masks(block)
    key_masks = lane_masks(span)
    counted = [jnp.where(mask, values, jnp.ones_like(values)) for mask in key_masks]

    def score(start):
        found = []
        for head in range(2):
            query = queries[start : start + block]
            query = jnp.where(masks[head], query, jnp.zeros_like(query)) * SCORE_SCALE
            if causal:
                row = lax.broadcasted_iota(jnp.int32, (block, block), 0)
                col = lax.broadcasted_iota(jnp.int32, (block, block), 1)
                parts = [(start, start + block, col <= row)]
                if start:
                    parts.append((0, start, None))
            else:
                col = lax.broadcasted_iota(jnp.int32, (block, span), 1)
                parts = [(0, span, col < limit)]
            scores = []
            for low, high, allowed in parts:
                value = dot_nt(query, keys[low:high])
                if allowed is not None:
                    value = jnp.where(allowed, value, MASKED)
                scores.append((low, high, value))
            found.append(scores)
        return found

    results = []
    ahead = score(0)
    for start in range(0, seq, block):
        found = ahead
        if start + block < seq:
            ahead = score(start + block)
        peaks, sums = [], []
        for head in range(2):
            peak = None
            for _, _, value in found[head]:
                most = jnp.max(value, axis=1, keepdims=True)
                peak = most if peak is None else jnp.maximum(peak, most)
            peaks.append(peak)
        for head in range(2):
            mixed = None
            for low, high, value in found[head]:
                weight = jnp.exp(value - peaks[head]).astype(LOW)
                part = dot_nn(weight, counted[head][low:high])
                mixed = part if mixed is None else mixed + part
            sums.append(mixed)
        mixed = jnp.where(masks[0], sums[0], sums[1])
        total = pltpu.roll(jnp.where(masks[0], sums[1], sums[0]), HD, 1)
        level = jnp.where(masks[0], peaks[0], peaks[1]) + jnp.log(total)
        results.append((start, start + block, (mixed / total).astype(LOW), level.T))
    return results


def backward_pair(queries, keys, values, mixed, upstream, levels, causal, limit):
    seq = queries.shape[0]
    span = keys.shape[0]
    block = min(TILE, span)
    masks = lane_masks(block)
    scaled = queries * SCORE_SCALE
    inner = (upstream.astype(FULL) * mixed.astype(FULL)).T
    products = [
        jnp.sum(inner[HD * head : HD * (head + 1)], axis=0, keepdims=True) for head in range(2)
    ]
    units = []
    for low in range(0, span, block):
        for head in range(2):
            if not causal:
                units.append((low, head, 0, seq, True))
                continue
            units.append((low, head, low, low + block, True))
            if low + block < seq:
                units.append((low, head, low + block, seq, False))

    def scores(unit):
        low, head, begin, end, checked = unit
        key, value = keys[low : low + block], values[low : low + block]
        key = jnp.where(masks[head], key, jnp.zeros_like(key))
        value = jnp.where(masks[head], value, jnp.zeros_like(value))
        return dot_nt(key, scaled[begin:end]), dot_nt(value, upstream[begin:end])

    def exponents(unit, score, grad_weight):
        low, head, begin, end, checked = unit
        if checked:
            row = lax.broadcasted_iota(jnp.int32, (block, end - begin), 0) + low
            if causal:
                col = lax.broadcasted_iota(jnp.int32, (block, end - begin), 1) + begin
                allowed = row <= col
            else:
                allowed = row < limit
            score = jnp.where(allowed, score, MASKED)
        weight = jnp.exp(score - levels[8 * head : 8 * head + 1, begin:end])
        grad_score = (weight * (grad_weight - products[head][:, begin:end])).astype(LOW)
        return weight.astype(LOW), grad_score

    grad_q = [[None] * (seq // block) for _ in range(2)]
    sums_k, sums_v = {}, {}

    def gather(unit, weight, grad_score):
        low, head, begin, end, _ = unit
        part_v = dot_nn(weight, upstream[begin:end])
        part_k = dot_nn(grad_score, scaled[begin:end])
        part_q = dot_tn(grad_score, keys[low : low + block])
        for sums, part in ((sums_k, part_k), (sums_v, part_v)):
            old = sums.get((low, head))
            sums[low, head] = part if old is None else old + part
        for at in range(begin, end, block):
            piece = part_q[at - begin : at - begin + block]
            old = grad_q[head][at // block]
            grad_q[head][at // block] = piece if old is None else old + piece

    ahead = scores(units[0])
    for number, unit in enumerate(units):
        found = ahead
        if number + 1 < len(units):
            ahead = scores(units[number + 1])
        gather(unit, *exponents(unit, *found))

    grad_k, grad_v, done_q = [], [], []
    for low in range(0, span, block):
        for sums, out in ((sums_k, grad_k), (sums_v, grad_v)):
            value = jnp.where(masks[0], sums[low, 0], sums[low, 1])
            out.append((low, low + block, value.astype(LOW)))
    for number, (one, two) in enumerate(zip(grad_q[0], grad_q[1])):
        value = (jnp.where(masks[0], one, two) * SCORE_SCALE).astype(LOW)
        done_q.append((number * block, (number + 1) * block, value))
    return done_q, grad_k, grad_v


def self_forward_kernel(qkv_ref, out_ref, level_ref):
    queries = qkv_ref[:, :PAIR]
    keys = qkv_ref[:, PAIR : 2 * PAIR]
    values = qkv_ref[:, 2 * PAIR :]
    for start, stop, out, level in forward_pair(queries, keys, values, True, None):
        out_ref[start:stop, :] = out
        level_ref[0, 0:8, start:stop] = level[0:8]
        level_ref[0, 8:16, start:stop] = level[HD : HD + 8]


def self_backward_kernel(qkv_ref, mixed_ref, upstream_ref, level_ref, *rest):
    grad_ref = rest[-1]
    queries = qkv_ref[:, :PAIR]
    keys = qkv_ref[:, PAIR : 2 * PAIR]
    values = qkv_ref[:, 2 * PAIR :]
    found = backward_pair(
        queries, keys, values, mixed_ref[...], upstream_ref[...], level_ref[0], True, None
    )
    for place, rows in enumerate(found):
        for start, stop, value in rows:
            grad_ref[start:stop, place * PAIR : (place + 1) * PAIR] = value


def cross_forward_kernel(limit_ref, query_ref, kv_ref, out_ref, level_ref):
    found = forward_pair(query_ref[...], kv_ref[:, :PAIR], kv_ref[:, PAIR:], False, limit_ref[0])
    for start, stop, out, level in found:
        out_ref[start:stop, :] = out
        level_ref[0, 0:8, start:stop] = level[0:8]
        level_ref[0, 8:16, start:stop] = level[HD : HD + 8]


def cross_backward_kernel(
    limit_ref, query_ref, kv_ref, mixed_ref, upstream_ref, level_ref, grad_q_ref, grad_kv_ref
):
    found = backward_pair(
        query_ref[...],
        kv_ref[:, :PAIR],
        kv_ref[:, PAIR:],
        mixed_ref[...],
        upstream_ref[...],
        level_ref[0],
        False,
        limit_ref[0],
    )
    for start, stop, value in found[0]:
        grad_q_ref[start:stop, :] = value
    for place, rows in enumerate(found[1:]):
        for start, stop, value in rows:
            grad_kv_ref[start:stop, place * PAIR : (place + 1) * PAIR] = value


LARGE = pltpu.CompilerParams(vmem_limit_bytes=56 * 1024 * 1024)
MIDDLE = pltpu.CompilerParams(vmem_limit_bytes=42 * 1024 * 1024)
PARAMS = pltpu.CompilerParams(vmem_limit_bytes=28 * 1024 * 1024)
SCALAR = pl.BlockSpec(memory_space=pltpu.SMEM)


def streamed(value):
    return pltpu.with_memory_space_constraint(value, pltpu.HBM)


def columns(rows, width, offset=0):
    return pl.BlockSpec((rows, width), lambda pair: (0, pair + offset))


def planes(seq):
    return pl.BlockSpec((1, 16, seq), lambda pair: (pair, 0, 0))


SHORT = pl.CostEstimate(flops=1, bytes_accessed=1, transcendentals=0)


def self_forward(qkv):
    seq, width = qkv.shape[0], qkv.shape[1] // 3
    pairs = width // PAIR
    return pl.pallas_call(
        self_forward_kernel,
        grid=(pairs,),
        in_specs=[columns(seq, 3 * PAIR)],
        out_specs=[columns(seq, PAIR), planes(seq)],
        out_shape=[
            jax.ShapeDtypeStruct((seq, width), LOW),
            jax.ShapeDtypeStruct((pairs, 16, seq), FULL),
        ],
        compiler_params=LARGE,
        cost_estimate=SHORT,
        name="self_forward",
    )(streamed(qkv))


def self_backward(qkv, mixed, upstream, levels, start, count, total=None, at=0, old=None):
    seq = qkv.shape[0]
    total = count if total is None else total
    old = [] if old is None else [old]
    return pl.pallas_call(
        self_backward_kernel,
        grid=(count,),
        in_specs=[
            columns(seq, 3 * PAIR, start),
            columns(seq, PAIR, start),
            columns(seq, PAIR, start),
            pl.BlockSpec((1, 16, seq), lambda pair: (pair + start, 0, 0)),
        ]
        + [pl.BlockSpec(memory_space=pl.ANY)] * len(old),
        out_specs=columns(seq, 3 * PAIR, at),
        out_shape=jax.ShapeDtypeStruct((seq, 3 * PAIR * total), LOW),
        input_output_aliases={4: 0} if old else {},
        compiler_params=PARAMS,
        cost_estimate=SHORT,
        name="self_backward",
    )(streamed(qkv), streamed(mixed), upstream, levels, *old)


def cross_forward(limit, queries, pair_states):
    seq, width = queries.shape
    span = pair_states.shape[0]
    pairs = width // PAIR
    return pl.pallas_call(
        cross_forward_kernel,
        grid=(pairs,),
        in_specs=[SCALAR, columns(seq, PAIR), columns(span, 2 * PAIR)],
        out_specs=[columns(seq, PAIR), planes(seq)],
        out_shape=[
            jax.ShapeDtypeStruct((seq, width), LOW),
            jax.ShapeDtypeStruct((pairs, 16, seq), FULL),
        ],
        compiler_params=PARAMS,
        cost_estimate=SHORT,
        name="cross_forward",
    )(limit, queries, pair_states)


def cross_backward(limit, queries, pair_states, mixed, upstream, levels):
    seq, width = queries.shape
    span = pair_states.shape[0]
    pairs = width // PAIR
    return pl.pallas_call(
        cross_backward_kernel,
        grid=(pairs,),
        in_specs=[
            SCALAR,
            columns(seq, PAIR),
            columns(span, 2 * PAIR),
            columns(seq, PAIR),
            columns(seq, PAIR),
            planes(seq),
        ],
        out_specs=[columns(seq, PAIR), columns(span, 2 * PAIR)],
        out_shape=[
            jax.ShapeDtypeStruct((seq, width), LOW),
            jax.ShapeDtypeStruct((span, 2 * width), LOW),
        ],
        compiler_params=PARAMS,
        cost_estimate=SHORT,
        name="cross_backward",
    )(limit, queries, pair_states, mixed, upstream, levels)


def mlp_kernel(order, core_ref, rows_ref, grad_ref, up_ref, down_ref, *rest):
    del core_ref
    count = 2 + max(piece for _, _, piece, _ in order) * 2
    halves_refs, rest = rest[-4 - count : -4], rest[-4:]
    out_ref, back_ref, rows_turned_ref, grad_turned_ref = rest
    step = pl.program_id(0)

    @pl.when(step == 0)
    def _():
        rows_turned_ref[...] = rows_ref[...].T
        grad_turned_ref[...] = grad_ref[...].T
        back_ref[...] = jnp.zeros_like(back_ref)

    seq = rows_ref.shape[0]
    size = min(512, seq)
    width = up_ref.shape[1]

    def ahead(start):
        rows = slice(start, start + size)
        return dot_nn(rows_ref[rows, :], up_ref[...]), dot_nn(grad_ref[rows, :], down_ref[...])

    down_grad, up_grad = None, None
    found = ahead(0)
    for start in range(0, seq, size):
        hidden, grad = found
        if start + size < seq:
            found = ahead(start + size)
        rows = slice(start, start + size)
        share = 0.5 + 0.5 * lax.erf(hidden * 0.7071067811865476)
        bell = jnp.exp(hidden * hidden * -0.5)
        active = (hidden * share).astype(LOW)
        grad_hidden = (grad * (share + hidden * (bell * 0.3989422804014327))).astype(LOW)
        out_ref[rows, :] = active
        down_part = dot_nn(grad_turned_ref[:, rows], active)
        up_part = dot_nn(rows_turned_ref[:, rows], grad_hidden)
        back_ref[rows, :] += dot_nt(grad_hidden, up_ref[...])
        down_grad = down_part if start == 0 else down_grad + down_part
        up_grad = up_part if start == 0 else up_grad + up_part

    for number, half_ref in enumerate(halves_refs):
        steps = [
            at for at, (_, side, piece, _) in enumerate(order) if 2 * piece + 1 - side == number
        ]

        @pl.when((step >= steps[0]) & (step <= steps[-1]))
        def _(half_ref=half_ref):
            half_ref[:, :width] = down_grad.astype(LOW)
            half_ref[:, width:] = up_grad.astype(LOW)


def mlp(core, rows, grad, weights, up_at, down_at, order, old=None):
    seq, width = rows.shape
    block = width // 2
    pieces = 1 + max(piece for _, _, piece, _ in order)

    def chosen(j, values):
        found = values[0]
        for number, value in enumerate(values[1:], 1):
            found = jnp.where(j == number, value, found)
        return found

    def place(j, core):
        quarter = chosen(j, [quarter for quarter, _, _, _ in order])
        return 2 * quarter + (core[0] ^ chosen(j, [side for _, side, _, _ in order]))

    def strip(start):
        return pl.BlockSpec((width, block), lambda j, core: (0, start // block + place(j, core)))

    once = pl.Buffered(1)

    def strips(number):
        mine = [at for at, (_, side, piece, _) in enumerate(order) if 2 * piece + 1 - side == number]
        places = [order[min(max(at, mine[0]), mine[-1])][3] for at in range(len(order))]
        return pl.BlockSpec(
            (width, width), lambda j, core: (0, chosen(j, places)), pipeline_mode=once
        )

    old = [] if old is None else list(old)
    whole = pl.BlockSpec((seq, width), lambda j, core: (0, 0), pipeline_mode=once)
    return pl.pallas_call(
        functools.partial(mlp_kernel, order),
        grid_spec=pltpu.PrefetchScalarGridSpec(
            num_scalar_prefetch=1,
            grid=(len(order),),
            in_specs=[whole, whole, strip(up_at), strip(down_at)]
            + [pl.BlockSpec(memory_space=pl.ANY)] * len(old),
            out_specs=[strips(number) for number in range(2 * pieces)]
            + [pl.BlockSpec((seq, block), lambda j, core: (0, place(j, core))), whole],
            scratch_shapes=[pltpu.VMEM((width, seq), LOW)] * 2,
        ),
        out_shape=[jax.ShapeDtypeStruct((width, 2 * width), LOW)] * (2 * pieces)
        + [
            jax.ShapeDtypeStruct((seq, len(order) * block), LOW),
            jax.ShapeDtypeStruct((seq, width), FULL),
        ],
        input_output_aliases={5: 0, 6: 1} if old else {},
        compiler_params=MIDDLE,
        cost_estimate=SHORT,
        name="mlp",
    )(core, rows, grad, weights, weights, *old)


def matmul_kernel(left_ref, right_ref, out_ref):
    out_ref[...] = dot_nn(left_ref[...], right_ref[...]).astype(LOW)


def matmul(left, right, at, count):
    seq, depth = left.shape
    block = min(512, count)
    return pl.pallas_call(
        matmul_kernel,
        grid=(count // block,),
        in_specs=[
            pl.BlockSpec((seq, depth), lambda step: (0, 0)),
            pl.BlockSpec((depth, block), lambda step: (0, at // block + step)),
        ],
        out_specs=pl.BlockSpec((seq, block), lambda step: (0, step)),
        out_shape=jax.ShapeDtypeStruct((seq, count), LOW),
        compiler_params=PARAMS,
        cost_estimate=SHORT,
        name="matmul",
    )(left, right)


def turned_kernel(left_ref, right_ref, out_ref):
    out_ref[...] = dot_nt(left_ref[...], right_ref[...])


def matmul_turned(left, right, at):
    seq, depth = left.shape
    width = right.shape[0]
    block = min(512, width)
    return pl.pallas_call(
        turned_kernel,
        grid=(width // block,),
        in_specs=[
            pl.BlockSpec((seq, depth), lambda step: (0, 0)),
            pl.BlockSpec((block, depth), lambda step: (step, at // depth)),
        ],
        out_specs=pl.BlockSpec((seq, block), lambda step: (0, step)),
        out_shape=jax.ShapeDtypeStruct((seq, width), FULL),
        compiler_params=PARAMS,
        cost_estimate=SHORT,
        name="matmul_turned",
    )(left, right)


def product_kernel(core_ref, left_ref, sent_ref, kept_ref, *rest):
    del core_ref
    send_ref, keep_ref, turned_ref = rest[-3:]

    @pl.when(pl.program_id(0) == 0)
    def _():
        turned_ref[...] = left_ref[...].T

    send_ref[...] = dot_nn(turned_ref[...], sent_ref[...]).astype(LOW)
    keep_ref[...] = dot_nn(turned_ref[...], kept_ref[...]).astype(LOW)


def product(core, left, right, total=None, at=0, old=None):
    rows, width = left.shape
    half = right.shape[1] // 2
    block = max(b for b in (128, 256, 384, 512) if half % b == 0 and at % b == 0)
    steps, offset = half // block, at // block
    total = half if total is None else total
    old = [] if old is None else list(old)
    return pl.pallas_call(
        product_kernel,
        grid_spec=pltpu.PrefetchScalarGridSpec(
            num_scalar_prefetch=1,
            grid=(steps,),
            in_specs=[
                pl.BlockSpec((rows, width), lambda j, core: (0, 0)),
                pl.BlockSpec((rows, block), lambda j, core: (0, (1 - core[0]) * steps + j)),
                pl.BlockSpec((rows, block), lambda j, core: (0, core[0] * steps + j)),
            ]
            + [pl.BlockSpec(memory_space=pl.ANY)] * len(old),
            out_specs=[pl.BlockSpec((width, block), lambda j, core: (0, offset + j))] * 2,
            scratch_shapes=[pltpu.VMEM((width, rows), LOW)],
        ),
        out_shape=[jax.ShapeDtypeStruct((width, total), LOW)] * 2,
        input_output_aliases={4: 0, 5: 1} if old else {},
        compiler_params=PARAMS,
        cost_estimate=SHORT,
        name="product",
    )(core, streamed(left), right, right, *old)


def pack_kernel(attn_ref, mlp_ref, norm_ref, out_ref, rest_ref):
    width = attn_ref.shape[2]
    hidden = mlp_ref.shape[2]
    quarter = hidden // 4
    for pair in range(width // PAIR):
        source = slice(pair * PAIR, (pair + 1) * PAIR)
        for kind in range(3):
            place = (3 * pair + kind) * PAIR
            out_ref[:, place : place + PAIR] = attn_ref[kind, :, source].astype(LOW)
        for kind in range(2):
            place = 5 * width + (2 * pair + kind) * PAIR
            out_ref[:, place : place + PAIR] = attn_ref[5 + kind, :, source].astype(LOW)
    out_ref[:, 3 * width : 4 * width] = attn_ref[3].astype(LOW)
    out_ref[:, 4 * width : 5 * width] = attn_ref[4].astype(LOW)
    out_ref[:, 7 * width : 8 * width] = attn_ref[7].astype(LOW)
    for kind in range(2):
        place = 8 * width + kind * quarter
        out_ref[:, place : place + quarter] = mlp_ref[kind, :, :quarter].astype(LOW)
        place = kind * 3 * quarter
        rest_ref[:, place : place + 3 * quarter] = mlp_ref[kind, :, quarter:].astype(LOW)
    out_ref[:, 8 * width + 2 * quarter :] = norm_ref[...].astype(LOW)


def pack(attn_master, mlp_master, norm_columns):
    _, rows, width = attn_master.shape
    hidden = mlp_master.shape[2]
    return pl.pallas_call(
        pack_kernel,
        out_shape=[
            jax.ShapeDtypeStruct((rows, 8 * width + hidden // 2 + norm_columns.shape[1]), LOW),
            jax.ShapeDtypeStruct((rows, 3 * hidden // 2), LOW),
        ],
        compiler_params=PARAMS,
        cost_estimate=SHORT,
        name="pack",
    )(attn_master, mlp_master, norm_columns)


class Grid:
    def __init__(self, sizes):
        self.outer, self.chips = sizes
        self.inner = 2 * self.chips
        self.count = self.outer * self.inner
        self.bits = (self.count - 1).bit_length()
        self.core = lax.axis_index("core")
        self.me = lax.axis_index(AXES)
        self.plane = lax.axis_index("dp")
        near = ((self.chips - 1).bit_length() + 1) // 2
        self.x = list(range(near, 0, -1))
        self.y = list(range((self.chips - 1).bit_length(), near, -1))

    def own(self, bit):
        return lax.shift_right_logical(self.me, jnp.int32(bit)) & 1

    def turn(self, value, mask):
        return lax.ppermute(value, AXES, [(i, i ^ mask) for i in range(self.count)])

    def add_all(self, value):
        for bit in range(self.bits):
            value = value + self.turn(value, 1 << bit)
        return value

    def unpair(self, total):
        total = total.reshape(2, total.shape[0] // 2, total.shape[1])
        mine = lax.dynamic_index_in_dim(total, self.core, 0, keepdims=False)
        other = lax.dynamic_index_in_dim(total, 1 - self.core, 0, keepdims=False)
        return mine, self.turn(other, 1)


def add_kernel(counts, side_ref, *refs):
    del side_ref
    outs = refs[sum(counts) :]
    at = 0
    for count, out_ref in zip(counts, outs):
        total = refs[at][...].reshape(out_ref.shape).astype(FULL)
        for ref in refs[at + 1 : at + count]:
            total = total + ref[...].reshape(out_ref.shape).astype(FULL)
        out_ref[...] = total.astype(LOW)
        at += count


def layer_kernel(outer, steps, first, one, two, side_ref, *refs):
    ins, outs = refs[: first + one + two], refs[first + one + two :]

    def fill(parts):
        for step in range(outer):
            plane = side_ref[0] ^ step
            out_ref = outs[step]
            total = parts[0][plane].reshape(out_ref.shape).astype(FULL)
            for part in parts[1:]:
                total = total + part[plane].reshape(out_ref.shape).astype(FULL)
            out_ref[...] = total.astype(out_ref.dtype)

    @pl.when(pl.program_id(0) < steps)
    def _():
        fill(ins[:first] + ins[first : first + one])

    @pl.when(pl.program_id(0) >= steps)
    def _():
        fill(ins[:first] + ins[first + one :])


def plane_kernel(steps, first, one, two, side_ref, *refs):
    del side_ref
    ins, out_ref = refs[:-1], refs[-1]

    def fill(parts):
        total = parts[0][...].reshape(out_ref.shape).astype(FULL)
        for part in parts[1:]:
            total = total + part[...].reshape(out_ref.shape).astype(FULL)
        out_ref[...] = total.astype(LOW)

    @pl.when(pl.program_id(0) < steps)
    def _():
        fill(ins[:first] + ins[first : first + one])

    @pl.when(pl.program_id(0) >= steps)
    def _():
        fill(ins[:first] + ins[first + one :])


class Sum:
    def __init__(self, grid, keep, got):
        self.grid = grid
        self.bits = sorted(grid.x + grid.y, reverse=True)
        self.cut = keep.shape[1] // 2
        self.block = max(b for b in (128, 256, 384, 512, 640) if self.cut % b == 0)
        self.steps = self.cut // self.block
        self.base = [(keep, []), (got, [])]
        self.orders = [grid.x + grid.y, grid.y + grid.x]
        self.extra = [[], []]
        self.stages = len(self.bits)
        sides = [grid.plane] + [grid.own(bit) for bit in self.bits]
        self.sides = jnp.stack(sides).astype(jnp.int32)

    def view(self, term):
        value, done = term
        left = [bit for bit in self.bits if bit not in done]
        outer = self.grid.outer
        share = value.shape[0] // (outer << len(left))
        return value.reshape([outer] + [2] * len(left) + [share, value.shape[1]]), left

    def spec(self, view, left, flips, column):
        places = {bit: 1 + self.bits.index(bit) for bit in flips}

        def index(j, side):
            picks = [
                (side[places[bit]] ^ flips[bit]) if bit in flips else 0 for bit in left
            ]
            return (0, *picks, 0, column(j))

        shape = [view.shape[0]] + [1 if bit in flips else 2 for bit in left]
        return pl.BlockSpec((*shape, view.shape[-2], self.block), index)

    def call(self, kernel, grid, views, specs, out_specs, out_shape, name):
        return pl.pallas_call(
            kernel,
            grid_spec=pltpu.PrefetchScalarGridSpec(
                num_scalar_prefetch=1, grid=grid, in_specs=specs, out_specs=out_specs
            ),
            out_shape=out_shape,
            compiler_params=PARAMS,
            cost_estimate=SHORT,
            name=name,
        )(self.sides, *(streamed(view) for view in views))

    def send(self, stage):
        views, specs, counts = [], [], []
        for half, order in enumerate(self.orders):
            flips = {bit: 0 for bit in order[:stage]}
            flips[order[stage]] = 1
            terms = self.base + self.extra[half]
            counts.append(len(terms))
            for number, term in enumerate(terms):
                view, left = self.view(term)
                shift = half * self.steps if number < len(self.base) else 0
                views.append(view)
                picked = {bit: flip for bit, flip in flips.items() if bit in left}
                specs.append(self.spec(view, left, picked, lambda j, shift=shift: shift + j))
        rows = self.base[0][0].shape[0] >> (stage + 1)
        return self.call(
            functools.partial(add_kernel, counts),
            (self.steps,),
            views,
            specs,
            [pl.BlockSpec((rows, self.block), lambda j, side: (0, j))] * 2,
            [jax.ShapeDtypeStruct((rows, self.cut), LOW)] * 2,
            "add",
        )

    def swap(self, stage, out):
        return [self.grid.turn(v, 1 << order[stage]) for order, v in zip(self.orders, out)]

    def receive(self, stage, got):
        for half, value in enumerate(got):
            self.extra[half].append((value, self.orders[half][: stage + 1]))

    def between(self, main):
        for stage in range(1, self.stages - 1):
            main, sent = tie((main, self.send(stage)))
            main, got = tie((main, self.swap(stage, sent)))
            self.receive(stage, got)
        return main

    def layers(self):
        views, specs, counts = self.columns()
        outer = self.grid.outer
        share = views[0].shape[-2]
        shape = (share, 2 * self.cut)
        return self.call(
            functools.partial(layer_kernel, outer, self.steps, *counts),
            (2 * self.steps,),
            views,
            specs,
            [pl.BlockSpec((share, self.block), lambda j, side: (0, j))] * outer,
            [jax.ShapeDtypeStruct(shape, FULL)] + [jax.ShapeDtypeStruct(shape, LOW)] * (outer - 1),
            "layers",
        )

    def planes(self):
        views, specs, counts = self.columns()
        rows = views[0].shape[0] * views[0].shape[-2]
        value = self.call(
            functools.partial(plane_kernel, self.steps, *counts),
            (2 * self.steps,),
            views,
            specs,
            pl.BlockSpec((rows, self.block), lambda j, side: (0, j)),
            jax.ShapeDtypeStruct((rows, 2 * self.cut), LOW),
            "planes",
        )
        return value

    def columns(self):
        views, specs = [], []
        steps = self.steps
        groups = (
            (self.base, lambda j: j),
            (self.extra[0], lambda j: jnp.minimum(j, steps - 1)),
            (self.extra[1], lambda j: jnp.maximum(j - steps, 0)),
        )
        for terms, column in groups:
            for term in terms:
                view, left = self.view(term)
                views.append(view)
                specs.append(self.spec(view, left, {bit: 0 for bit in left}, column))
        return views, specs, [len(terms) for terms, _ in groups]

    def turn_layers(self, layers, steps=None):
        grid = self.grid
        found = [
            grid.turn(layers[step], step * grid.inner) for step in steps or range(1, grid.outer)
        ]
        return found if steps else [layers[0]] + found

    def finish(self, got):
        return sum((value.astype(FULL) for value in got[1:]), got[0])


def norm_forward(rows, gain, bias):
    centre = jnp.mean(rows, axis=-1, keepdims=True)
    centred = rows - centre
    spread = jnp.mean(centred * centred, axis=-1, keepdims=True)
    scale = lax.rsqrt(spread + EPSILON)
    return (centred * scale * gain + bias).astype(LOW)


def norm_backward_kernel(count, rows_ref, gain_ref, base_ref, *rest):
    grad_refs, out_ref, rest = rest[:count], rest[count], rest[count + 1 :]
    sums_ref = rest[-1]
    rows = rows_ref[...].astype(FULL)
    centred = rows - jnp.mean(rows, axis=1, keepdims=True)
    spread = jnp.mean(centred * centred, axis=1, keepdims=True)
    scale = lax.rsqrt(spread + EPSILON)
    plain = centred * scale
    grad = grad_refs[0][...]
    for ref in grad_refs[1:]:
        grad = grad + ref[...]
    weighted = grad * gain_ref[...]
    mean_one = jnp.mean(weighted, axis=1, keepdims=True)
    mean_two = jnp.mean(weighted * plain, axis=1, keepdims=True)
    total = base_ref[...].astype(FULL) + scale * (weighted - mean_one - plain * mean_two)
    out_ref[...] = total
    if len(rest) > 1:
        rest[0][...] = total.astype(LOW)

    @pl.when(pl.program_id(0) == 0)
    def _():
        sums_ref[...] = jnp.zeros_like(sums_ref)

    sums_ref[0:1, :] += jnp.sum(grad * plain, axis=0, keepdims=True)
    sums_ref[1:2, :] += jnp.sum(grad, axis=0, keepdims=True)


def norm_backward(rows, gain, grads, base, rounded=True):
    seq, width = rows.shape
    block = pl.BlockSpec((min(TILE, seq), width), lambda step: (step, 0))
    more = [jax.ShapeDtypeStruct((seq, width), LOW)] if rounded else []
    out = pl.pallas_call(
        functools.partial(norm_backward_kernel, len(grads)),
        grid=(max(1, seq // TILE),),
        in_specs=[block, pl.BlockSpec((1, width), lambda step: (0, 0)), block]
        + [block] * len(grads),
        out_specs=[block] * (1 + len(more)) + [pl.BlockSpec((8, width), lambda step: (0, 0))],
        out_shape=[jax.ShapeDtypeStruct((seq, width), FULL)]
        + more
        + [jax.ShapeDtypeStruct((8, width), FULL)],
        compiler_params=PARAMS,
        cost_estimate=SHORT,
        name="norm_backward",
    )(streamed(rows), gain.reshape(1, width), streamed(base), *(map(streamed, grads) if len(grads) > 1 else grads))
    return *out[:-1], out[-1][:2]


def adam_update(master, first, second, gradient, factor, rate, decay):
    gradient = gradient * factor
    first_new = BETA_ONE * first + (1.0 - BETA_ONE) * gradient
    second_new = BETA_TWO * second + (1.0 - BETA_TWO) * gradient * gradient
    first_fix = 1.0 - BETA_ONE**STEP
    second_fix = 1.0 - BETA_TWO**STEP
    update = first_new / first_fix / (jnp.sqrt(second_new / second_fix) + ADAM_EPSILON)
    master_new = master - rate * (update + decay * master)
    return (first_new, second_new, master_new, master_new.astype(LOW))


def adam_places(width, hidden):
    pairs = width // PAIR
    cut, half = pairs // 2, width // 2
    places = []
    for side in range(2):
        block = hidden // 8
        for piece, part in ((0, 0), (0, 1), (1, 0), (1, 1)):
            number = 4 * piece + 2 * part + side
            for kind in range(2):
                start = (2 * part + kind) * block
                places.append((1, 1 - kind, number * block, piece, start, side, block))
        for piece, first, count in ((3, 0, cut), (4, cut, pairs - cut)):
            for pair in range(count // 2):
                column = (first + side * (count // 2) + pair) * PAIR
                for kind in range(3):
                    places.append((0, kind, column, piece, (3 * pair + kind) * PAIR, side, PAIR))
        places.append((0, 3, side * half, 3, 3 * PAIR * cut // 2, side, half))
        places.append((0, 4, side * half, 2, half, side, half))
        for pair in range(pairs // 2):
            column = (side * (pairs // 2) + pair) * PAIR
            for kind in range(2):
                start = width + (2 * pair + kind) * PAIR
                places.append((0, 5 + kind, column, 2, start, side, PAIR))
        places.append((0, 7, side * half, 2, 0, side, half))
    return places


def adam_kernel(places, factor_ref, core_ref, *refs):
    grads, olds, news = refs[:10], refs[10:16], refs[16:]
    factor = factor_ref[0]
    core = core_ref[0]
    for into, matrix, column, piece, start, side, size in places:
        mine, other = (ref[:, start : start + size] for ref in grads[2 * piece : 2 * piece + 2])
        gradient = jnp.where(core == side, mine, other)
        old = [ref[matrix, :, column : column + size] for ref in olds[3 * into : 3 * into + 3]]
        new = adam_update(*old, gradient, factor, MATRIX_RATE, WEIGHT_DECAY)
        for ref, value in zip(news[4 * into : 4 * into + 4], new):
            ref[matrix, :, column : column + size] = value


def adam(factor, core, pieces, attn, mlp):
    width, hidden = attn[0].shape[2], mlp[0].shape[2]
    shapes = []
    for group in (attn, mlp):
        shape = group[0].shape
        shapes += [jax.ShapeDtypeStruct(shape, FULL)] * 3 + [jax.ShapeDtypeStruct(shape, LOW)]
    operands = [value for pair in pieces for value in pair] + list(attn) + list(mlp)
    def whole(value):
        return pl.BlockSpec(value.shape, lambda step: (0,) * len(value.shape))

    out = pl.pallas_call(
        functools.partial(adam_kernel, adam_places(width, hidden)),
        grid=(1,),
        in_specs=[SCALAR, SCALAR] + [whole(value) for value in operands],
        out_specs=[whole(value) for value in shapes],
        out_shape=shapes,
        compiler_params=LARGE,
        cost_estimate=SHORT,
        name="adam",
    )(factor.reshape(1), core, *operands)
    return out[:4], out[4:]


def tie(values):
    return lax.optimization_barrier(values)


def local(
    sizes,
    tokens,
    prompt,
    prompt_len,
    cotangent,
    attn_master,
    attn_first,
    attn_second,
    mlp_master,
    mlp_first,
    mlp_second,
    norm_master,
    norm_first,
    norm_second,
):
    grid = Grid(sizes)
    _, seq, width = tokens.shape
    own_rows = attn_master.shape[1]
    hidden = mlp_master.shape[2]
    norm_columns = jnp.pad(norm_master.T, ((0, 0), (0, PAIR - norm_master.shape[0])))
    shard, rest_shard = pack(attn_master, mlp_master, norm_columns)
    weights = lax.all_gather(shard, AXES, axis=0, tiled=True)
    rest_w = lax.all_gather(rest_shard, AXES, axis=0, tiled=True)
    grad_out = cotangent[0]
    up_at, quarter = 8 * width, hidden // 4
    gains = weights[:, up_at + 2 * quarter :].T[: norm_master.shape[0]].astype(FULL)
    out_w, cq_w, ckv_w, cout_w = (
        weights[:, low * width : high * width] for low, high in ((3, 4), (4, 5), (5, 7), (7, 8))
    )

    inputs = tokens[0].astype(FULL)
    normed_one = norm_forward(inputs, gains[0], gains[1])
    qkv = matmul(normed_one, weights, 0, 3 * width)
    mixed, levels = self_forward(qkv)
    after_self = inputs + dot_nn(mixed, out_w)
    normed_two = norm_forward(after_self, gains[2], gains[3])
    cross_q = dot_nn(normed_two, cq_w).astype(LOW)
    states = prompt[0]
    cross_kv = dot_nn(states, ckv_w).astype(LOW)
    crossed, cross_levels = cross_forward(prompt_len, cross_q, cross_kv)
    after_cross = after_self + dot_nn(crossed, cout_w)
    normed_three = norm_forward(after_cross, gains[4], gains[5])

    core = grid.core.astype(jnp.int32).reshape(1)
    half = width // 2
    pairs = width // PAIR
    def across(value):
        return lax.psum_scatter(value, "dp", scatter_dimension=0, tiled=True)

    *one_halves, active_one, back_one = mlp(
        core,
        normed_three,
        grad_out,
        weights,
        up_at,
        up_at + quarter,
        ((0, 0, 0, 0), (0, 1, 0, 0)),
    )
    normed_three, one_halves, rest_w = tie((normed_three, one_halves, rest_w))
    *halves, active_two, back_two = mlp(
        core,
        normed_three,
        grad_out,
        rest_w,
        0,
        3 * quarter,
        ((0, 0, 0, 1), (0, 1, 0, 1), (1, 0, 1, 0), (2, 0, 1, 1), (1, 1, 1, 0), (2, 1, 1, 1)),
        one_halves,
    )
    one_halves, two_halves = halves[:2], halves[2:]
    grads, one_halves, two_halves = tie(((back_one, back_two), one_halves, two_halves))

    one_got = grid.turn(one_halves[0], 1)
    grad_after_cross, branch, norm_three = norm_backward(after_cross, gains[4], grads, grad_out)
    cross_halves = product(core, crossed, branch, 2 * width, 0)
    grad_crossed = dot_nt(branch, cout_w).astype(LOW)
    grad_crossed, one_got, cross_halves = tie((grad_crossed, one_got, cross_halves))
    one_sum = Sum(grid, one_halves[1], one_got)
    last = one_sum.stages - 1
    sent = one_sum.send(0)
    grad_crossed, sent, two_halves = tie((grad_crossed, sent, two_halves))

    one_got, two_got = one_sum.swap(0, sent), grid.turn(two_halves[0], 1)
    grad_cq, grad_ckv = cross_backward(
        prompt_len, cross_q, cross_kv, crossed, grad_crossed, cross_levels
    )
    cross_halves = product(core, normed_two, grad_cq, 2 * width, half, cross_halves)
    cross_halves = product(core, states, grad_ckv, 2 * width, width, cross_halves)
    grad_cq, cross_halves, two_got = tie((grad_cq, cross_halves, two_got))

    grad_normed = matmul_turned(grad_cq, weights, 4 * width)
    grad_after_self, branch, norm_two = norm_backward(
        after_self, gains[2], [grad_normed], grad_after_cross
    )
    branch, one_got, cross_halves = tie((branch, one_got, cross_halves))
    one_sum.receive(0, one_got)
    branch = one_sum.between(branch)
    two_sum = Sum(grid, two_halves[1], two_got)
    sent, begun = one_sum.send(last), two_sum.send(0)
    branch, sent, begun = tie((branch, sent, begun))

    cross_got = grid.turn(cross_halves[0], 1)
    one_got, two_got = one_sum.swap(last, sent), two_sum.swap(0, begun)
    cut = pairs // 2
    part_width = 3 * PAIR * cut // 2
    front_width = half + part_width
    front_halves = product(core, mixed, branch, front_width, part_width)
    grad_mixed = dot_nt(branch, out_w).astype(LOW)
    grad_front = self_backward(qkv, mixed, grad_mixed, levels, 0, cut)
    front_halves = product(core, normed_one, grad_front, front_width, 0, front_halves)
    grad_mixed, grad_front, one_got, two_got, front_halves, cross_got = tie(
        (grad_mixed, grad_front, one_got, two_got, front_halves, cross_got)
    )
    two_sum.receive(0, two_got)
    grad_mixed = two_sum.between(grad_mixed)
    sent = two_sum.send(last)
    grad_mixed, grad_front, sent, one_got, cross_got = tie(
        (grad_mixed, grad_front, sent, one_got, cross_got)
    )

    two_got, front_got = two_sum.swap(last, sent), grid.turn(front_halves[0], 1)
    one_sum.receive(last, one_got)
    one_total = one_sum.planes()
    cross_sum = Sum(grid, cross_halves[1], cross_got)
    begun = cross_sum.send(0)
    split = 3 * PAIR * cut
    grad_normed = dot_nt(grad_front, weights[:, :split])
    grad_mixed, grad_normed, two_got, front_got, begun, one_total = tie(
        (grad_mixed, grad_normed, two_got, front_got, begun, one_total)
    )

    one_total = across(one_total)
    cross_got = cross_sum.swap(0, begun)
    two_sum.receive(last, two_got)
    two_total = two_sum.planes()
    some = (pairs - cut) // 2
    grad_back = self_backward(qkv, mixed, grad_mixed, levels, cut, some, pairs - cut)
    grad_mixed, grad_back, two_total = tie((grad_mixed, grad_back, two_total))
    grad_back = self_backward(
        qkv, mixed, grad_mixed, levels, cut + some, pairs - cut - some, pairs - cut, some, grad_back
    )
    back_halves = product(core, normed_one, grad_back)
    grad_back, back_halves, cross_got, one_total, two_total = tie(
        (grad_back, back_halves, cross_got, one_total, two_total)
    )
    two_total = across(two_total)
    cross_sum.receive(0, cross_got)
    grad_back = cross_sum.between(grad_back)
    front_sum = Sum(grid, front_halves[1], front_got)
    sent, begun = cross_sum.send(last), front_sum.send(0)
    grad_back, sent, begun, grad_ckv, active_one = tie(
        (grad_back, sent, begun, grad_ckv, active_one)
    )

    cross_got, front_got = cross_sum.swap(last, sent), front_sum.swap(0, begun)
    back_got = grid.turn(back_halves[0], 1)
    grad_normed = grad_normed + dot_nt(grad_back, weights[:, split : 3 * width])
    token_grad, norm_one = norm_backward(
        tokens[0], gains[0], [grad_normed], grad_after_self, False
    )
    token_grad = token_grad[None]
    prompt_grad = dot_nt(grad_ckv, ckv_w)[None]
    down_at = up_at + quarter
    output = after_cross + dot_nt(active_one, weights[:, down_at : down_at + quarter])
    token_grad, prompt_grad, output, cross_got, front_got, back_got, two_total = tie(
        (token_grad, prompt_grad, output, cross_got, front_got, back_got, two_total)
    )
    front_sum.receive(0, front_got)
    token_grad = front_sum.between(token_grad)
    back_sum = Sum(grid, back_halves[1], back_got)
    sent, begun = front_sum.send(last), back_sum.send(0)
    output, sent, begun, cross_got, active_two = tie(
        (output, sent, begun, cross_got, active_two)
    )

    cross_sum.receive(last, cross_got)
    cross_total = cross_sum.planes()
    front_got, back_got = front_sum.swap(last, sent), back_sum.swap(0, begun)
    output = output + dot_nt(active_two[:, : 2 * quarter], rest_w[:, 3 * quarter : 5 * quarter])
    output, front_got, back_got, cross_total = tie((output, front_got, back_got, cross_total))
    cross_total = across(cross_total)
    front_sum.receive(last, front_got)
    back_sum.receive(0, back_got)
    output = back_sum.between(output)
    layers, sent = front_sum.layers(), back_sum.send(last)
    output, active_two, layers, sent = tie((output, active_two, layers, sent))

    front_layers, got = front_sum.turn_layers(layers), back_sum.swap(last, sent)
    output = output + dot_nt(active_two[:, 2 * quarter :], rest_w[:, 5 * quarter :])
    output = output.astype(LOW)[None]
    output, got = tie((output, got))
    back_sum.receive(last, got)
    layers = back_sum.layers()
    one_total, two_total, layers = tie((one_total, two_total, layers))

    back_layers = back_sum.turn_layers(layers)
    totals = [total.astype(FULL) for total in (one_total, two_total, cross_total)]
    totals.append(front_sum.finish(front_layers))
    squares = sum(jnp.sum(total * total) for total in totals)
    squares, back_layers = tie((squares, back_layers))
    totals.append(back_sum.finish(back_layers))
    squares = squares + jnp.sum(totals[-1] * totals[-1])

    norm_stack = jnp.concatenate([norm_one, norm_two, norm_three])
    payload = jnp.concatenate([norm_stack, jnp.full((2, width), squares, FULL)])
    payload = grid.add_all(payload)
    norm_grads = payload[:-2]
    grad_norm = jnp.sqrt(payload[-1, 0] + jnp.sum(norm_grads * norm_grads))
    norm_grads = lax.dynamic_slice_in_dim(norm_grads, grid.me * own_rows, own_rows, 1)
    factor = CLIP_NORM / jnp.maximum(grad_norm, CLIP_NORM)
    attn_out, mlp_out = adam(
        factor,
        core,
        [grid.unpair(total) for total in totals],
        (attn_master, attn_first, attn_second),
        (mlp_master, mlp_first, mlp_second),
    )
    norm_out = adam_update(
        norm_master, norm_first, norm_second, norm_grads, factor, VECTOR_RATE, 0.0
    )
    return (output, token_grad, prompt_grad, grad_norm, *attn_out, *mlp_out, *norm_out)


def solution(mesh):
    outer, inner = mesh.shape["dp"], mesh.shape["fsdp"]
    fine = jax.sharding.Mesh(mesh.devices.reshape(outer, inner // 2, 2), AXES)
    items = P(AXES, None, None)
    weights = P(None, AXES, None)
    vectors = P(None, AXES)
    return jax.shard_map(
        functools.partial(local, (outer, inner // 2)),
        mesh=fine,
        in_specs=(items, items, P(AXES), items) + (weights,) * 6 + (vectors,) * 3,
        out_specs=(items,) * 3 + (P(),) + (weights,) * 8 + (vectors,) * 4,
        check_vma=False,
    )
```

```python
import functools

import jax
import jax.numpy as jnp
from jax import lax
from jax.experimental import pallas as pl
from jax.experimental.pallas import tpu as pltpu
from jax.sharding import PartitionSpec as P

HD = 64
PAIR = 2 * HD
STEP = 10
TILE = 256

EPSILON = 1e-05
CLIP_NORM = 1.0
BETA_ONE = 0.5
BETA_TWO = 0.5
MATRIX_RATE = 0.04
VECTOR_RATE = 0.3
WEIGHT_DECAY = 0.1
ADAM_EPSILON = 1e-08
SCORE_SCALE = 0.125
MASKED = -1000000000.0
AXES = ("dp", "chip", "core")
LOW = jnp.bfloat16
FULL = jnp.float32


def dot_nn(left, right):
    return lax.dot_general(left, right, (((1,), (0,)), ((), ())), preferred_element_type=FULL)


def dot_nt(left, right):
    return lax.dot_general(left, right, (((1,), (1,)), ((), ())), preferred_element_type=FULL)


def dot_tn(left, right):
    return lax.dot_general(left, right, (((0,), (0,)), ((), ())), preferred_element_type=FULL)


def lane_masks(rows):
    lane = lax.broadcasted_iota(jnp.int32, (rows, PAIR), 1)
    return (lane < HD, lane >= HD)


def forward_pair(queries, keys, values, causal, limit):
    seq = queries.shape[0]
    span = keys.shape[0]
    block = min(TILE, seq)
    masks = lane_masks(block)
    key_masks = lane_masks(span)
    counted = [jnp.where(mask, values, jnp.ones_like(values)) for mask in key_masks]

    def score(start):
        found = []
        for head in range(2):
            query = queries[start : start + block]
            query = jnp.where(masks[head], query, jnp.zeros_like(query)) * SCORE_SCALE
            if causal:
                row = lax.broadcasted_iota(jnp.int32, (block, block), 0)
                col = lax.broadcasted_iota(jnp.int32, (block, block), 1)
                parts = [(start, start + block, col <= row)]
                if start:
                    parts.append((0, start, None))
            else:
                col = lax.broadcasted_iota(jnp.int32, (block, span), 1)
                parts = [(0, span, col < limit)]
            scores = []
            for low, high, allowed in parts:
                value = dot_nt(query, keys[low:high])
                if allowed is not None:
                    value = jnp.where(allowed, value, MASKED)
                scores.append((low, high, value))
            found.append(scores)
        return found

    results = []
    ahead = score(0)
    for start in range(0, seq, block):
        found = ahead
        if start + block < seq:
            ahead = score(start + block)
        peaks, sums = [], []
        for head in range(2):
            peak = None
            for _, _, value in found[head]:
                most = jnp.max(value, axis=1, keepdims=True)
                peak = most if peak is None else jnp.maximum(peak, most)
            peaks.append(peak)
        for head in range(2):
            mixed = None
            for low, high, value in found[head]:
                weight = jnp.exp(value - peaks[head]).astype(LOW)
                part = dot_nn(weight, counted[head][low:high])
                mixed = part if mixed is None else mixed + part
            sums.append(mixed)
        mixed = jnp.where(masks[0], sums[0], sums[1])
        total = pltpu.roll(jnp.where(masks[0], sums[1], sums[0]), HD, 1)
        level = jnp.where(masks[0], peaks[0], peaks[1]) + jnp.log(total)
        results.append((start, start + block, (mixed / total).astype(LOW), level.T))
    return results


def backward_pair(queries, keys, values, mixed, upstream, levels, causal, limit):
    seq = queries.shape[0]
    span = keys.shape[0]
    block = min(TILE, span)
    masks = lane_masks(block)
    scaled = queries * SCORE_SCALE
    inner = (upstream.astype(FULL) * mixed.astype(FULL)).T
    products = [
        jnp.sum(inner[HD * head : HD * (head + 1)], axis=0, keepdims=True) for head in range(2)
    ]
    units = []
    for low in range(0, span, block):
        for head in range(2):
            if not causal:
                units.append((low, head, 0, seq, True))
                continue
            units.append((low, head, low, low + block, True))
            if low + block < seq:
                units.append((low, head, low + block, seq, False))

    def scores(unit):
        low, head, begin, end, checked = unit
        key, value = keys[low : low + block], values[low : low + block]
        key = jnp.where(masks[head], key, jnp.zeros_like(key))
        value = jnp.where(masks[head], value, jnp.zeros_like(value))
        return dot_nt(key, scaled[begin:end]), dot_nt(value, upstream[begin:end])

    def exponents(unit, score, grad_weight):
        low, head, begin, end, checked = unit
        if checked:
            row = lax.broadcasted_iota(jnp.int32, (block, end - begin), 0) + low
            if causal:
                col = lax.broadcasted_iota(jnp.int32, (block, end - begin), 1) + begin
                allowed = row <= col
            else:
                allowed = row < limit
            score = jnp.where(allowed, score, MASKED)
        weight = jnp.exp(score - levels[8 * head : 8 * head + 1, begin:end])
        grad_score = (weight * (grad_weight - products[head][:, begin:end])).astype(LOW)
        return weight.astype(LOW), grad_score

    grad_q = [[None] * (seq // block) for _ in range(2)]
    sums_k, sums_v = {}, {}

    def gather(unit, weight, grad_score):
        low, head, begin, end, _ = unit
        part_v = dot_nn(weight, upstream[begin:end])
        part_k = dot_nn(grad_score, scaled[begin:end])
        part_q = dot_tn(grad_score, keys[low : low + block])
        for sums, part in ((sums_k, part_k), (sums_v, part_v)):
            old = sums.get((low, head))
            sums[low, head] = part if old is None else old + part
        for at in range(begin, end, block):
            piece = part_q[at - begin : at - begin + block]
            old = grad_q[head][at // block]
            grad_q[head][at // block] = piece if old is None else old + piece

    ahead = scores(units[0])
    for number, unit in enumerate(units):
        found = ahead
        if number + 1 < len(units):
            ahead = scores(units[number + 1])
        gather(unit, *exponents(unit, *found))

    grad_k, grad_v, done_q = [], [], []
    for low in range(0, span, block):
        for sums, out in ((sums_k, grad_k), (sums_v, grad_v)):
            value = jnp.where(masks[0], sums[low, 0], sums[low, 1])
            out.append((low, low + block, value.astype(LOW)))
    for number, (one, two) in enumerate(zip(grad_q[0], grad_q[1])):
        value = (jnp.where(masks[0], one, two) * SCORE_SCALE).astype(LOW)
        done_q.append((number * block, (number + 1) * block, value))
    return done_q, grad_k, grad_v


def self_forward_kernel(qkv_ref, out_ref, level_ref):
    queries = qkv_ref[:, :PAIR]
    keys = qkv_ref[:, PAIR : 2 * PAIR]
    values = qkv_ref[:, 2 * PAIR :]
    for start, stop, out, level in forward_pair(queries, keys, values, True, None):
        out_ref[start:stop, :] = out
        level_ref[0, 0:8, start:stop] = level[0:8]
        level_ref[0, 8:16, start:stop] = level[HD : HD + 8]


def self_backward_kernel(qkv_ref, mixed_ref, upstream_ref, level_ref, *rest):
    grad_ref = rest[-1]
    queries = qkv_ref[:, :PAIR]
    keys = qkv_ref[:, PAIR : 2 * PAIR]
    values = qkv_ref[:, 2 * PAIR :]
    found = backward_pair(
        queries, keys, values, mixed_ref[...], upstream_ref[...], level_ref[0], True, None
    )
    for place, rows in enumerate(found):
        for start, stop, value in rows:
            grad_ref[start:stop, place * PAIR : (place + 1) * PAIR] = value


def cross_forward_kernel(limit_ref, query_ref, kv_ref, out_ref, level_ref):
    found = forward_pair(query_ref[...], kv_ref[:, :PAIR], kv_ref[:, PAIR:], False, limit_ref[0])
    for start, stop, out, level in found:
        out_ref[start:stop, :] = out
        level_ref[0, 0:8, start:stop] = level[0:8]
        level_ref[0, 8:16, start:stop] = level[HD : HD + 8]


def cross_backward_kernel(
    limit_ref, query_ref, kv_ref, mixed_ref, upstream_ref, level_ref, grad_q_ref, grad_kv_ref
):
    found = backward_pair(
        query_ref[...],
        kv_ref[:, :PAIR],
        kv_ref[:, PAIR:],
        mixed_ref[...],
        upstream_ref[...],
        level_ref[0],
        False,
        limit_ref[0],
    )
    for start, stop, value in found[0]:
        grad_q_ref[start:stop, :] = value
    for place, rows in enumerate(found[1:]):
        for start, stop, value in rows:
            grad_kv_ref[start:stop, place * PAIR : (place + 1) * PAIR] = value


LARGE = pltpu.CompilerParams(vmem_limit_bytes=56 * 1024 * 1024)
MIDDLE = pltpu.CompilerParams(vmem_limit_bytes=42 * 1024 * 1024)
PARAMS = pltpu.CompilerParams(vmem_limit_bytes=28 * 1024 * 1024)
SCALAR = pl.BlockSpec(memory_space=pltpu.SMEM)


def streamed(value):
    return pltpu.with_memory_space_constraint(value, pltpu.HBM)


def columns(rows, width, offset=0):
    return pl.BlockSpec((rows, width), lambda pair: (0, pair + offset))


def planes(seq):
    return pl.BlockSpec((1, 16, seq), lambda pair: (pair, 0, 0))


SHORT = pl.CostEstimate(flops=1, bytes_accessed=1, transcendentals=0)


def self_forward(qkv):
    seq, width = qkv.shape[0], qkv.shape[1] // 3
    pairs = width // PAIR
    return pl.pallas_call(
        self_forward_kernel,
        grid=(pairs,),
        in_specs=[columns(seq, 3 * PAIR)],
        out_specs=[columns(seq, PAIR), planes(seq)],
        out_shape=[
            jax.ShapeDtypeStruct((seq, width), LOW),
            jax.ShapeDtypeStruct((pairs, 16, seq), FULL),
        ],
        compiler_params=LARGE,
        cost_estimate=SHORT,
        name="self_forward",
    )(streamed(qkv))


def self_backward(qkv, mixed, upstream, levels, start, count, total=None, at=0, old=None):
    seq = qkv.shape[0]
    total = count if total is None else total
    old = [] if old is None else [old]
    return pl.pallas_call(
        self_backward_kernel,
        grid=(count,),
        in_specs=[
            columns(seq, 3 * PAIR, start),
            columns(seq, PAIR, start),
            columns(seq, PAIR, start),
            pl.BlockSpec((1, 16, seq), lambda pair: (pair + start, 0, 0)),
        ]
        + [pl.BlockSpec(memory_space=pl.ANY)] * len(old),
        out_specs=columns(seq, 3 * PAIR, at),
        out_shape=jax.ShapeDtypeStruct((seq, 3 * PAIR * total), LOW),
        input_output_aliases={4: 0} if old else {},
        compiler_params=PARAMS,
        cost_estimate=SHORT,
        name="self_backward",
    )(streamed(qkv), streamed(mixed), upstream, levels, *old)


def cross_forward(limit, queries, pair_states):
    seq, width = queries.shape
    span = pair_states.shape[0]
    pairs = width // PAIR
    return pl.pallas_call(
        cross_forward_kernel,
        grid=(pairs,),
        in_specs=[SCALAR, columns(seq, PAIR), columns(span, 2 * PAIR)],
        out_specs=[columns(seq, PAIR), planes(seq)],
        out_shape=[
            jax.ShapeDtypeStruct((seq, width), LOW),
            jax.ShapeDtypeStruct((pairs, 16, seq), FULL),
        ],
        compiler_params=PARAMS,
        cost_estimate=SHORT,
        name="cross_forward",
    )(limit, queries, pair_states)


def cross_backward(limit, queries, pair_states, mixed, upstream, levels):
    seq, width = queries.shape
    span = pair_states.shape[0]
    pairs = width // PAIR
    return pl.pallas_call(
        cross_backward_kernel,
        grid=(pairs,),
        in_specs=[
            SCALAR,
            columns(seq, PAIR),
            columns(span, 2 * PAIR),
            columns(seq, PAIR),
            columns(seq, PAIR),
            planes(seq),
        ],
        out_specs=[columns(seq, PAIR), columns(span, 2 * PAIR)],
        out_shape=[
            jax.ShapeDtypeStruct((seq, width), LOW),
            jax.ShapeDtypeStruct((span, 2 * width), LOW),
        ],
        compiler_params=PARAMS,
        cost_estimate=SHORT,
        name="cross_backward",
    )(limit, queries, pair_states, mixed, upstream, levels)


def mlp_kernel(order, core_ref, rows_ref, grad_ref, up_ref, down_ref, *rest):
    del core_ref
    count = 2 + max(piece for _, _, piece, _ in order) * 2
    halves_refs, rest = rest[-4 - count : -4], rest[-4:]
    out_ref, back_ref, rows_turned_ref, grad_turned_ref = rest
    step = pl.program_id(0)

    @pl.when(step == 0)
    def _():
        rows_turned_ref[...] = rows_ref[...].T
        grad_turned_ref[...] = grad_ref[...].T
        back_ref[...] = jnp.zeros_like(back_ref)

    seq = rows_ref.shape[0]
    size = min(512, seq)
    width = up_ref.shape[1]

    def ahead(start):
        rows = slice(start, start + size)
        return dot_nn(rows_ref[rows, :], up_ref[...]), dot_nn(grad_ref[rows, :], down_ref[...])

    down_grad, up_grad = None, None
    found = ahead(0)
    for start in range(0, seq, size):
        hidden, grad = found
        if start + size < seq:
            found = ahead(start + size)
        rows = slice(start, start + size)
        share = 0.5 + 0.5 * lax.erf(hidden * 0.7071067811865476)
        bell = jnp.exp(hidden * hidden * -0.5)
        active = (hidden * share).astype(LOW)
        grad_hidden = (grad * (share + hidden * (bell * 0.3989422804014327))).astype(LOW)
        out_ref[rows, :] = active
        down_part = dot_nn(grad_turned_ref[:, rows], active)
        up_part = dot_nn(rows_turned_ref[:, rows], grad_hidden)
        back_ref[rows, :] += dot_nt(grad_hidden, up_ref[...])
        down_grad = down_part if start == 0 else down_grad + down_part
        up_grad = up_part if start == 0 else up_grad + up_part

    for number, half_ref in enumerate(halves_refs):
        steps = [
            at for at, (_, side, piece, _) in enumerate(order) if 2 * piece + 1 - side == number
        ]

        @pl.when((step >= steps[0]) & (step <= steps[-1]))
        def _(half_ref=half_ref):
            half_ref[:, :width] = down_grad.astype(LOW)
            half_ref[:, width:] = up_grad.astype(LOW)


def mlp(core, rows, grad, weights, up_at, down_at, order, old=None):
    seq, width = rows.shape
    block = width // 2
    pieces = 1 + max(piece for _, _, piece, _ in order)

    def chosen(j, values):
        found = values[0]
        for number, value in enumerate(values[1:], 1):
            found = jnp.where(j == number, value, found)
        return found

    def place(j, core):
        quarter = chosen(j, [quarter for quarter, _, _, _ in order])
        return 2 * quarter + (core[0] ^ chosen(j, [side for _, side, _, _ in order]))

    def strip(start):
        return pl.BlockSpec((width, block), lambda j, core: (0, start // block + place(j, core)))

    once = pl.Buffered(1)

    def strips(number):
        mine = [at for at, (_, side, piece, _) in enumerate(order) if 2 * piece + 1 - side == number]
        places = [order[min(max(at, mine[0]), mine[-1])][3] for at in range(len(order))]
        return pl.BlockSpec(
            (width, width), lambda j, core: (0, chosen(j, places)), pipeline_mode=once
        )

    old = [] if old is None else list(old)
    whole = pl.BlockSpec((seq, width), lambda j, core: (0, 0), pipeline_mode=once)
    return pl.pallas_call(
        functools.partial(mlp_kernel, order),
        grid_spec=pltpu.PrefetchScalarGridSpec(
            num_scalar_prefetch=1,
            grid=(len(order),),
            in_specs=[whole, whole, strip(up_at), strip(down_at)]
            + [pl.BlockSpec(memory_space=pl.ANY)] * len(old),
            out_specs=[strips(number) for number in range(2 * pieces)]
            + [pl.BlockSpec((seq, block), lambda j, core: (0, place(j, core))), whole],
            scratch_shapes=[pltpu.VMEM((width, seq), LOW)] * 2,
        ),
        out_shape=[jax.ShapeDtypeStruct((width, 2 * width), LOW)] * (2 * pieces)
        + [
            jax.ShapeDtypeStruct((seq, len(order) * block), LOW),
            jax.ShapeDtypeStruct((seq, width), FULL),
        ],
        input_output_aliases={5: 0, 6: 1} if old else {},
        compiler_params=MIDDLE,
        cost_estimate=SHORT,
        name="mlp",
    )(core, rows, grad, weights, weights, *old)


def matmul_kernel(left_ref, right_ref, out_ref):
    out_ref[...] = dot_nn(left_ref[...], right_ref[...]).astype(LOW)


def matmul(left, right, at, count):
    seq, depth = left.shape
    block = min(512, count)
    return pl.pallas_call(
        matmul_kernel,
        grid=(count // block,),
        in_specs=[
            pl.BlockSpec((seq, depth), lambda step: (0, 0)),
            pl.BlockSpec((depth, block), lambda step: (0, at // block + step)),
        ],
        out_specs=pl.BlockSpec((seq, block), lambda step: (0, step)),
        out_shape=jax.ShapeDtypeStruct((seq, count), LOW),
        compiler_params=PARAMS,
        cost_estimate=SHORT,
        name="matmul",
    )(left, right)


def turned_kernel(left_ref, right_ref, out_ref):
    out_ref[...] = dot_nt(left_ref[...], right_ref[...])


def matmul_turned(left, right, at):
    seq, depth = left.shape
    width = right.shape[0]
    block = min(512, width)
    return pl.pallas_call(
        turned_kernel,
        grid=(width // block,),
        in_specs=[
            pl.BlockSpec((seq, depth), lambda step: (0, 0)),
            pl.BlockSpec((block, depth), lambda step: (step, at // depth)),
        ],
        out_specs=pl.BlockSpec((seq, block), lambda step: (0, step)),
        out_shape=jax.ShapeDtypeStruct((seq, width), FULL),
        compiler_params=PARAMS,
        cost_estimate=SHORT,
        name="matmul_turned",
    )(left, right)


def product_kernel(core_ref, left_ref, sent_ref, kept_ref, *rest):
    del core_ref
    send_ref, keep_ref, turned_ref = rest[-3:]

    @pl.when(pl.program_id(0) == 0)
    def _():
        turned_ref[...] = left_ref[...].T

    send_ref[...] = dot_nn(turned_ref[...], sent_ref[...]).astype(LOW)
    keep_ref[...] = dot_nn(turned_ref[...], kept_ref[...]).astype(LOW)


def product(core, left, right, total=None, at=0, old=None):
    rows, width = left.shape
    half = right.shape[1] // 2
    block = max(b for b in (128, 256, 384, 512) if half % b == 0 and at % b == 0)
    steps, offset = half // block, at // block
    total = half if total is None else total
    old = [] if old is None else list(old)
    return pl.pallas_call(
        product_kernel,
        grid_spec=pltpu.PrefetchScalarGridSpec(
            num_scalar_prefetch=1,
            grid=(steps,),
            in_specs=[
                pl.BlockSpec((rows, width), lambda j, core: (0, 0)),
                pl.BlockSpec((rows, block), lambda j, core: (0, (1 - core[0]) * steps + j)),
                pl.BlockSpec((rows, block), lambda j, core: (0, core[0] * steps + j)),
            ]
            + [pl.BlockSpec(memory_space=pl.ANY)] * len(old),
            out_specs=[pl.BlockSpec((width, block), lambda j, core: (0, offset + j))] * 2,
            scratch_shapes=[pltpu.VMEM((width, rows), LOW)],
        ),
        out_shape=[jax.ShapeDtypeStruct((width, total), LOW)] * 2,
        input_output_aliases={4: 0, 5: 1} if old else {},
        compiler_params=PARAMS,
        cost_estimate=SHORT,
        name="product",
    )(core, streamed(left), right, right, *old)


def pack_kernel(attn_ref, mlp_ref, norm_ref, out_ref, rest_ref):
    width = attn_ref.shape[2]
    hidden = mlp_ref.shape[2]
    quarter = hidden // 4
    for pair in range(width // PAIR):
        source = slice(pair * PAIR, (pair + 1) * PAIR)
        for kind in range(3):
            place = (3 * pair + kind) * PAIR
            out_ref[:, place : place + PAIR] = attn_ref[kind, :, source].astype(LOW)
        for kind in range(2):
            place = 5 * width + (2 * pair + kind) * PAIR
            out_ref[:, place : place + PAIR] = attn_ref[5 + kind, :, source].astype(LOW)
    out_ref[:, 3 * width : 4 * width] = attn_ref[3].astype(LOW)
    out_ref[:, 4 * width : 5 * width] = attn_ref[4].astype(LOW)
    out_ref[:, 7 * width : 8 * width] = attn_ref[7].astype(LOW)
    for kind in range(2):
        place = 8 * width + kind * quarter
        out_ref[:, place : place + quarter] = mlp_ref[kind, :, :quarter].astype(LOW)
        place = kind * 3 * quarter
        rest_ref[:, place : place + 3 * quarter] = mlp_ref[kind, :, quarter:].astype(LOW)
    out_ref[:, 8 * width + 2 * quarter :] = norm_ref[...].astype(LOW)


def pack(attn_master, mlp_master, norm_columns):
    _, rows, width = attn_master.shape
    hidden = mlp_master.shape[2]
    return pl.pallas_call(
        pack_kernel,
        out_shape=[
            jax.ShapeDtypeStruct((rows, 8 * width + hidden // 2 + norm_columns.shape[1]), LOW),
            jax.ShapeDtypeStruct((rows, 3 * hidden // 2), LOW),
        ],
        compiler_params=PARAMS,
        cost_estimate=SHORT,
        name="pack",
    )(attn_master, mlp_master, norm_columns)


class Grid:
    def __init__(self, sizes):
        self.outer, self.chips = sizes
        self.inner = 2 * self.chips
        self.count = self.outer * self.inner
        self.bits = (self.count - 1).bit_length()
        self.core = lax.axis_index("core")
        self.me = lax.axis_index(AXES)
        self.plane = lax.axis_index("dp")
        near = ((self.chips - 1).bit_length() + 1) // 2
        self.x = list(range(near, 0, -1))
        self.y = list(range((self.chips - 1).bit_length(), near, -1))

    def own(self, bit):
        return lax.shift_right_logical(self.me, jnp.int32(bit)) & 1

    def turn(self, value, mask):
        return lax.ppermute(value, AXES, [(i, i ^ mask) for i in range(self.count)])

    def add_all(self, value):
        low = 1
        for size in (2, self.chips, self.outer):
            found = [value] + [self.turn(value, step * low) for step in range(1, size)]
            place = (self.me // low) % size
            if size > 2:
                stack = jnp.stack(found)
                found = [self.pick(stack, place ^ step) for step in range(size)]
            value = sum(found[1:], found[0])
            low *= size
        return value

    def pick(self, stack, index):
        return lax.dynamic_index_in_dim(stack, index, 0, keepdims=False)

    def unpair(self, total):
        total = total.reshape(2, total.shape[0] // 2, total.shape[1])
        mine = lax.dynamic_index_in_dim(total, self.core, 0, keepdims=False)
        other = lax.dynamic_index_in_dim(total, 1 - self.core, 0, keepdims=False)
        return mine, self.turn(other, 1)


def add_kernel(counts, side_ref, *refs):
    del side_ref
    outs = refs[sum(counts) :]
    at = 0
    for count, out_ref in zip(counts, outs):
        total = refs[at][...].reshape(out_ref.shape).astype(FULL)
        for ref in refs[at + 1 : at + count]:
            total = total + ref[...].reshape(out_ref.shape).astype(FULL)
        out_ref[...] = total.astype(LOW)
        at += count


def layer_kernel(outer, steps, first, one, two, side_ref, *refs):
    ins, outs = refs[: first + one + two], refs[first + one + two :]

    def fill(parts):
        for step in range(outer):
            plane = side_ref[0] ^ step
            out_ref = outs[step]
            total = parts[0][plane].reshape(out_ref.shape).astype(FULL)
            for part in parts[1:]:
                total = total + part[plane].reshape(out_ref.shape).astype(FULL)
            out_ref[...] = total.astype(out_ref.dtype)

    @pl.when(pl.program_id(0) < steps)
    def _():
        fill(ins[:first] + ins[first : first + one])

    @pl.when(pl.program_id(0) >= steps)
    def _():
        fill(ins[:first] + ins[first + one :])


def plane_kernel(steps, first, one, two, side_ref, *refs):
    del side_ref
    ins, out_ref = refs[:-1], refs[-1]

    def fill(parts):
        total = parts[0][...].reshape(out_ref.shape).astype(FULL)
        for part in parts[1:]:
            total = total + part[...].reshape(out_ref.shape).astype(FULL)
        out_ref[...] = total.astype(LOW)

    @pl.when(pl.program_id(0) < steps)
    def _():
        fill(ins[:first] + ins[first : first + one])

    @pl.when(pl.program_id(0) >= steps)
    def _():
        fill(ins[:first] + ins[first + one :])


class Sum:
    def __init__(self, grid, keep, got):
        self.grid = grid
        self.bits = sorted(grid.x + grid.y, reverse=True)
        self.cut = keep.shape[1] // 2
        self.block = max(b for b in (128, 256, 384, 512, 640) if self.cut % b == 0)
        self.steps = self.cut // self.block
        self.base = [(keep, []), (got, [])]
        self.orders = [grid.x + grid.y, grid.y + grid.x]
        self.extra = [[], []]
        self.stages = len(self.bits)
        sides = [grid.plane] + [grid.own(bit) for bit in self.bits]
        self.sides = jnp.stack(sides).astype(jnp.int32)

    def view(self, term):
        value, done = term
        left = [bit for bit in self.bits if bit not in done]
        outer = self.grid.outer
        share = value.shape[0] // (outer << len(left))
        return value.reshape([outer] + [2] * len(left) + [share, value.shape[1]]), left

    def spec(self, view, left, flips, column):
        places = {bit: 1 + self.bits.index(bit) for bit in flips}

        def index(j, side):
            picks = [
                (side[places[bit]] ^ flips[bit]) if bit in flips else 0 for bit in left
            ]
            return (0, *picks, 0, column(j))

        shape = [view.shape[0]] + [1 if bit in flips else 2 for bit in left]
        return pl.BlockSpec((*shape, view.shape[-2], self.block), index)

    def call(self, kernel, grid, views, specs, out_specs, out_shape, name):
        return pl.pallas_call(
            kernel,
            grid_spec=pltpu.PrefetchScalarGridSpec(
                num_scalar_prefetch=1, grid=grid, in_specs=specs, out_specs=out_specs
            ),
            out_shape=out_shape,
            compiler_params=PARAMS,
            cost_estimate=SHORT,
            name=name,
        )(self.sides, *(streamed(view) for view in views))

    def send(self, stage):
        views, specs, counts = [], [], []
        for half, order in enumerate(self.orders):
            flips = {bit: 0 for bit in order[:stage]}
            flips[order[stage]] = 1
            terms = self.base + self.extra[half]
            counts.append(len(terms))
            for number, term in enumerate(terms):
                view, left = self.view(term)
                shift = half * self.steps if number < len(self.base) else 0
                views.append(view)
                picked = {bit: flip for bit, flip in flips.items() if bit in left}
                specs.append(self.spec(view, left, picked, lambda j, shift=shift: shift + j))
        rows = self.base[0][0].shape[0] >> (stage + 1)
        return self.call(
            functools.partial(add_kernel, counts),
            (self.steps,),
            views,
            specs,
            [pl.BlockSpec((rows, self.block), lambda j, side: (0, j))] * 2,
            [jax.ShapeDtypeStruct((rows, self.cut), LOW)] * 2,
            "add",
        )

    def swap(self, stage, out):
        return [self.grid.turn(v, 1 << order[stage]) for order, v in zip(self.orders, out)]

    def receive(self, stage, got):
        for half, value in enumerate(got):
            self.extra[half].append((value, self.orders[half][: stage + 1]))

    def between(self, main):
        for stage in range(1, self.stages - 1):
            main, sent = tie((main, self.send(stage)))
            main, got = tie((main, self.swap(stage, sent)))
            self.receive(stage, got)
        return main

    def layers(self):
        views, specs, counts = self.columns()
        outer = self.grid.outer
        share = views[0].shape[-2]
        shape = (share, 2 * self.cut)
        return self.call(
            functools.partial(layer_kernel, outer, self.steps, *counts),
            (2 * self.steps,),
            views,
            specs,
            [pl.BlockSpec((share, self.block), lambda j, side: (0, j))] * outer,
            [jax.ShapeDtypeStruct(shape, FULL)] + [jax.ShapeDtypeStruct(shape, LOW)] * (outer - 1),
            "layers",
        )

    def planes(self):
        views, specs, counts = self.columns()
        rows = views[0].shape[0] * views[0].shape[-2]
        value = self.call(
            functools.partial(plane_kernel, self.steps, *counts),
            (2 * self.steps,),
            views,
            specs,
            pl.BlockSpec((rows, self.block), lambda j, side: (0, j)),
            jax.ShapeDtypeStruct((rows, 2 * self.cut), LOW),
            "planes",
        )
        return value

    def columns(self):
        views, specs = [], []
        steps = self.steps
        groups = (
            (self.base, lambda j: j),
            (self.extra[0], lambda j: jnp.minimum(j, steps - 1)),
            (self.extra[1], lambda j: jnp.maximum(j - steps, 0)),
        )
        for terms, column in groups:
            for term in terms:
                view, left = self.view(term)
                views.append(view)
                specs.append(self.spec(view, left, {bit: 0 for bit in left}, column))
        return views, specs, [len(terms) for terms, _ in groups]

    def turn_layers(self, layers, steps=None):
        grid = self.grid
        found = [
            grid.turn(layers[step], step * grid.inner) for step in steps or range(1, grid.outer)
        ]
        return found if steps else [layers[0]] + found

    def finish(self, got):
        return sum((value.astype(FULL) for value in got[1:]), got[0])


def norm_forward(rows, gain, bias):
    centre = jnp.mean(rows, axis=-1, keepdims=True)
    centred = rows - centre
    spread = jnp.mean(centred * centred, axis=-1, keepdims=True)
    scale = lax.rsqrt(spread + EPSILON)
    return (centred * scale * gain + bias).astype(LOW)


def norm_backward_kernel(count, rows_ref, gain_ref, base_ref, *rest):
    grad_refs, out_ref, rest = rest[:count], rest[count], rest[count + 1 :]
    sums_ref = rest[-1]
    rows = rows_ref[...].astype(FULL)
    centred = rows - jnp.mean(rows, axis=1, keepdims=True)
    spread = jnp.mean(centred * centred, axis=1, keepdims=True)
    scale = lax.rsqrt(spread + EPSILON)
    plain = centred * scale
    grad = grad_refs[0][...]
    for ref in grad_refs[1:]:
        grad = grad + ref[...]
    weighted = grad * gain_ref[...]
    mean_one = jnp.mean(weighted, axis=1, keepdims=True)
    mean_two = jnp.mean(weighted * plain, axis=1, keepdims=True)
    total = base_ref[...].astype(FULL) + scale * (weighted - mean_one - plain * mean_two)
    out_ref[...] = total
    if len(rest) > 1:
        rest[0][...] = total.astype(LOW)

    @pl.when(pl.program_id(0) == 0)
    def _():
        sums_ref[...] = jnp.zeros_like(sums_ref)

    sums_ref[0:1, :] += jnp.sum(grad * plain, axis=0, keepdims=True)
    sums_ref[1:2, :] += jnp.sum(grad, axis=0, keepdims=True)


def norm_backward(rows, gain, grads, base, rounded=True):
    seq, width = rows.shape
    block = pl.BlockSpec((min(TILE, seq), width), lambda step: (step, 0))
    more = [jax.ShapeDtypeStruct((seq, width), LOW)] if rounded else []
    out = pl.pallas_call(
        functools.partial(norm_backward_kernel, len(grads)),
        grid=(max(1, seq // TILE),),
        in_specs=[block, pl.BlockSpec((1, width), lambda step: (0, 0)), block]
        + [block] * len(grads),
        out_specs=[block] * (1 + len(more)) + [pl.BlockSpec((8, width), lambda step: (0, 0))],
        out_shape=[jax.ShapeDtypeStruct((seq, width), FULL)]
        + more
        + [jax.ShapeDtypeStruct((8, width), FULL)],
        compiler_params=PARAMS,
        cost_estimate=SHORT,
        name="norm_backward",
    )(streamed(rows), gain.reshape(1, width), streamed(base), *(map(streamed, grads) if len(grads) > 1 else grads))
    return *out[:-1], out[-1][:2]


def adam_update(master, first, second, gradient, factor, rate, decay):
    gradient = gradient * factor
    first_new = BETA_ONE * first + (1.0 - BETA_ONE) * gradient
    second_new = BETA_TWO * second + (1.0 - BETA_TWO) * gradient * gradient
    first_fix = 1.0 - BETA_ONE**STEP
    second_fix = 1.0 - BETA_TWO**STEP
    update = first_new / first_fix / (jnp.sqrt(second_new / second_fix) + ADAM_EPSILON)
    master_new = master - rate * (update + decay * master)
    return (first_new, second_new, master_new, master_new.astype(LOW))


def adam_places(width, hidden):
    pairs = width // PAIR
    cut, half = pairs // 2, width // 2
    places = []
    for side in range(2):
        block = hidden // 8
        for piece, part in ((0, 0), (0, 1), (1, 0), (1, 1)):
            number = 4 * piece + 2 * part + side
            for kind in range(2):
                start = (2 * part + kind) * block
                places.append((1, 1 - kind, number * block, piece, start, side, block))
        for piece, first, count in ((3, 0, cut), (4, cut, pairs - cut)):
            for pair in range(count // 2):
                column = (first + side * (count // 2) + pair) * PAIR
                for kind in range(3):
                    places.append((0, kind, column, piece, (3 * pair + kind) * PAIR, side, PAIR))
        places.append((0, 3, side * half, 3, 3 * PAIR * cut // 2, side, half))
        places.append((0, 4, side * half, 2, half, side, half))
        for pair in range(pairs // 2):
            column = (side * (pairs // 2) + pair) * PAIR
            for kind in range(2):
                start = width + (2 * pair + kind) * PAIR
                places.append((0, 5 + kind, column, 2, start, side, PAIR))
        places.append((0, 7, side * half, 2, 0, side, half))
    return places


def adam_kernel(places, factor_ref, core_ref, *refs):
    grads, olds, news = refs[:10], refs[10:16], refs[16:]
    factor = factor_ref[0]
    core = core_ref[0]
    for into, matrix, column, piece, start, side, size in places:
        mine, other = (ref[:, start : start + size] for ref in grads[2 * piece : 2 * piece + 2])
        gradient = jnp.where(core == side, mine, other)
        old = [ref[matrix, :, column : column + size] for ref in olds[3 * into : 3 * into + 3]]
        new = adam_update(*old, gradient, factor, MATRIX_RATE, WEIGHT_DECAY)
        for ref, value in zip(news[4 * into : 4 * into + 4], new):
            ref[matrix, :, column : column + size] = value


def adam(factor, core, pieces, attn, mlp):
    width, hidden = attn[0].shape[2], mlp[0].shape[2]
    shapes = []
    for group in (attn, mlp):
        shape = group[0].shape
        shapes += [jax.ShapeDtypeStruct(shape, FULL)] * 3 + [jax.ShapeDtypeStruct(shape, LOW)]
    operands = [value for pair in pieces for value in pair] + list(attn) + list(mlp)
    def whole(value):
        return pl.BlockSpec(value.shape, lambda step: (0,) * len(value.shape))

    out = pl.pallas_call(
        functools.partial(adam_kernel, adam_places(width, hidden)),
        grid=(1,),
        in_specs=[SCALAR, SCALAR] + [whole(value) for value in operands],
        out_specs=[whole(value) for value in shapes],
        out_shape=shapes,
        compiler_params=LARGE,
        cost_estimate=SHORT,
        name="adam",
    )(factor.reshape(1), core, *operands)
    return out[:4], out[4:]


def tie(values):
    return lax.optimization_barrier(values)


def local(
    sizes,
    tokens,
    prompt,
    prompt_len,
    cotangent,
    attn_master,
    attn_first,
    attn_second,
    mlp_master,
    mlp_first,
    mlp_second,
    norm_master,
    norm_first,
    norm_second,
):
    grid = Grid(sizes)
    _, seq, width = tokens.shape
    own_rows = attn_master.shape[1]
    hidden = mlp_master.shape[2]
    norm_columns = jnp.pad(norm_master.T, ((0, 0), (0, PAIR - norm_master.shape[0])))
    shard, rest_shard = pack(attn_master, mlp_master, norm_columns)
    weights = lax.all_gather(shard, AXES, axis=0, tiled=True)
    rest_w = lax.all_gather(rest_shard, AXES, axis=0, tiled=True)
    grad_out = cotangent[0]
    up_at, quarter = 8 * width, hidden // 4
    gains = weights[:, up_at + 2 * quarter :].T[: norm_master.shape[0]].astype(FULL)
    out_w, cq_w, ckv_w, cout_w = (
        weights[:, low * width : high * width] for low, high in ((3, 4), (4, 5), (5, 7), (7, 8))
    )

    inputs = tokens[0].astype(FULL)
    normed_one = norm_forward(inputs, gains[0], gains[1])
    qkv = matmul(normed_one, weights, 0, 3 * width)
    mixed, levels = self_forward(qkv)
    after_self = inputs + dot_nn(mixed, out_w)
    normed_two = norm_forward(after_self, gains[2], gains[3])
    cross_q = dot_nn(normed_two, cq_w).astype(LOW)
    states = prompt[0]
    cross_kv = dot_nn(states, ckv_w).astype(LOW)
    crossed, cross_levels = cross_forward(prompt_len, cross_q, cross_kv)
    after_cross = after_self + dot_nn(crossed, cout_w)
    normed_three = norm_forward(after_cross, gains[4], gains[5])

    core = grid.core.astype(jnp.int32).reshape(1)
    half = width // 2
    pairs = width // PAIR
    def across(value):
        return lax.psum_scatter(value, "dp", scatter_dimension=0, tiled=True)

    *one_halves, active_one, back_one = mlp(
        core,
        normed_three,
        grad_out,
        weights,
        up_at,
        up_at + quarter,
        ((0, 0, 0, 0), (0, 1, 0, 0)),
    )
    normed_three, one_halves, rest_w = tie((normed_three, one_halves, rest_w))
    *halves, active_two, back_two = mlp(
        core,
        normed_three,
        grad_out,
        rest_w,
        0,
        3 * quarter,
        ((0, 0, 0, 1), (0, 1, 0, 1), (1, 0, 1, 0), (2, 0, 1, 1), (1, 1, 1, 0), (2, 1, 1, 1)),
        one_halves,
    )
    one_halves, two_halves = halves[:2], halves[2:]
    grads, one_halves, two_halves = tie(((back_one, back_two), one_halves, two_halves))

    one_got = grid.turn(one_halves[0], 1)
    grad_after_cross, branch, norm_three = norm_backward(after_cross, gains[4], grads, grad_out)
    cross_halves = product(core, crossed, branch, 2 * width, 0)
    grad_crossed = dot_nt(branch, cout_w).astype(LOW)
    grad_crossed, one_got, cross_halves = tie((grad_crossed, one_got, cross_halves))
    one_sum = Sum(grid, one_halves[1], one_got)
    last = one_sum.stages - 1
    sent = one_sum.send(0)
    grad_crossed, sent, two_halves = tie((grad_crossed, sent, two_halves))

    one_got, two_got = one_sum.swap(0, sent), grid.turn(two_halves[0], 1)
    grad_cq, grad_ckv = cross_backward(
        prompt_len, cross_q, cross_kv, crossed, grad_crossed, cross_levels
    )
    cross_halves = product(core, normed_two, grad_cq, 2 * width, half, cross_halves)
    cross_halves = product(core, states, grad_ckv, 2 * width, width, cross_halves)
    grad_cq, cross_halves, two_got = tie((grad_cq, cross_halves, two_got))

    grad_normed = matmul_turned(grad_cq, weights, 4 * width)
    grad_after_self, branch, norm_two = norm_backward(
        after_self, gains[2], [grad_normed], grad_after_cross
    )
    branch, one_got, cross_halves = tie((branch, one_got, cross_halves))
    one_sum.receive(0, one_got)
    branch = one_sum.between(branch)
    two_sum = Sum(grid, two_halves[1], two_got)
    sent, begun = one_sum.send(last), two_sum.send(0)
    branch, sent, begun = tie((branch, sent, begun))

    cross_got = grid.turn(cross_halves[0], 1)
    one_got, two_got = one_sum.swap(last, sent), two_sum.swap(0, begun)
    cut = pairs // 2
    part_width = 3 * PAIR * cut // 2
    front_width = half + part_width
    front_halves = product(core, mixed, branch, front_width, part_width)
    grad_mixed = dot_nt(branch, out_w).astype(LOW)
    grad_front = self_backward(qkv, mixed, grad_mixed, levels, 0, cut)
    front_halves = product(core, normed_one, grad_front, front_width, 0, front_halves)
    grad_mixed, grad_front, one_got, two_got, front_halves, cross_got = tie(
        (grad_mixed, grad_front, one_got, two_got, front_halves, cross_got)
    )
    two_sum.receive(0, two_got)
    grad_mixed = two_sum.between(grad_mixed)
    sent = two_sum.send(last)
    grad_mixed, grad_front, sent, one_got, cross_got = tie(
        (grad_mixed, grad_front, sent, one_got, cross_got)
    )

    two_got, front_got = two_sum.swap(last, sent), grid.turn(front_halves[0], 1)
    one_sum.receive(last, one_got)
    one_total = one_sum.planes()
    cross_sum = Sum(grid, cross_halves[1], cross_got)
    begun = cross_sum.send(0)
    split = 3 * PAIR * cut
    grad_normed = dot_nt(grad_front, weights[:, :split])
    grad_mixed, grad_normed, two_got, front_got, begun, one_total = tie(
        (grad_mixed, grad_normed, two_got, front_got, begun, one_total)
    )

    one_total = across(one_total)
    cross_got = cross_sum.swap(0, begun)
    two_sum.receive(last, two_got)
    two_total = two_sum.planes()
    some = (pairs - cut) // 2
    grad_back = self_backward(qkv, mixed, grad_mixed, levels, cut, some, pairs - cut)
    grad_mixed, grad_back, two_total = tie((grad_mixed, grad_back, two_total))
    grad_back = self_backward(
        qkv, mixed, grad_mixed, levels, cut + some, pairs - cut - some, pairs - cut, some, grad_back
    )
    grad_back, one_total, two_total = tie((grad_back, one_total, two_total))

    two_total = across(two_total)
    back_halves = product(core, normed_one, grad_back)
    grad_back, back_halves, cross_got = tie((grad_back, back_halves, cross_got))
    cross_sum.receive(0, cross_got)
    grad_back = cross_sum.between(grad_back)
    sent = cross_sum.send(last)
    grad_back, sent, grad_ckv, active_one, front_got = tie(
        (grad_back, sent, grad_ckv, active_one, front_got)
    )

    cross_got, back_got = cross_sum.swap(last, sent), grid.turn(back_halves[0], 1)
    front_sum = Sum(grid, front_halves[1], front_got)
    begun = front_sum.send(0)
    grad_normed = grad_normed + dot_nt(grad_back, weights[:, split : 3 * width])
    prompt_grad = dot_nt(grad_ckv, ckv_w)[None]
    grad_normed, prompt_grad, cross_got, back_got, two_total, begun = tie(
        (grad_normed, prompt_grad, cross_got, back_got, two_total, begun)
    )

    front_got = front_sum.swap(0, begun)
    cross_sum.receive(last, cross_got)
    cross_total = cross_sum.planes()
    grad_normed, cross_total = tie((grad_normed, cross_total))
    cross_total = across(cross_total)
    token_grad, norm_one = norm_backward(
        tokens[0], gains[0], [grad_normed], grad_after_self, False
    )
    token_grad = token_grad[None]
    down_at = up_at + quarter
    output = after_cross + dot_nt(active_one, weights[:, down_at : down_at + quarter])
    token_grad, output, front_got = tie((token_grad, output, front_got))
    front_sum.receive(0, front_got)
    token_grad = front_sum.between(token_grad)
    back_sum = Sum(grid, back_halves[1], back_got)
    sent, begun = front_sum.send(last), back_sum.send(0)
    output, sent, begun, active_two = tie((output, sent, begun, active_two))

    front_got, back_got = front_sum.swap(last, sent), back_sum.swap(0, begun)
    output = output + dot_nt(active_two[:, : 2 * quarter], rest_w[:, 3 * quarter : 5 * quarter])
    output, front_got, back_got, cross_total = tie((output, front_got, back_got, cross_total))
    front_sum.receive(last, front_got)
    back_sum.receive(0, back_got)
    output = back_sum.between(output)
    layers, sent = front_sum.layers(), back_sum.send(last)
    output, active_two, layers, sent = tie((output, active_two, layers, sent))

    front_layers, got = front_sum.turn_layers(layers), back_sum.swap(last, sent)
    output = output + dot_nt(active_two[:, 2 * quarter :], rest_w[:, 5 * quarter :])
    output = output.astype(LOW)[None]
    output, got = tie((output, got))
    back_sum.receive(last, got)
    layers = back_sum.layers()
    one_total, two_total, layers = tie((one_total, two_total, layers))

    back_layers = back_sum.turn_layers(layers)
    totals = [total.astype(FULL) for total in (one_total, two_total, cross_total)]
    totals.append(front_sum.finish(front_layers))
    squares = sum(jnp.sum(total * total) for total in totals)
    squares, back_layers = tie((squares, back_layers))
    totals.append(back_sum.finish(back_layers))
    squares = squares + jnp.sum(totals[-1] * totals[-1])

    norm_stack = jnp.concatenate([norm_one, norm_two, norm_three])
    payload = jnp.concatenate([norm_stack, jnp.full((2, width), squares, FULL)])
    payload = grid.add_all(payload)
    norm_grads = payload[:-2]
    grad_norm = jnp.sqrt(payload[-1, 0] + jnp.sum(norm_grads * norm_grads))
    norm_grads = lax.dynamic_slice_in_dim(norm_grads, grid.me * own_rows, own_rows, 1)
    factor = CLIP_NORM / jnp.maximum(grad_norm, CLIP_NORM)
    attn_out, mlp_out = adam(
        factor,
        core,
        [grid.unpair(total) for total in totals],
        (attn_master, attn_first, attn_second),
        (mlp_master, mlp_first, mlp_second),
    )
    norm_out = adam_update(
        norm_master, norm_first, norm_second, norm_grads, factor, VECTOR_RATE, 0.0
    )
    return (output, token_grad, prompt_grad, grad_norm, *attn_out, *mlp_out, *norm_out)


def solution(mesh):
    outer, inner = mesh.shape["dp"], mesh.shape["fsdp"]
    fine = jax.sharding.Mesh(mesh.devices.reshape(outer, inner // 2, 2), AXES)
    items = P(AXES, None, None)
    weights = P(None, AXES, None)
    vectors = P(None, AXES)
    return jax.shard_map(
        functools.partial(local, (outer, inner // 2)),
        mesh=fine,
        in_specs=(items, items, P(AXES), items) + (weights,) * 6 + (vectors,) * 3,
        out_specs=(items,) * 3 + (P(),) + (weights,) * 8 + (vectors,) * 4,
        check_vma=False,
    )
```

```python
import functools

import jax
import jax.numpy as jnp
from jax import lax
from jax.experimental import pallas as pl
from jax.experimental.pallas import tpu as pltpu
from jax.sharding import PartitionSpec as P

HD = 64
PAIR = 2 * HD
STEP = 10
TILE = 256

EPSILON = 1e-05
CLIP_NORM = 1.0
BETA_ONE = 0.5
BETA_TWO = 0.5
MATRIX_RATE = 0.04
VECTOR_RATE = 0.3
WEIGHT_DECAY = 0.1
ADAM_EPSILON = 1e-08
SCORE_SCALE = 0.125
MASKED = -1000000000.0
AXES = ("dp", "chip", "core")
LOW = jnp.bfloat16
FULL = jnp.float32


def dot_nn(left, right):
    return lax.dot_general(left, right, (((1,), (0,)), ((), ())), preferred_element_type=FULL)


def dot_nt(left, right):
    return lax.dot_general(left, right, (((1,), (1,)), ((), ())), preferred_element_type=FULL)


def dot_tn(left, right):
    return lax.dot_general(left, right, (((0,), (0,)), ((), ())), preferred_element_type=FULL)


def lane_masks(rows):
    lane = lax.broadcasted_iota(jnp.int32, (rows, PAIR), 1)
    return (lane < HD, lane >= HD)


def forward_pair(queries, keys, values, causal, limit):
    seq = queries.shape[0]
    span = keys.shape[0]
    block = min(TILE, seq)
    masks = lane_masks(block)
    key_masks = lane_masks(span)
    counted = [jnp.where(mask, values, jnp.ones_like(values)) for mask in key_masks]

    def score(start):
        found = []
        for head in range(2):
            query = queries[start : start + block]
            query = jnp.where(masks[head], query, jnp.zeros_like(query)) * SCORE_SCALE
            if causal:
                row = lax.broadcasted_iota(jnp.int32, (block, block), 0)
                col = lax.broadcasted_iota(jnp.int32, (block, block), 1)
                parts = [(start, start + block, col <= row)]
                if start:
                    parts.append((0, start, None))
            else:
                col = lax.broadcasted_iota(jnp.int32, (block, span), 1)
                parts = [(0, span, col < limit)]
            scores = []
            for low, high, allowed in parts:
                value = dot_nt(query, keys[low:high])
                if allowed is not None:
                    value = jnp.where(allowed, value, MASKED)
                scores.append((low, high, value))
            found.append(scores)
        return found

    results = []
    ahead = score(0)
    for start in range(0, seq, block):
        found = ahead
        if start + block < seq:
            ahead = score(start + block)
        peaks, sums = [], []
        for head in range(2):
            peak = None
            for _, _, value in found[head]:
                most = jnp.max(value, axis=1, keepdims=True)
                peak = most if peak is None else jnp.maximum(peak, most)
            peaks.append(peak)
        for head in range(2):
            mixed = None
            for low, high, value in found[head]:
                weight = jnp.exp(value - peaks[head]).astype(LOW)
                part = dot_nn(weight, counted[head][low:high])
                mixed = part if mixed is None else mixed + part
            sums.append(mixed)
        mixed = jnp.where(masks[0], sums[0], sums[1])
        total = pltpu.roll(jnp.where(masks[0], sums[1], sums[0]), HD, 1)
        level = jnp.where(masks[0], peaks[0], peaks[1]) + jnp.log(total)
        results.append((start, start + block, (mixed / total).astype(LOW), level.T))
    return results


def backward_pair(queries, keys, values, mixed, upstream, levels, causal, limit):
    seq = queries.shape[0]
    span = keys.shape[0]
    block = min(TILE, span)
    masks = lane_masks(block)
    scaled = queries * SCORE_SCALE
    inner = (upstream.astype(FULL) * mixed.astype(FULL)).T
    products = [
        jnp.sum(inner[HD * head : HD * (head + 1)], axis=0, keepdims=True) for head in range(2)
    ]
    units = []
    for low in range(0, span, block):
        for head in range(2):
            if not causal:
                units.append((low, head, 0, seq, True))
                continue
            units.append((low, head, low, low + block, True))
            if low + block < seq:
                units.append((low, head, low + block, seq, False))

    def scores(unit):
        low, head, begin, end, checked = unit
        key, value = keys[low : low + block], values[low : low + block]
        key = jnp.where(masks[head], key, jnp.zeros_like(key))
        value = jnp.where(masks[head], value, jnp.zeros_like(value))
        return dot_nt(key, scaled[begin:end]), dot_nt(value, upstream[begin:end])

    def exponents(unit, score, grad_weight):
        low, head, begin, end, checked = unit
        if checked:
            row = lax.broadcasted_iota(jnp.int32, (block, end - begin), 0) + low
            if causal:
                col = lax.broadcasted_iota(jnp.int32, (block, end - begin), 1) + begin
                allowed = row <= col
            else:
                allowed = row < limit
            score = jnp.where(allowed, score, MASKED)
        weight = jnp.exp(score - levels[8 * head : 8 * head + 1, begin:end])
        grad_score = (weight * (grad_weight - products[head][:, begin:end])).astype(LOW)
        return weight.astype(LOW), grad_score

    grad_q = [[None] * (seq // block) for _ in range(2)]
    sums_k, sums_v = {}, {}

    def gather(unit, weight, grad_score):
        low, head, begin, end, _ = unit
        part_v = dot_nn(weight, upstream[begin:end])
        part_k = dot_nn(grad_score, scaled[begin:end])
        part_q = dot_tn(grad_score, keys[low : low + block])
        for sums, part in ((sums_k, part_k), (sums_v, part_v)):
            old = sums.get((low, head))
            sums[low, head] = part if old is None else old + part
        for at in range(begin, end, block):
            piece = part_q[at - begin : at - begin + block]
            old = grad_q[head][at // block]
            grad_q[head][at // block] = piece if old is None else old + piece

    ahead = scores(units[0])
    for number, unit in enumerate(units):
        found = ahead
        if number + 1 < len(units):
            ahead = scores(units[number + 1])
        gather(unit, *exponents(unit, *found))

    grad_k, grad_v, done_q = [], [], []
    for low in range(0, span, block):
        for sums, out in ((sums_k, grad_k), (sums_v, grad_v)):
            value = jnp.where(masks[0], sums[low, 0], sums[low, 1])
            out.append((low, low + block, value.astype(LOW)))
    for number, (one, two) in enumerate(zip(grad_q[0], grad_q[1])):
        value = (jnp.where(masks[0], one, two) * SCORE_SCALE).astype(LOW)
        done_q.append((number * block, (number + 1) * block, value))
    return done_q, grad_k, grad_v


def self_forward_kernel(qkv_ref, out_ref, level_ref):
    queries = qkv_ref[:, :PAIR]
    keys = qkv_ref[:, PAIR : 2 * PAIR]
    values = qkv_ref[:, 2 * PAIR :]
    for start, stop, out, level in forward_pair(queries, keys, values, True, None):
        out_ref[start:stop, :] = out
        level_ref[0, 0:8, start:stop] = level[0:8]
        level_ref[0, 8:16, start:stop] = level[HD : HD + 8]


def self_backward_kernel(qkv_ref, mixed_ref, upstream_ref, level_ref, *rest):
    grad_ref = rest[-1]
    queries = qkv_ref[:, :PAIR]
    keys = qkv_ref[:, PAIR : 2 * PAIR]
    values = qkv_ref[:, 2 * PAIR :]
    found = backward_pair(
        queries, keys, values, mixed_ref[...], upstream_ref[...], level_ref[0], True, None
    )
    for place, rows in enumerate(found):
        for start, stop, value in rows:
            grad_ref[start:stop, place * PAIR : (place + 1) * PAIR] = value


def cross_forward_kernel(limit_ref, query_ref, kv_ref, out_ref, level_ref):
    found = forward_pair(query_ref[...], kv_ref[:, :PAIR], kv_ref[:, PAIR:], False, limit_ref[0])
    for start, stop, out, level in found:
        out_ref[start:stop, :] = out
        level_ref[0, 0:8, start:stop] = level[0:8]
        level_ref[0, 8:16, start:stop] = level[HD : HD + 8]


def cross_backward_kernel(
    limit_ref, query_ref, kv_ref, mixed_ref, upstream_ref, level_ref, grad_q_ref, grad_kv_ref
):
    found = backward_pair(
        query_ref[...],
        kv_ref[:, :PAIR],
        kv_ref[:, PAIR:],
        mixed_ref[...],
        upstream_ref[...],
        level_ref[0],
        False,
        limit_ref[0],
    )
    for start, stop, value in found[0]:
        grad_q_ref[start:stop, :] = value
    for place, rows in enumerate(found[1:]):
        for start, stop, value in rows:
            grad_kv_ref[start:stop, place * PAIR : (place + 1) * PAIR] = value


LARGE = pltpu.CompilerParams(vmem_limit_bytes=56 * 1024 * 1024)
MIDDLE = pltpu.CompilerParams(vmem_limit_bytes=42 * 1024 * 1024)
PARAMS = pltpu.CompilerParams(vmem_limit_bytes=28 * 1024 * 1024)
SCALAR = pl.BlockSpec(memory_space=pltpu.SMEM)


def streamed(value):
    return pltpu.with_memory_space_constraint(value, pltpu.HBM)


def columns(rows, width, offset=0):
    return pl.BlockSpec((rows, width), lambda pair: (0, pair + offset))


def planes(seq):
    return pl.BlockSpec((1, 16, seq), lambda pair: (pair, 0, 0))


SHORT = pl.CostEstimate(flops=1, bytes_accessed=1, transcendentals=0)


def self_forward(qkv):
    seq, width = qkv.shape[0], qkv.shape[1] // 3
    pairs = width // PAIR
    return pl.pallas_call(
        self_forward_kernel,
        grid=(pairs,),
        in_specs=[columns(seq, 3 * PAIR)],
        out_specs=[columns(seq, PAIR), planes(seq)],
        out_shape=[
            jax.ShapeDtypeStruct((seq, width), LOW),
            jax.ShapeDtypeStruct((pairs, 16, seq), FULL),
        ],
        compiler_params=LARGE,
        cost_estimate=SHORT,
        name="self_forward",
    )(streamed(qkv))


def self_backward(qkv, mixed, upstream, levels, start, count, total=None, at=0, old=None):
    seq = qkv.shape[0]
    total = count if total is None else total
    old = [] if old is None else [old]
    return pl.pallas_call(
        self_backward_kernel,
        grid=(count,),
        in_specs=[
            columns(seq, 3 * PAIR, start),
            columns(seq, PAIR, start),
            columns(seq, PAIR, start),
            pl.BlockSpec((1, 16, seq), lambda pair: (pair + start, 0, 0)),
        ]
        + [pl.BlockSpec(memory_space=pl.ANY)] * len(old),
        out_specs=columns(seq, 3 * PAIR, at),
        out_shape=jax.ShapeDtypeStruct((seq, 3 * PAIR * total), LOW),
        input_output_aliases={4: 0} if old else {},
        compiler_params=PARAMS,
        cost_estimate=SHORT,
        name="self_backward",
    )(streamed(qkv), streamed(mixed), upstream, levels, *old)


def cross_forward(limit, queries, pair_states):
    seq, width = queries.shape
    span = pair_states.shape[0]
    pairs = width // PAIR
    return pl.pallas_call(
        cross_forward_kernel,
        grid=(pairs,),
        in_specs=[SCALAR, columns(seq, PAIR), columns(span, 2 * PAIR)],
        out_specs=[columns(seq, PAIR), planes(seq)],
        out_shape=[
            jax.ShapeDtypeStruct((seq, width), LOW),
            jax.ShapeDtypeStruct((pairs, 16, seq), FULL),
        ],
        compiler_params=PARAMS,
        cost_estimate=SHORT,
        name="cross_forward",
    )(limit, queries, pair_states)


def cross_backward(limit, queries, pair_states, mixed, upstream, levels):
    seq, width = queries.shape
    span = pair_states.shape[0]
    pairs = width // PAIR
    return pl.pallas_call(
        cross_backward_kernel,
        grid=(pairs,),
        in_specs=[
            SCALAR,
            columns(seq, PAIR),
            columns(span, 2 * PAIR),
            columns(seq, PAIR),
            columns(seq, PAIR),
            planes(seq),
        ],
        out_specs=[columns(seq, PAIR), columns(span, 2 * PAIR)],
        out_shape=[
            jax.ShapeDtypeStruct((seq, width), LOW),
            jax.ShapeDtypeStruct((span, 2 * width), LOW),
        ],
        compiler_params=PARAMS,
        cost_estimate=SHORT,
        name="cross_backward",
    )(limit, queries, pair_states, mixed, upstream, levels)


def mlp_kernel(order, core_ref, rows_ref, grad_ref, up_ref, down_ref, *rest):
    del core_ref
    count = 2 + max(piece for _, _, piece, _ in order) * 2
    halves_refs, rest = rest[-4 - count : -4], rest[-4:]
    out_ref, back_ref, rows_turned_ref, grad_turned_ref = rest
    step = pl.program_id(0)

    @pl.when(step == 0)
    def _():
        rows_turned_ref[...] = rows_ref[...].T
        grad_turned_ref[...] = grad_ref[...].T
        back_ref[...] = jnp.zeros_like(back_ref)

    seq = rows_ref.shape[0]
    size = min(512, seq)
    width = up_ref.shape[1]

    def ahead(start):
        rows = slice(start, start + size)
        return dot_nn(rows_ref[rows, :], up_ref[...]), dot_nn(grad_ref[rows, :], down_ref[...])

    down_grad, up_grad = None, None
    found = ahead(0)
    for start in range(0, seq, size):
        hidden, grad = found
        if start + size < seq:
            found = ahead(start + size)
        rows = slice(start, start + size)
        share = 0.5 + 0.5 * lax.erf(hidden * 0.7071067811865476)
        bell = jnp.exp(hidden * hidden * -0.5)
        active = (hidden * share).astype(LOW)
        grad_hidden = (grad * (share + hidden * (bell * 0.3989422804014327))).astype(LOW)
        out_ref[rows, :] = active
        down_part = dot_nn(grad_turned_ref[:, rows], active)
        up_part = dot_nn(rows_turned_ref[:, rows], grad_hidden)
        back_ref[rows, :] += dot_nt(grad_hidden, up_ref[...])
        down_grad = down_part if start == 0 else down_grad + down_part
        up_grad = up_part if start == 0 else up_grad + up_part

    for number, half_ref in enumerate(halves_refs):
        steps = [
            at for at, (_, side, piece, _) in enumerate(order) if 2 * piece + 1 - side == number
        ]

        @pl.when((step >= steps[0]) & (step <= steps[-1]))
        def _(half_ref=half_ref):
            half_ref[:, :width] = down_grad.astype(LOW)
            half_ref[:, width:] = up_grad.astype(LOW)


def mlp(core, rows, grad, weights, up_at, down_at, order, old=None):
    seq, width = rows.shape
    block = width // 2
    pieces = 1 + max(piece for _, _, piece, _ in order)

    def chosen(j, values):
        found = values[0]
        for number, value in enumerate(values[1:], 1):
            found = jnp.where(j == number, value, found)
        return found

    def place(j, core):
        quarter = chosen(j, [quarter for quarter, _, _, _ in order])
        return 2 * quarter + (core[0] ^ chosen(j, [side for _, side, _, _ in order]))

    def strip(start):
        return pl.BlockSpec((width, block), lambda j, core: (0, start // block + place(j, core)))

    once = pl.Buffered(1)

    def strips(number):
        mine = [at for at, (_, side, piece, _) in enumerate(order) if 2 * piece + 1 - side == number]
        places = [order[min(max(at, mine[0]), mine[-1])][3] for at in range(len(order))]
        return pl.BlockSpec(
            (width, width), lambda j, core: (0, chosen(j, places)), pipeline_mode=once
        )

    old = [] if old is None else list(old)
    whole = pl.BlockSpec((seq, width), lambda j, core: (0, 0), pipeline_mode=once)
    return pl.pallas_call(
        functools.partial(mlp_kernel, order),
        grid_spec=pltpu.PrefetchScalarGridSpec(
            num_scalar_prefetch=1,
            grid=(len(order),),
            in_specs=[whole, whole, strip(up_at), strip(down_at)]
            + [pl.BlockSpec(memory_space=pl.ANY)] * len(old),
            out_specs=[strips(number) for number in range(2 * pieces)]
            + [pl.BlockSpec((seq, block), lambda j, core: (0, place(j, core))), whole],
            scratch_shapes=[pltpu.VMEM((width, seq), LOW)] * 2,
        ),
        out_shape=[jax.ShapeDtypeStruct((width, 2 * width), LOW)] * (2 * pieces)
        + [
            jax.ShapeDtypeStruct((seq, len(order) * block), LOW),
            jax.ShapeDtypeStruct((seq, width), FULL),
        ],
        input_output_aliases={5: 0, 6: 1} if old else {},
        compiler_params=MIDDLE,
        cost_estimate=SHORT,
        name="mlp",
    )(core, rows, grad, weights, weights, *old)


def matmul_kernel(left_ref, right_ref, out_ref):
    out_ref[...] = dot_nn(left_ref[...], right_ref[...]).astype(LOW)


def matmul(left, right, at, count):
    seq, depth = left.shape
    block = min(512, count)
    return pl.pallas_call(
        matmul_kernel,
        grid=(count // block,),
        in_specs=[
            pl.BlockSpec((seq, depth), lambda step: (0, 0)),
            pl.BlockSpec((depth, block), lambda step: (0, at // block + step)),
        ],
        out_specs=pl.BlockSpec((seq, block), lambda step: (0, step)),
        out_shape=jax.ShapeDtypeStruct((seq, count), LOW),
        compiler_params=PARAMS,
        cost_estimate=SHORT,
        name="matmul",
    )(left, right)


def turned_kernel(left_ref, right_ref, out_ref):
    out_ref[...] = dot_nt(left_ref[...], right_ref[...])


def matmul_turned(left, right, at):
    seq, depth = left.shape
    width = right.shape[0]
    block = min(512, width)
    return pl.pallas_call(
        turned_kernel,
        grid=(width // block,),
        in_specs=[
            pl.BlockSpec((seq, depth), lambda step: (0, 0)),
            pl.BlockSpec((block, depth), lambda step: (step, at // depth)),
        ],
        out_specs=pl.BlockSpec((seq, block), lambda step: (0, step)),
        out_shape=jax.ShapeDtypeStruct((seq, width), FULL),
        compiler_params=PARAMS,
        cost_estimate=SHORT,
        name="matmul_turned",
    )(left, right)


def product_kernel(core_ref, left_ref, sent_ref, kept_ref, *rest):
    del core_ref
    send_ref, keep_ref, turned_ref = rest[-3:]

    @pl.when(pl.program_id(0) == 0)
    def _():
        turned_ref[...] = left_ref[...].T

    send_ref[...] = dot_nn(turned_ref[...], sent_ref[...]).astype(LOW)
    keep_ref[...] = dot_nn(turned_ref[...], kept_ref[...]).astype(LOW)


def product(core, left, right, total=None, at=0, old=None):
    rows, width = left.shape
    half = right.shape[1] // 2
    block = max(b for b in (128, 256, 384, 512) if half % b == 0 and at % b == 0)
    steps, offset = half // block, at // block
    total = half if total is None else total
    old = [] if old is None else list(old)
    return pl.pallas_call(
        product_kernel,
        grid_spec=pltpu.PrefetchScalarGridSpec(
            num_scalar_prefetch=1,
            grid=(steps,),
            in_specs=[
                pl.BlockSpec((rows, width), lambda j, core: (0, 0)),
                pl.BlockSpec((rows, block), lambda j, core: (0, (1 - core[0]) * steps + j)),
                pl.BlockSpec((rows, block), lambda j, core: (0, core[0] * steps + j)),
            ]
            + [pl.BlockSpec(memory_space=pl.ANY)] * len(old),
            out_specs=[pl.BlockSpec((width, block), lambda j, core: (0, offset + j))] * 2,
            scratch_shapes=[pltpu.VMEM((width, rows), LOW)],
        ),
        out_shape=[jax.ShapeDtypeStruct((width, total), LOW)] * 2,
        input_output_aliases={4: 0, 5: 1} if old else {},
        compiler_params=PARAMS,
        cost_estimate=SHORT,
        name="product",
    )(core, streamed(left), right, right, *old)


def pack_kernel(attn_ref, mlp_ref, norm_ref, out_ref, rest_ref):
    width = attn_ref.shape[2]
    hidden = mlp_ref.shape[2]
    quarter = hidden // 4
    for pair in range(width // PAIR):
        source = slice(pair * PAIR, (pair + 1) * PAIR)
        for kind in range(3):
            place = (3 * pair + kind) * PAIR
            out_ref[:, place : place + PAIR] = attn_ref[kind, :, source].astype(LOW)
        for kind in range(2):
            place = 5 * width + (2 * pair + kind) * PAIR
            out_ref[:, place : place + PAIR] = attn_ref[5 + kind, :, source].astype(LOW)
    out_ref[:, 3 * width : 4 * width] = attn_ref[3].astype(LOW)
    out_ref[:, 4 * width : 5 * width] = attn_ref[4].astype(LOW)
    out_ref[:, 7 * width : 8 * width] = attn_ref[7].astype(LOW)
    for kind in range(2):
        place = 8 * width + kind * quarter
        out_ref[:, place : place + quarter] = mlp_ref[kind, :, :quarter].astype(LOW)
        place = kind * 3 * quarter
        rest_ref[:, place : place + 3 * quarter] = mlp_ref[kind, :, quarter:].astype(LOW)
    out_ref[:, 8 * width + 2 * quarter :] = norm_ref[...].astype(LOW)


def pack(attn_master, mlp_master, norm_columns):
    _, rows, width = attn_master.shape
    hidden = mlp_master.shape[2]
    return pl.pallas_call(
        pack_kernel,
        out_shape=[
            jax.ShapeDtypeStruct((rows, 8 * width + hidden // 2 + norm_columns.shape[1]), LOW),
            jax.ShapeDtypeStruct((rows, 3 * hidden // 2), LOW),
        ],
        compiler_params=PARAMS,
        cost_estimate=SHORT,
        name="pack",
    )(attn_master, mlp_master, norm_columns)


class Grid:
    def __init__(self, sizes):
        self.outer, self.chips = sizes
        self.inner = 2 * self.chips
        self.count = self.outer * self.inner
        self.bits = (self.count - 1).bit_length()
        self.core = lax.axis_index("core")
        self.me = lax.axis_index(AXES)
        self.plane = lax.axis_index("dp")
        near = ((self.chips - 1).bit_length() + 1) // 2
        self.x = list(range(near, 0, -1))
        self.y = list(range((self.chips - 1).bit_length(), near, -1))

    def own(self, bit):
        return lax.shift_right_logical(self.me, jnp.int32(bit)) & 1

    def turn(self, value, mask):
        return lax.ppermute(value, AXES, [(i, i ^ mask) for i in range(self.count)])

    def add_all(self, value):
        low = 1
        for size in (2, self.chips, self.outer):
            found = [value] + [self.turn(value, step * low) for step in range(1, size)]
            place = (self.me // low) % size
            if size > 2:
                stack = jnp.stack(found)
                found = [self.pick(stack, place ^ step) for step in range(size)]
            value = sum(found[1:], found[0])
            low *= size
        return value

    def pick(self, stack, index):
        return lax.dynamic_index_in_dim(stack, index, 0, keepdims=False)

    def unpair(self, total):
        total = total.reshape(2, total.shape[0] // 2, total.shape[1])
        mine = lax.dynamic_index_in_dim(total, self.core, 0, keepdims=False)
        other = lax.dynamic_index_in_dim(total, 1 - self.core, 0, keepdims=False)
        return mine, self.turn(other, 1)


def add_kernel(counts, side_ref, *refs):
    del side_ref
    outs = refs[sum(counts) :]
    at = 0
    for count, out_ref in zip(counts, outs):
        total = refs[at][...].reshape(out_ref.shape).astype(FULL)
        for ref in refs[at + 1 : at + count]:
            total = total + ref[...].reshape(out_ref.shape).astype(FULL)
        out_ref[...] = total.astype(LOW)
        at += count


def layer_kernel(outer, steps, first, one, two, side_ref, *refs):
    ins, outs = refs[: first + one + two], refs[first + one + two :]

    def fill(parts):
        for step in range(outer):
            plane = side_ref[0] ^ step
            out_ref = outs[step]
            total = parts[0][plane].reshape(out_ref.shape).astype(FULL)
            for part in parts[1:]:
                total = total + part[plane].reshape(out_ref.shape).astype(FULL)
            out_ref[...] = total.astype(out_ref.dtype)

    @pl.when(pl.program_id(0) < steps)
    def _():
        fill(ins[:first] + ins[first : first + one])

    @pl.when(pl.program_id(0) >= steps)
    def _():
        fill(ins[:first] + ins[first + one :])


def plane_kernel(steps, first, one, two, side_ref, *refs):
    del side_ref
    ins, out_ref = refs[:-1], refs[-1]

    def fill(parts):
        total = parts[0][...].reshape(out_ref.shape).astype(FULL)
        for part in parts[1:]:
            total = total + part[...].reshape(out_ref.shape).astype(FULL)
        out_ref[...] = total.astype(LOW)

    @pl.when(pl.program_id(0) < steps)
    def _():
        fill(ins[:first] + ins[first : first + one])

    @pl.when(pl.program_id(0) >= steps)
    def _():
        fill(ins[:first] + ins[first + one :])


class Sum:
    def __init__(self, grid, keep, got):
        self.grid = grid
        self.bits = sorted(grid.x + grid.y, reverse=True)
        self.cut = keep.shape[1] // 2
        self.block = max(b for b in (128, 256, 384, 512, 640) if self.cut % b == 0)
        self.steps = self.cut // self.block
        self.base = [(keep, []), (got, [])]
        self.orders = [grid.x + grid.y, grid.y + grid.x]
        self.extra = [[], []]
        self.stages = len(self.bits)
        sides = [grid.plane] + [grid.own(bit) for bit in self.bits]
        self.sides = jnp.stack(sides).astype(jnp.int32)

    def view(self, term):
        value, done = term
        left = [bit for bit in self.bits if bit not in done]
        outer = self.grid.outer
        share = value.shape[0] // (outer << len(left))
        return value.reshape([outer] + [2] * len(left) + [share, value.shape[1]]), left

    def spec(self, view, left, flips, column):
        places = {bit: 1 + self.bits.index(bit) for bit in flips}

        def index(j, side):
            picks = [
                (side[places[bit]] ^ flips[bit]) if bit in flips else 0 for bit in left
            ]
            return (0, *picks, 0, column(j))

        shape = [view.shape[0]] + [1 if bit in flips else 2 for bit in left]
        return pl.BlockSpec((*shape, view.shape[-2], self.block), index)

    def call(self, kernel, grid, views, specs, out_specs, out_shape, name):
        return pl.pallas_call(
            kernel,
            grid_spec=pltpu.PrefetchScalarGridSpec(
                num_scalar_prefetch=1, grid=grid, in_specs=specs, out_specs=out_specs
            ),
            out_shape=out_shape,
            compiler_params=PARAMS,
            cost_estimate=SHORT,
            name=name,
        )(self.sides, *(streamed(view) for view in views))

    def send(self, stage):
        views, specs, counts = [], [], []
        for half, order in enumerate(self.orders):
            flips = {bit: 0 for bit in order[:stage]}
            flips[order[stage]] = 1
            terms = self.base + self.extra[half]
            counts.append(len(terms))
            for number, term in enumerate(terms):
                view, left = self.view(term)
                shift = half * self.steps if number < len(self.base) else 0
                views.append(view)
                picked = {bit: flip for bit, flip in flips.items() if bit in left}
                specs.append(self.spec(view, left, picked, lambda j, shift=shift: shift + j))
        rows = self.base[0][0].shape[0] >> (stage + 1)
        return self.call(
            functools.partial(add_kernel, counts),
            (self.steps,),
            views,
            specs,
            [pl.BlockSpec((rows, self.block), lambda j, side: (0, j))] * 2,
            [jax.ShapeDtypeStruct((rows, self.cut), LOW)] * 2,
            "add",
        )

    def swap(self, stage, out):
        return [self.grid.turn(v, 1 << order[stage]) for order, v in zip(self.orders, out)]

    def receive(self, stage, got):
        for half, value in enumerate(got):
            self.extra[half].append((value, self.orders[half][: stage + 1]))

    def between(self, main):
        for stage in range(1, self.stages - 1):
            main, sent = tie((main, self.send(stage)))
            main, got = tie((main, self.swap(stage, sent)))
            self.receive(stage, got)
        return main

    def layers(self):
        views, specs, counts = self.columns()
        outer = self.grid.outer
        share = views[0].shape[-2]
        shape = (share, 2 * self.cut)
        return self.call(
            functools.partial(layer_kernel, outer, self.steps, *counts),
            (2 * self.steps,),
            views,
            specs,
            [pl.BlockSpec((share, self.block), lambda j, side: (0, j))] * outer,
            [jax.ShapeDtypeStruct(shape, FULL)] + [jax.ShapeDtypeStruct(shape, LOW)] * (outer - 1),
            "layers",
        )

    def planes(self):
        views, specs, counts = self.columns()
        rows = views[0].shape[0] * views[0].shape[-2]
        value = self.call(
            functools.partial(plane_kernel, self.steps, *counts),
            (2 * self.steps,),
            views,
            specs,
            pl.BlockSpec((rows, self.block), lambda j, side: (0, j)),
            jax.ShapeDtypeStruct((rows, 2 * self.cut), LOW),
            "planes",
        )
        return value

    def columns(self):
        views, specs = [], []
        steps = self.steps
        groups = (
            (self.base, lambda j: j),
            (self.extra[0], lambda j: jnp.minimum(j, steps - 1)),
            (self.extra[1], lambda j: jnp.maximum(j - steps, 0)),
        )
        for terms, column in groups:
            for term in terms:
                view, left = self.view(term)
                views.append(view)
                specs.append(self.spec(view, left, {bit: 0 for bit in left}, column))
        return views, specs, [len(terms) for terms, _ in groups]

    def turn_layers(self, layers, steps=None):
        grid = self.grid
        found = [
            grid.turn(layers[step], step * grid.inner) for step in steps or range(1, grid.outer)
        ]
        return found if steps else [layers[0]] + found

    def finish(self, got):
        return sum((value.astype(FULL) for value in got[1:]), got[0])


def norm_forward(rows, gain, bias):
    centre = jnp.mean(rows, axis=-1, keepdims=True)
    centred = rows - centre
    spread = jnp.mean(centred * centred, axis=-1, keepdims=True)
    scale = lax.rsqrt(spread + EPSILON)
    return (centred * scale * gain + bias).astype(LOW)


def norm_backward_kernel(count, rows_ref, gain_ref, base_ref, *rest):
    grad_refs, out_ref, rest = rest[:count], rest[count], rest[count + 1 :]
    sums_ref = rest[-1]
    rows = rows_ref[...].astype(FULL)
    centred = rows - jnp.mean(rows, axis=1, keepdims=True)
    spread = jnp.mean(centred * centred, axis=1, keepdims=True)
    scale = lax.rsqrt(spread + EPSILON)
    plain = centred * scale
    grad = grad_refs[0][...]
    for ref in grad_refs[1:]:
        grad = grad + ref[...]
    weighted = grad * gain_ref[...]
    mean_one = jnp.mean(weighted, axis=1, keepdims=True)
    mean_two = jnp.mean(weighted * plain, axis=1, keepdims=True)
    total = base_ref[...].astype(FULL) + scale * (weighted - mean_one - plain * mean_two)
    out_ref[...] = total
    if len(rest) > 1:
        rest[0][...] = total.astype(LOW)

    @pl.when(pl.program_id(0) == 0)
    def _():
        sums_ref[...] = jnp.zeros_like(sums_ref)

    sums_ref[0:1, :] += jnp.sum(grad * plain, axis=0, keepdims=True)
    sums_ref[1:2, :] += jnp.sum(grad, axis=0, keepdims=True)


def norm_backward(rows, gain, grads, base, rounded=True):
    seq, width = rows.shape
    block = pl.BlockSpec((min(TILE, seq), width), lambda step: (step, 0))
    more = [jax.ShapeDtypeStruct((seq, width), LOW)] if rounded else []
    out = pl.pallas_call(
        functools.partial(norm_backward_kernel, len(grads)),
        grid=(max(1, seq // TILE),),
        in_specs=[block, pl.BlockSpec((1, width), lambda step: (0, 0)), block]
        + [block] * len(grads),
        out_specs=[block] * (1 + len(more)) + [pl.BlockSpec((8, width), lambda step: (0, 0))],
        out_shape=[jax.ShapeDtypeStruct((seq, width), FULL)]
        + more
        + [jax.ShapeDtypeStruct((8, width), FULL)],
        compiler_params=PARAMS,
        cost_estimate=SHORT,
        name="norm_backward",
    )(streamed(rows), gain.reshape(1, width), streamed(base), *(map(streamed, grads) if len(grads) > 1 else grads))
    return *out[:-1], out[-1][:2]


def adam_update(master, first, second, gradient, factor, rate, decay):
    gradient = gradient * factor
    first_new = BETA_ONE * first + (1.0 - BETA_ONE) * gradient
    second_new = BETA_TWO * second + (1.0 - BETA_TWO) * gradient * gradient
    first_fix = 1.0 - BETA_ONE**STEP
    second_fix = 1.0 - BETA_TWO**STEP
    update = first_new / first_fix / (jnp.sqrt(second_new / second_fix) + ADAM_EPSILON)
    master_new = master - rate * (update + decay * master)
    return (first_new, second_new, master_new, master_new.astype(LOW))


def adam_places(width, hidden):
    pairs = width // PAIR
    cut, half = pairs // 2, width // 2
    places = []
    for side in range(2):
        block = hidden // 8
        for piece, part in ((0, 0), (0, 1), (1, 0), (1, 1)):
            number = 4 * piece + 2 * part + side
            for kind in range(2):
                start = (2 * part + kind) * block
                places.append((1, 1 - kind, number * block, piece, start, side, block))
        for piece, first, count in ((3, 0, cut), (4, cut, pairs - cut)):
            for pair in range(count // 2):
                column = (first + side * (count // 2) + pair) * PAIR
                for kind in range(3):
                    places.append((0, kind, column, piece, (3 * pair + kind) * PAIR, side, PAIR))
        places.append((0, 3, side * half, 3, 3 * PAIR * cut // 2, side, half))
        places.append((0, 4, side * half, 2, half, side, half))
        for pair in range(pairs // 2):
            column = (side * (pairs // 2) + pair) * PAIR
            for kind in range(2):
                start = width + (2 * pair + kind) * PAIR
                places.append((0, 5 + kind, column, 2, start, side, PAIR))
        places.append((0, 7, side * half, 2, 0, side, half))
    return places


def adam_kernel(places, factor_ref, core_ref, *refs):
    grads, olds, news = refs[:10], refs[10:16], refs[16:]
    factor = factor_ref[0]
    core = core_ref[0]
    for into, matrix, column, piece, start, side, size in places:
        mine, other = (ref[:, start : start + size] for ref in grads[2 * piece : 2 * piece + 2])
        gradient = jnp.where(core == side, mine, other)
        old = [ref[matrix, :, column : column + size] for ref in olds[3 * into : 3 * into + 3]]
        new = adam_update(*old, gradient, factor, MATRIX_RATE, WEIGHT_DECAY)
        for ref, value in zip(news[4 * into : 4 * into + 4], new):
            ref[matrix, :, column : column + size] = value


def adam(factor, core, pieces, attn, mlp):
    width, hidden = attn[0].shape[2], mlp[0].shape[2]
    shapes = []
    for group in (attn, mlp):
        shape = group[0].shape
        shapes += [jax.ShapeDtypeStruct(shape, FULL)] * 3 + [jax.ShapeDtypeStruct(shape, LOW)]
    operands = [value for pair in pieces for value in pair] + list(attn) + list(mlp)
    def whole(value):
        return pl.BlockSpec(value.shape, lambda step: (0,) * len(value.shape))

    out = pl.pallas_call(
        functools.partial(adam_kernel, adam_places(width, hidden)),
        grid=(1,),
        in_specs=[SCALAR, SCALAR] + [whole(value) for value in operands],
        out_specs=[whole(value) for value in shapes],
        out_shape=shapes,
        compiler_params=LARGE,
        cost_estimate=SHORT,
        name="adam",
    )(factor.reshape(1), core, *operands)
    return out[:4], out[4:]


def tie(values):
    return lax.optimization_barrier(values)


def local(
    sizes,
    tokens,
    prompt,
    prompt_len,
    cotangent,
    attn_master,
    attn_first,
    attn_second,
    mlp_master,
    mlp_first,
    mlp_second,
    norm_master,
    norm_first,
    norm_second,
):
    grid = Grid(sizes)
    _, seq, width = tokens.shape
    own_rows = attn_master.shape[1]
    hidden = mlp_master.shape[2]
    norm_columns = jnp.pad(norm_master.T, ((0, 0), (0, PAIR - norm_master.shape[0])))
    shard, rest_shard = pack(attn_master, mlp_master, norm_columns)
    weights = lax.all_gather(shard, AXES, axis=0, tiled=True)
    rest_w = lax.all_gather(rest_shard, AXES, axis=0, tiled=True)
    grad_out = cotangent[0]
    up_at, quarter = 8 * width, hidden // 4
    gains = weights[:, up_at + 2 * quarter :].T[: norm_master.shape[0]].astype(FULL)
    out_w, cq_w, ckv_w, cout_w = (
        weights[:, low * width : high * width] for low, high in ((3, 4), (4, 5), (5, 7), (7, 8))
    )

    inputs = tokens[0].astype(FULL)
    normed_one = norm_forward(inputs, gains[0], gains[1])
    qkv = matmul(normed_one, weights, 0, 3 * width)
    mixed, levels = self_forward(qkv)
    after_self = inputs + dot_nn(mixed, out_w)
    normed_two = norm_forward(after_self, gains[2], gains[3])
    cross_q = dot_nn(normed_two, cq_w).astype(LOW)
    states = prompt[0]
    cross_kv = dot_nn(states, ckv_w).astype(LOW)
    crossed, cross_levels = cross_forward(prompt_len, cross_q, cross_kv)
    after_cross = after_self + dot_nn(crossed, cout_w)
    normed_three = norm_forward(after_cross, gains[4], gains[5])

    core = grid.core.astype(jnp.int32).reshape(1)
    half = width // 2
    pairs = width // PAIR
    def across(value):
        return lax.psum_scatter(value, "dp", scatter_dimension=0, tiled=True)

    *one_halves, active_one, back_one = mlp(
        core,
        normed_three,
        grad_out,
        weights,
        up_at,
        up_at + quarter,
        ((0, 0, 0, 0), (0, 1, 0, 0)),
    )
    normed_three, one_halves, rest_w = tie((normed_three, one_halves, rest_w))
    *halves, active_two, back_two = mlp(
        core,
        normed_three,
        grad_out,
        rest_w,
        0,
        3 * quarter,
        ((0, 0, 0, 1), (0, 1, 0, 1), (1, 0, 1, 0), (2, 0, 1, 1), (1, 1, 1, 0), (2, 1, 1, 1)),
        one_halves,
    )
    one_halves, two_halves = halves[:2], halves[2:]
    grads, one_halves, two_halves = tie(((back_one, back_two), one_halves, two_halves))

    one_got = grid.turn(one_halves[0], 1)
    grad_after_cross, branch, norm_three = norm_backward(after_cross, gains[4], grads, grad_out)
    cross_halves = product(core, crossed, branch, 2 * width, 0)
    grad_crossed = dot_nt(branch, cout_w).astype(LOW)
    grad_crossed, one_got, cross_halves = tie((grad_crossed, one_got, cross_halves))
    one_sum = Sum(grid, one_halves[1], one_got)
    last = one_sum.stages - 1
    sent = one_sum.send(0)
    grad_crossed, sent, two_halves = tie((grad_crossed, sent, two_halves))

    one_got, two_got = one_sum.swap(0, sent), grid.turn(two_halves[0], 1)
    grad_cq, grad_ckv = cross_backward(
        prompt_len, cross_q, cross_kv, crossed, grad_crossed, cross_levels
    )
    cross_halves = product(core, normed_two, grad_cq, 2 * width, half, cross_halves)
    cross_halves = product(core, states, grad_ckv, 2 * width, width, cross_halves)
    grad_cq, cross_halves, two_got = tie((grad_cq, cross_halves, two_got))

    grad_normed = matmul_turned(grad_cq, weights, 4 * width)
    grad_after_self, branch, norm_two = norm_backward(
        after_self, gains[2], [grad_normed], grad_after_cross
    )
    branch, one_got, cross_halves = tie((branch, one_got, cross_halves))
    one_sum.receive(0, one_got)
    branch = one_sum.between(branch)
    two_sum = Sum(grid, two_halves[1], two_got)
    sent, begun = one_sum.send(last), two_sum.send(0)
    branch, sent, begun = tie((branch, sent, begun))

    cross_got = grid.turn(cross_halves[0], 1)
    one_got, two_got = one_sum.swap(last, sent), two_sum.swap(0, begun)
    cut = pairs // 2
    part_width = 3 * PAIR * cut // 2
    front_width = half + part_width
    front_halves = product(core, mixed, branch, front_width, part_width)
    grad_mixed = dot_nt(branch, out_w).astype(LOW)
    grad_front = self_backward(qkv, mixed, grad_mixed, levels, 0, cut)
    front_halves = product(core, normed_one, grad_front, front_width, 0, front_halves)
    grad_mixed, grad_front, one_got, two_got, front_halves, cross_got = tie(
        (grad_mixed, grad_front, one_got, two_got, front_halves, cross_got)
    )
    two_sum.receive(0, two_got)
    grad_mixed = two_sum.between(grad_mixed)
    sent = two_sum.send(last)
    grad_mixed, grad_front, sent, one_got, cross_got = tie(
        (grad_mixed, grad_front, sent, one_got, cross_got)
    )

    two_got, front_got = two_sum.swap(last, sent), grid.turn(front_halves[0], 1)
    one_sum.receive(last, one_got)
    one_total = one_sum.planes()
    cross_sum = Sum(grid, cross_halves[1], cross_got)
    begun = cross_sum.send(0)
    split = 3 * PAIR * cut
    grad_normed = dot_nt(grad_front, weights[:, :split])
    grad_mixed, grad_normed, two_got, front_got, begun, one_total = tie(
        (grad_mixed, grad_normed, two_got, front_got, begun, one_total)
    )

    one_total = across(one_total)
    cross_got = cross_sum.swap(0, begun)
    two_sum.receive(last, two_got)
    two_total = two_sum.planes()
    some = (pairs - cut) // 2
    grad_back = self_backward(qkv, mixed, grad_mixed, levels, cut, some, pairs - cut)
    grad_mixed, grad_back, two_total = tie((grad_mixed, grad_back, two_total))
    grad_back = self_backward(
        qkv, mixed, grad_mixed, levels, cut + some, pairs - cut - some, pairs - cut, some, grad_back
    )
    grad_back, one_total, two_total = tie((grad_back, one_total, two_total))

    two_total = across(two_total)
    back_halves = product(core, normed_one, grad_back)
    grad_back, back_halves, cross_got = tie((grad_back, back_halves, cross_got))
    cross_sum.receive(0, cross_got)
    grad_back = cross_sum.between(grad_back)
    sent = cross_sum.send(last)
    grad_back, sent, grad_ckv, active_one, front_got = tie(
        (grad_back, sent, grad_ckv, active_one, front_got)
    )

    cross_got, back_got = cross_sum.swap(last, sent), grid.turn(back_halves[0], 1)
    front_sum = Sum(grid, front_halves[1], front_got)
    begun = front_sum.send(0)
    grad_normed = grad_normed + dot_nt(grad_back, weights[:, split : 3 * width])
    prompt_grad = dot_nt(grad_ckv, ckv_w)[None]
    grad_normed, prompt_grad, cross_got, back_got, two_total, begun = tie(
        (grad_normed, prompt_grad, cross_got, back_got, two_total, begun)
    )

    front_got = front_sum.swap(0, begun)
    token_grad, norm_one = norm_backward(
        tokens[0], gains[0], [grad_normed], grad_after_self, False
    )
    token_grad, cross_got = tie((token_grad[None], cross_got))
    cross_sum.receive(last, cross_got)
    cross_total = cross_sum.planes()
    down_at = up_at + quarter
    output = after_cross + dot_nt(active_one, weights[:, down_at : down_at + quarter])
    token_grad, output, front_got, cross_total = tie((token_grad, output, front_got, cross_total))
    cross_total = across(cross_total)
    front_sum.receive(0, front_got)
    token_grad = front_sum.between(token_grad)
    back_sum = Sum(grid, back_halves[1], back_got)
    sent, begun = front_sum.send(last), back_sum.send(0)
    output, sent, begun, active_two = tie((output, sent, begun, active_two))

    front_got, back_got = front_sum.swap(last, sent), back_sum.swap(0, begun)
    output = output + dot_nt(active_two[:, : 2 * quarter], rest_w[:, 3 * quarter : 5 * quarter])
    output, front_got, back_got, cross_total = tie((output, front_got, back_got, cross_total))
    front_sum.receive(last, front_got)
    back_sum.receive(0, back_got)
    output = back_sum.between(output)
    layers, sent = front_sum.layers(), back_sum.send(last)
    output, active_two, layers, sent = tie((output, active_two, layers, sent))

    front_layers, got = front_sum.turn_layers(layers), back_sum.swap(last, sent)
    output = output + dot_nt(active_two[:, 2 * quarter :], rest_w[:, 5 * quarter :])
    output = output.astype(LOW)[None]
    output, got = tie((output, got))
    back_sum.receive(last, got)
    layers = back_sum.layers()
    one_total, two_total, layers = tie((one_total, two_total, layers))

    back_layers = back_sum.turn_layers(layers)
    totals = [total.astype(FULL) for total in (one_total, two_total, cross_total)]
    totals.append(front_sum.finish(front_layers))
    squares = sum(jnp.sum(total * total) for total in totals)
    squares, back_layers = tie((squares, back_layers))
    totals.append(back_sum.finish(back_layers))
    squares = squares + jnp.sum(totals[-1] * totals[-1])

    norm_stack = jnp.concatenate([norm_one, norm_two, norm_three])
    payload = jnp.concatenate([norm_stack, jnp.full((2, width), squares, FULL)])
    payload = grid.add_all(payload)
    norm_grads = payload[:-2]
    grad_norm = jnp.sqrt(payload[-1, 0] + jnp.sum(norm_grads * norm_grads))
    norm_grads = lax.dynamic_slice_in_dim(norm_grads, grid.me * own_rows, own_rows, 1)
    factor = CLIP_NORM / jnp.maximum(grad_norm, CLIP_NORM)
    attn_out, mlp_out = adam(
        factor,
        core,
        [grid.unpair(total) for total in totals],
        (attn_master, attn_first, attn_second),
        (mlp_master, mlp_first, mlp_second),
    )
    norm_out = adam_update(
        norm_master, norm_first, norm_second, norm_grads, factor, VECTOR_RATE, 0.0
    )
    return (output, token_grad, prompt_grad, grad_norm, *attn_out, *mlp_out, *norm_out)


def solution(mesh):
    outer, inner = mesh.shape["dp"], mesh.shape["fsdp"]
    fine = jax.sharding.Mesh(mesh.devices.reshape(outer, inner // 2, 2), AXES)
    items = P(AXES, None, None)
    weights = P(None, AXES, None)
    vectors = P(None, AXES)
    return jax.shard_map(
        functools.partial(local, (outer, inner // 2)),
        mesh=fine,
        in_specs=(items, items, P(AXES), items) + (weights,) * 6 + (vectors,) * 3,
        out_specs=(items,) * 3 + (P(),) + (weights,) * 8 + (vectors,) * 4,
        check_vma=False,
    )
```
